32 devices in a mesh: dp: 4 (over z), shard: 8 (over y, x, core).
Axes of the slice: x: 2, y: 2, z: 4, core: 2. Of those that a mesh axis runs over, the one named last changes fastest.
Arguments:
- roi_features: bfloat16 [32, 512, 2048], P(('dp', 'shard')), may hold values from -150 to 150
- doc_ids: int32 [32, 512], P(('dp', 'shard')), may hold values from 0 to 5, never falling along the last dimension, each value on 1 to 160 neighbouring positions
- w_roi: bfloat16 [2048, 768], P('shard'), may hold values from -0.125 to 0.125
- bn_gain: bfloat16 [768], P('shard'), may hold values from 0.099609375 to 1.8984375
- bn_beta: bfloat16 [768], P('shard'), may hold values from -3 to 3
- w_qkv: bfloat16 [768, 2304], P('shard'), may hold values from -0.21875 to 0.21875
- w_out: bfloat16 [768, 768], P('shard'), may hold values from -0.625 to 0.625
- ln1_gain: bfloat16 [768], P('shard'), may hold values from 0.099609375 to 1.8984375
- ln1_beta: bfloat16 [768], P('shard'), may hold values from -3 to 3
- w_up: bfloat16 [768, 3072], P('shard'), may hold values from -0.21875 to 0.21875
- w_down: bfloat16 [3072, 768], P('shard'), may hold values from -0.21875 to 0.21875
- ln2_gain: bfloat16 [768], P('shard'), may hold values from 0.099609375 to 1.8984375
- ln2_beta: bfloat16 [768], P('shard'), may hold values from -3 to 3
- cotangent: bfloat16 [32, 512, 768], P(('dp', 'shard')), may hold values from -6 to 6
Outputs:
- layer_out: bfloat16 [32, 512, 768], P(('dp', 'shard'))
- roi_grad: float32 [32, 512, 2048], P(('dp', 'shard'))
- grad_w_roi: float32 [2048, 768], P('shard')
- grad_bn_gain: float32 [768], P('shard')
- grad_bn_beta: float32 [768], P('shard')
- grad_w_qkv: float32 [768, 2304], P('shard')
- grad_w_out: float32 [768, 768], P('shard')
- grad_ln1_gain: float32 [768], P('shard')
- grad_ln1_beta: float32 [768], P('shard')
- grad_w_up: float32 [768, 3072], P('shard')
- grad_w_down: float32 [3072, 768], P('shard')
- grad_ln2_gain: float32 [768], P('shard')
- grad_ln2_beta: float32 [768], P('shard')
- bn_mean: float32 [768], replicated
- bn_var: float32 [768], replicated
The draws below stay inside these ranges and needn't reach their ends.
Inputs may be any that keep to these rules, and one draw needn't show every extreme that they name: `doc_ids`: document numbers never fall along a packed row, and each document holds 1 to 160 tokens.
All inputs are finite; a program needn't handle non-finite values.
Results may differ from the reference program's by a relative error of at most 0.015.
Values may be sent and summed in bfloat16 or wider, within the bound.
No kernel may reach another device: no remote copies, remote signals or barrier semaphores. Data moves between devices by JAX's collectives and lax.ppermute only.
A program may use at most 192 MiB of HBM per device.

```python
import math
import jax
import jax.numpy as jnp
import numpy as np
from jax import lax

D = 768
HEADS = 12
HEAD_DIM = 64
FF = 3072
ROI_DIM = 2048
LEN = 512
DOCS = 6
DOC_MOST = 160
ROWS = 32


def draw_roi_features(key, part):
    key = jax.random.fold_in(key, 11)
    key_base = jax.random.fold_in(key, 0)
    key_token = jax.random.fold_in(key, 1)
    key_feature = jax.random.fold_in(key, 2)
    key_order = jax.random.fold_in(key, 4)
    row_pos = jnp.arange(ROWS, dtype=jnp.float32)
    rising = 1.0 + 2.0 * row_pos / max(ROWS - 1, 1)
    order = jax.random.permutation(key_order, ROWS)
    rising = rising[order]
    token_scale = jnp.exp(jax.random.uniform(key_token, (ROWS, LEN, 1), jnp.float32) * math.log(4.0))
    feature_scale = jnp.exp(jax.random.uniform(key_feature, (1, 1, ROI_DIM), jnp.float32) * math.log(3.0))
    base = jnp.clip(jax.random.normal(key_base, (ROWS, LEN, ROI_DIM), jnp.float32), -4.0, 4.0)
    scaled = base * rising[:, None, None] * token_scale * feature_scale
    return scaled.astype(jnp.bfloat16)


def draw_cotangent(key, part):
    key = jax.random.fold_in(key, 13)
    key_base, key_offset = jax.random.split(key, 2)
    base = jax.random.normal(key_base, (ROWS, LEN, D), jnp.float32)
    offset = 0.4 * jax.random.normal(key_offset, (1, 1, D), jnp.float32)
    return jnp.clip(base + offset, -6.0, 6.0).astype(jnp.bfloat16)


def block_scale(key, dims, shards, low, high):
    def one(axis_at, parts):
        heights = jax.random.uniform(jax.random.fold_in(jax.random.fold_in(key, 6), axis_at), (parts,), jnp.float32, low / len(shards), high / len(shards))
        return jnp.repeat(jnp.exp(heights), dims[axis_at] // parts).reshape((-1,) + (1,) * (len(dims) - axis_at - 1))

    loudness = one(*shards[0])
    for cut in shards[1:]:
        loudness = loudness * one(*cut)
    return loudness


def split_up(number_of, total, reach, lean):
    weights = [(1 << 20) // math.isqrt(grade ** lean) + 1 for grade in range(2, number_of + 1)]
    rest, holding = total - reach - (number_of - 1), [1] * (number_of - 1)
    while rest > 0:
        movable = [i for i in range(number_of - 1) if holding[i] < reach]
        whole, budget = sum([weights[i] for i in movable]), rest
        for i in movable:
            addition = min(reach - holding[i], max(1, budget * weights[i] // whole), rest)
            holding[i] = holding[i] + addition
            rest = rest - addition
    return np.array([reach] + holding)


def uneven_parts(key, number_of, total, reach, skew):
    if number_of == 2:
        one = jax.random.randint(key, (), max(1, total - reach), min(reach, total - 1) + 1)
        return jnp.stack([one, total - one])
    sizes = jnp.asarray(split_up(number_of, total, reach, skew), jnp.int32)
    pairs = (number_of - 1) // 2
    giver, taker = sizes[1:1 + 2 * pairs:2], sizes[2:2 + 2 * pairs:2]
    room = jnp.minimum(giver - 1, reach - taker)
    passed = jax.random.randint(jax.random.fold_in(key, 1), (pairs,), 0, 1 << 20) % (room + 1)
    sizes = sizes.at[1:1 + 2 * pairs:2].set(giver - passed).at[2:2 + 2 * pairs:2].set(taker + passed)
    return sizes[jax.random.permutation(jax.random.fold_in(key, 2), number_of)]


def noise(stream_key, extent, scale, most, cuts=(), kind=jnp.bfloat16):
    values = scale * jax.random.normal(stream_key, extent, jnp.float32)
    if cuts:
        values = values * block_scale(stream_key, extent, cuts, -0.22, 0.18)
    return jnp.clip(values, -most, most).astype(kind)


def setup_inputs(seed: int = 0) -> dict:
    key_of = jax.random.split(jax.random.key(seed), 15)
    return {
        "roi_features": draw_roi_features(jax.random.fold_in(key_of[14], 71), 0),
        "doc_ids": jax.vmap(lambda own: jnp.searchsorted(jnp.cumsum(uneven_parts(own, DOCS, LEN, DOC_MOST, 1)), jnp.arange(LEN), side="right"))(jax.random.split(key_of[1], ROWS)).reshape((ROWS, LEN)).astype(jnp.int32),
        "w_roi": noise(key_of[2], (ROI_DIM, D), ROI_DIM ** -0.5, 0.125, ((0, 8),)),
        "bn_gain": jnp.clip(1.0 + 0.18 * jax.random.normal(key_of[3], (D,), jnp.float32), 0.099609375, 1.8984375).astype(jnp.bfloat16),
        "bn_beta": noise(key_of[4], (D,), 0.5, 3.0, ((0, 8),)),
        "w_qkv": noise(key_of[5], (D, 3 * D), D ** -0.5, 0.21875, ((0, 8),)),
        "w_out": noise(key_of[6], (D, D), (D // 8) ** -0.5, 0.625, ((0, 8),)),
        "ln1_gain": jnp.clip(1.0 + 0.18 * jax.random.normal(key_of[7], (D,), jnp.float32), 0.099609375, 1.8984375).astype(jnp.bfloat16),
        "ln1_beta": noise(key_of[8], (D,), 0.5, 3.0, ((0, 8),)),
        "w_up": noise(key_of[9], (D, FF), D ** -0.5, 0.21875, ((0, 8),)),
        "w_down": noise(key_of[10], (FF, D), (FF // 4) ** -0.5, 0.21875, ((0, 8),)),
        "ln2_gain": jnp.clip(1.0 + 0.18 * jax.random.normal(key_of[11], (D,), jnp.float32), 0.099609375, 1.8984375).astype(jnp.bfloat16),
        "ln2_beta": noise(key_of[12], (D,), 0.5, 3.0, ((0, 8),)),
        "cotangent": draw_cotangent(jax.random.fold_in(key_of[14], 71), 0),
    }


EPSILON = 1e-05
SCORE_SCALE = 0.125
PRECISE = lax.Precision.HIGHEST

@jax.custom_vjp
def low(v):
    return lax.optimization_barrier(v.astype(jnp.bfloat16)).astype(jnp.float32)

@jax.custom_vjp
def low_back(v):
    return v

def low_keep(v):
    return (low(v), None)

def low_pass(kept, grad):
    return (grad,)

def back_keep(v):
    return (v, None)

def back_low(kept, grad):
    return (low(grad),)
low.defvjp(low_keep, low_pass)
low_back.defvjp(back_keep, back_low)

def product(matrix_a, matrix_b):
    return jnp.dot(matrix_a, matrix_b, precision=PRECISE, preferred_element_type=jnp.float32)

def layer_norm(values, gain_vec, offset):
    center = values - lax.optimization_barrier(jnp.mean(values, axis=-1, keepdims=True))
    normed = center * lax.rsqrt(lax.optimization_barrier(jnp.mean(center * center, axis=-1, keepdims=True)) + EPSILON)
    return normed * gain_vec + offset

def reference(roi_features, doc_ids, w_roi, bn_gain, bn_beta, w_qkv, w_out, ln1_gain, ln1_beta, w_up, w_down, ln2_gain, ln2_beta, cotangent):
    weights_all = tuple((array_in.astype(jnp.float32) for array_in in (w_roi, bn_gain, bn_beta, w_qkv, w_out, ln1_gain, ln1_beta, w_up, w_down, ln2_gain, ln2_beta)))
    roi_wide = roi_features.astype(jnp.float32)
    group_rows = 8
    groups = ROWS // group_rows

    def forward(weight_set, roi_all):
        proj_w, gain_bn, beta_bn, qkv_w, out_w, gain_one, beta_one, up_w, down_w, gain_two, beta_two = weight_set
        projected = low_back(product(roi_all.reshape(ROWS * LEN, ROI_DIM), proj_w))
        batch_mean = lax.optimization_barrier(jnp.mean(projected, axis=0))
        batch_var = lax.optimization_barrier(jnp.mean(projected * projected, axis=0)) - batch_mean * batch_mean
        normed = (projected - batch_mean) * lax.rsqrt(batch_var + EPSILON)
        embedded = normed * gain_bn + beta_bn

        def block_rows(inputs_pair):
            emb_rows, id_rows = inputs_pair
            emb_flat = emb_rows.reshape(group_rows * LEN, D)
            packed = low(low_back(product(low(emb_flat), qkv_w)))
            packed = packed.reshape(group_rows, LEN, 3, HEADS, HEAD_DIM)
            queries = packed[:, :, 0]
            keys_part = packed[:, :, 1]
            values_part = packed[:, :, 2]
            scores = low_back(jnp.einsum('bqhd,bkhd->bhqk', queries, keys_part, precision=PRECISE) * SCORE_SCALE)
            same_doc = id_rows[:, :, None] == id_rows[:, None, :]
            scores = jnp.where(same_doc[:, None], scores, -1000000000.0)
            row_max = lax.optimization_barrier(jnp.max(scores, axis=-1, keepdims=True))
            expo = jnp.exp(scores - row_max)
            probs = expo / lax.optimization_barrier(jnp.sum(expo, axis=-1, keepdims=True))
            attended = low(low_back(jnp.einsum('bhqk,bkhd->bqhd', low(probs), values_part, precision=PRECISE)))
            attn_branch = low_back(product(attended.reshape(group_rows * LEN, D), out_w))
            normed_one = layer_norm(emb_flat + attn_branch, gain_one, beta_one)
            up_act = low_back(product(low(normed_one), up_w))
            activated = low(jax.nn.gelu(up_act, approximate=False))
            down_branch = low_back(product(activated, down_w))
            result = layer_norm(normed_one + down_branch, gain_two, beta_two)
            return result.reshape(group_rows, LEN, D)
        outputs = lax.map(jax.checkpoint(block_rows), (embedded.reshape(groups, group_rows, LEN, D), doc_ids.reshape(groups, group_rows, LEN)))
        return (outputs.reshape(ROWS, LEN, D), (batch_mean, batch_var))
    result, pullback, stats = jax.vjp(forward, weights_all, roi_wide, has_aux=True)
    weight_grads, roi_grad = pullback(cotangent.astype(jnp.float32))
    g_roi, g_bng, g_bnb, g_qkv, g_out, g_l1g, g_l1b, g_up, g_down, g_l2g, g_l2b = weight_grads
    return (result.astype(jnp.bfloat16), roi_grad, g_roi, g_bng, g_bnb, g_qkv, g_out, g_l1g, g_l1b, g_up, g_down, g_l2g, g_l2b, stats[0], stats[1])
```

```python
import jax
import jax.numpy as jnp
from jax import lax
from jax.experimental import pallas as pl
from jax.experimental.pallas import tpu as pltpu
from jax.sharding import PartitionSpec as P

HEAD_DIM = 64


EPSILON = 1e-05
SCORE_SCALE = 0.125


def matmul(matrix_a, matrix_b):
    return jnp.dot(matrix_a, matrix_b, preferred_element_type=jnp.float32)


def matmul_tn(matrix_a, matrix_b):
    return lax.dot_general(
        matrix_a, matrix_b, (((0,), (0,)), ((), ())), preferred_element_type=jnp.float32
    )


def matmul_nt(matrix_a, matrix_b):
    return lax.dot_general(
        matrix_a, matrix_b, (((1,), (1,)), ((), ())), preferred_element_type=jnp.float32
    )


def gelu_exact(values):
    return jax.nn.gelu(values, approximate=False)


def layer_norm(values, gain_vec, offset):
    center = values - jnp.mean(values, axis=-1, keepdims=True)
    inv_std = lax.rsqrt(jnp.mean(center * center, axis=-1, keepdims=True) + EPSILON)
    normed = center * inv_std
    return (normed * gain_vec + offset, normed, inv_std)


def layer_norm_back(gradient, normed, inv_std, gain_vec):
    scaled = gradient * gain_vec
    return inv_std * (
        scaled
        - jnp.mean(scaled, axis=-1, keepdims=True)
        - normed * jnp.mean(scaled * normed, axis=-1, keepdims=True)
    )


def split_heads(packed_row):
    length = packed_row.shape[0]
    head_count = packed_row.shape[1] // (3 * HEAD_DIM)
    split_qkv = packed_row.reshape(length, 3, head_count, HEAD_DIM)
    return (split_qkv[:, 0], split_qkv[:, 1], split_qkv[:, 2])


def masked_scores(queries, keys_part, doc_row):
    scores = (
        jnp.einsum("qhd,khd->hqk", queries, keys_part, preferred_element_type=jnp.float32)
        * SCORE_SCALE
    )
    same_doc = doc_row[:, None] == doc_row[None, :]
    return jnp.where(same_doc[None], scores, -1000000000.0)


def attend_row(inputs_pair):
    packed_row, doc_row = inputs_pair
    queries, keys_part, values_part = split_heads(packed_row)
    scores = masked_scores(queries, keys_part, doc_row)
    row_max = jnp.max(scores, axis=-1, keepdims=True)
    expo = jnp.exp(scores - row_max)
    totals = jnp.sum(expo, axis=-1, keepdims=True)
    probs = (expo / totals).astype(jnp.bfloat16)
    mixed_rows = jnp.einsum("hqk,khd->qhd", probs, values_part, preferred_element_type=jnp.float32)
    return (mixed_rows.reshape(packed_row.shape[0], -1), row_max + jnp.log(totals))


def attend_back(inputs_four):
    packed_row, doc_row, lse_row, grad_row = inputs_four
    queries, keys_part, values_part = split_heads(packed_row)
    length = packed_row.shape[0]
    grad_heads = grad_row.reshape(length, queries.shape[1], HEAD_DIM)
    scores = masked_scores(queries, keys_part, doc_row)
    probs = jnp.exp(scores - lse_row)
    grad_probs = jnp.einsum(
        "qhd,khd->hqk", grad_heads, values_part, preferred_element_type=jnp.float32
    )
    grad_values = jnp.einsum(
        "hqk,qhd->khd", probs.astype(jnp.bfloat16), grad_heads, preferred_element_type=jnp.float32
    )
    inner = jnp.sum(probs * grad_probs, axis=-1, keepdims=True)
    grad_scores = (probs * (grad_probs - inner)).astype(jnp.bfloat16)
    grad_queries = (
        jnp.einsum("hqk,khd->qhd", grad_scores, keys_part, preferred_element_type=jnp.float32)
        * SCORE_SCALE
    )
    grad_keys = (
        jnp.einsum("hqk,qhd->khd", grad_scores, queries, preferred_element_type=jnp.float32)
        * SCORE_SCALE
    )
    stacked = jnp.stack([grad_queries, grad_keys, grad_values], axis=1)
    return stacked.reshape(length, -1).astype(jnp.bfloat16)


CORE, ACROSS, ALONG = 1, 2, 4


def direct_mesh():
    return lax.axis_size("shard") == 8 and lax.axis_size("dp") == 4


def swap(values, step, axis="shard"):
    size = lax.axis_size(axis)
    return lax.ppermute(values, axis, [(i, i ^ step) for i in range(size)])


def add_low(*terms):
    total = terms[0].astype(jnp.float32)
    for term in terms[1:]:
        total = total + term.astype(jnp.float32)
    return total.astype(jnp.bfloat16)


def sum_everywhere(part):
    if not direct_mesh():
        return lax.psum(part, ("dp", "shard"))
    part = part + swap(part, CORE)
    part = (part + swap(part, ACROSS)) + (swap(part, ALONG) + swap(part, ACROSS | ALONG))
    return (part + swap(part, 1, "dp")) + (swap(part, 2, "dp") + swap(part, 3, "dp"))


def pack_kernel(index_ref, mine_ref, other_ref, mine_out, other_out):
    mine_out[0] = mine_ref[...].astype(mine_out.dtype)
    other_out[0] = other_ref[...].astype(other_out.dtype)


def pack_gradient(gradient):
    rows, cols = gradient.shape[0] // 8, gradient.shape[1]
    me = lax.axis_index("shard")
    index = jnp.stack([me ^ (2 * j + k) for k in range(2) for j in range(4)]).astype(jnp.int32)
    block = pl.BlockSpec((1, rows, cols), lambda j, index_ref: (j, 0, 0))
    return pl.pallas_call(
        pack_kernel,
        grid_spec=pltpu.PrefetchScalarGridSpec(
            num_scalar_prefetch=1,
            grid=(4,),
            in_specs=[
                pl.BlockSpec((rows, cols), lambda j, index_ref: (index_ref[j], 0)),
                pl.BlockSpec((rows, cols), lambda j, index_ref: (index_ref[4 + j], 0)),
            ],
            out_specs=[block, block],
        ),
        out_shape=[jax.ShapeDtypeStruct((4, rows, cols), jnp.bfloat16)] * 2,
        compiler_params=pltpu.CompilerParams(vmem_limit_bytes=40 * 2**20),
    )(index, gradient, gradient)


def plane_sum(mine, other, first):
    second = ACROSS + ALONG - first
    near, far = first // 2, second // 2
    got = swap(other, CORE)
    sent = add_low(jnp.stack([mine[near], mine[3]]), jnp.stack([got[near], got[3]]))
    came = swap(sent, first)
    passed = add_low(mine[far], got[far], came[1])
    back = swap(passed, second)
    return add_low(mine[0], got[0], came[0], back)


def line_sum(part):
    part = add_low(part, lax.ppermute(part, "dp", [(0, 1), (3, 2)]))
    part = add_low(part, lax.ppermute(part, "dp", [(1, 2), (2, 1)]))
    outer = lax.ppermute(part, "dp", [(1, 0), (2, 3)])
    place = lax.axis_index("dp")
    return jnp.where((place == 1) | (place == 2), part, outer).astype(jnp.float32)


def sum_to_owner(gradient, first):
    if not direct_mesh():
        part = lax.psum_scatter(gradient.astype(jnp.bfloat16), "shard", scatter_dimension=0, tiled=True)
        return lax.psum(part, "dp").astype(jnp.float32)
    mine, other = pack_gradient(gradient)
    return line_sum(plane_sum(mine, other, first))


def per_device(
    roi_features,
    doc_ids,
    w_roi,
    bn_gain,
    bn_beta,
    w_qkv,
    w_out,
    ln1_gain,
    ln1_beta,
    w_up,
    w_down,
    ln2_gain,
    ln2_beta,
    cotangent,
):
    whole_roi = lax.all_gather(w_roi, "shard", axis=0, tiled=True)
    whole_qkv = lax.all_gather(w_qkv, "shard", axis=0, tiled=True)
    whole_out = lax.all_gather(w_out, "shard", axis=0, tiled=True)
    whole_up = lax.all_gather(w_up, "shard", axis=0, tiled=True)
    whole_down = lax.all_gather(w_down, "shard", axis=0, tiled=True)
    own_width = bn_gain.shape[0]
    own_start = lax.axis_index("shard") * own_width
    own_params = jnp.stack([bn_gain, bn_beta, ln1_gain, ln1_beta, ln2_gain, ln2_beta]).astype(jnp.float32)
    own_params = jnp.where(lax.axis_index("dp") == 0, own_params, 0.0)
    row_count, length, roi_width = roi_features.shape
    token_count = row_count * length
    population = token_count * lax.axis_size("dp") * lax.axis_size("shard")
    roi_flat = roi_features.reshape(token_count, roi_width)
    projected = matmul(roi_flat, whole_roi)
    first_part = jnp.zeros((8, projected.shape[1]), jnp.float32)
    first_part = first_part.at[0].set(jnp.sum(projected, axis=0)).at[1].set(jnp.sum(projected * projected, axis=0))
    first_part = lax.dynamic_update_slice(first_part, own_params, (2, own_start))
    whole_first = sum_everywhere(first_part)
    first_sum, square_sum = whole_first[0], whole_first[1]
    gain_bn, beta_bn, gain_one, beta_one, gain_two, beta_two = [whole_first[2 + i] for i in range(6)]
    batch_mean = first_sum / population
    batch_var = square_sum / population - batch_mean * batch_mean
    batch_inv = lax.rsqrt(batch_var + EPSILON)
    bn_normed = (projected - batch_mean) * batch_inv
    embedded = bn_normed * gain_bn + beta_bn
    embedded_low = embedded.astype(jnp.bfloat16)
    packed = matmul(embedded_low, whole_qkv).astype(jnp.bfloat16)
    packed_rows = packed.reshape(row_count, length, -1)
    attended, lse_all = lax.map(attend_row, (packed_rows, doc_ids))
    attended_low = attended.reshape(token_count, -1).astype(jnp.bfloat16)
    attn_branch = matmul(attended_low, whole_out)
    normed_one, hat_one, inv_one = layer_norm(embedded + attn_branch, gain_one, beta_one)
    normed_one_low = normed_one.astype(jnp.bfloat16)
    up_act = matmul(normed_one_low, whole_up)
    activated, gelu_back = jax.vjp(gelu_exact, up_act)
    activated_low = activated.astype(jnp.bfloat16)
    down_branch = matmul(activated_low, whole_down)
    output_rows, hat_two, inv_two = layer_norm(normed_one + down_branch, gain_two, beta_two)
    layer_out = output_rows.astype(jnp.bfloat16).reshape(row_count, length, -1)
    grad_output = cotangent.reshape(token_count, -1).astype(jnp.float32)
    grad_gain_two = jnp.sum(grad_output * hat_two, axis=0)
    grad_beta_two = jnp.sum(grad_output, axis=0)
    grad_second = layer_norm_back(grad_output, hat_two, inv_two, gain_two)
    grad_down_low = grad_second.astype(jnp.bfloat16)
    grad_w_down = matmul_tn(activated_low, grad_down_low)
    (grad_up,) = gelu_back(matmul_nt(grad_down_low, whole_down))
    grad_up_low = grad_up.astype(jnp.bfloat16)
    grad_w_up = matmul_tn(normed_one_low, grad_up_low)
    grad_normed_one = grad_second + matmul_nt(grad_up_low, whole_up)
    grad_gain_one = jnp.sum(grad_normed_one * hat_one, axis=0)
    grad_beta_one = jnp.sum(grad_normed_one, axis=0)
    grad_first = layer_norm_back(grad_normed_one, hat_one, inv_one, gain_one)
    grad_attn_low = grad_first.astype(jnp.bfloat16)
    grad_w_out = matmul_tn(attended_low, grad_attn_low)
    grad_attended = matmul_nt(grad_attn_low, whole_out).astype(jnp.bfloat16)
    grad_packed = lax.map(
        attend_back, (packed_rows, doc_ids, lse_all, grad_attended.reshape(row_count, length, -1))
    )
    grad_packed_flat = grad_packed.reshape(token_count, -1)
    grad_w_qkv = matmul_tn(embedded_low, grad_packed_flat)
    grad_embedded = grad_first + matmul_nt(grad_packed_flat, whole_qkv)
    whole_second = sum_everywhere(
        jnp.stack(
            [
                jnp.sum(grad_embedded, axis=0),
                jnp.sum(grad_embedded * bn_normed, axis=0),
                grad_gain_one,
                grad_beta_one,
                grad_gain_two,
                grad_beta_two,
                jnp.zeros_like(grad_gain_one),
                jnp.zeros_like(grad_gain_one),
            ]
        )
    )
    sum_beta, sum_gain = whole_second[0], whole_second[1]
    grad_projected = (
        gain_bn
        * batch_inv
        * (grad_embedded - sum_beta / population - bn_normed * (sum_gain / population))
    )
    grad_proj_low = grad_projected.astype(jnp.bfloat16)
    grad_w_roi = matmul_tn(roi_flat, grad_proj_low)
    roi_grad = matmul_nt(grad_proj_low, whole_roi).reshape(row_count, length, roi_width)
    own_second = lax.dynamic_slice_in_dim(whole_second, own_start, own_width, 1)
    grad_bn_beta, grad_bn_gain, sum_gain_one, sum_beta_one, sum_gain_two, sum_beta_two = [own_second[i] for i in range(6)]
    sum_down = sum_to_owner(grad_w_down, ACROSS)
    sum_up = sum_to_owner(grad_w_up, ALONG)
    sum_qkv = sum_to_owner(grad_w_qkv, ACROSS)
    sum_out = sum_to_owner(grad_w_out, ALONG)
    sum_roi = sum_to_owner(grad_w_roi, ALONG)
    return (
        layer_out,
        roi_grad,
        sum_roi,
        grad_bn_gain,
        grad_bn_beta,
        sum_qkv,
        sum_out,
        sum_gain_one,
        sum_beta_one,
        sum_up,
        sum_down,
        sum_gain_two,
        sum_beta_two,
        batch_mean,
        batch_var,
    )


def solution(mesh):
    placed = (
        P(("dp", "shard"), None, None),
        P(("dp", "shard"), None),
        P("shard", None),
        P("shard"),
        P("shard"),
        P("shard", None),
        P("shard", None),
        P("shard"),
        P("shard"),
        P("shard", None),
        P("shard", None),
        P("shard"),
        P("shard"),
        P(("dp", "shard"), None, None),
    )
    return jax.shard_map(
        per_device,
        mesh=mesh,
        in_specs=placed,
        out_specs=(
            P(("dp", "shard"), None, None),
            P(("dp", "shard"), None, None),
            P("shard", None),
            P("shard"),
            P("shard"),
            P("shard", None),
            P("shard", None),
            P("shard"),
            P("shard"),
            P("shard", None),
            P("shard", None),
            P("shard"),
            P("shard"),
            P(),
            P(),
        ),
        check_vma=False,
    )
```

```python
import functools

import jax
import jax.numpy as jnp
from jax import lax
from jax.experimental import pallas as pl
from jax.experimental.pallas import tpu as pltpu
from jax.sharding import PartitionSpec as P

HEAD_DIM = 64
EPSILON = 1e-05
SCORE_SCALE = 0.125
MASKED = -1000000000.0
CORE, ACROSS, ALONG = 1, 2, 4
TILE = 256
VMEM_LIMIT = 56 * 2**20
F32, LOW = jnp.float32, jnp.bfloat16

ERFC_RATE = 0.33
ERFC = (
    0.18636612594127655,
    0.18283699452877045,
    0.20192526280879974,
    0.04500619322061539,
    0.4125494658946991,
    -0.3554469347000122,
    0.46269258856773376,
    -0.13592977821826935,
)


def direct_mesh():
    return lax.axis_size("shard") == 8 and lax.axis_size("dp") == 4


def swap(values, step, axis="shard"):
    size = lax.axis_size(axis)
    return lax.ppermute(values, axis, [(i, i ^ step) for i in range(size)])


def add_low(*terms):
    total = terms[0].astype(F32)
    for term in terms[1:]:
        total = total + term.astype(F32)
    return total.astype(LOW)


def sum_everywhere(part):
    if not direct_mesh():
        return lax.psum(part, ("dp", "shard"))
    part = part + swap(part, CORE)
    part = (part + swap(part, ACROSS)) + (swap(part, ALONG) + swap(part, ACROSS | ALONG))
    return (part + swap(part, 1, "dp")) + (swap(part, 2, "dp") + swap(part, 3, "dp"))


def plane_sum(mine, other, first):
    second = ACROSS + ALONG - first
    near, far = first // 2, second // 2
    got = swap(other, CORE)
    sent = add_low(jnp.stack([mine[near], mine[3]]), jnp.stack([got[near], got[3]]))
    came = swap(sent, first)
    passed = add_low(mine[far], got[far], came[1])
    back = swap(passed, second)
    return add_low(mine[0], got[0], came[0], back)


def line_sum(part):
    part = add_low(part, lax.ppermute(part, "dp", [(0, 1), (3, 2)]))
    part = add_low(part, lax.ppermute(part, "dp", [(1, 2), (2, 1)]))
    outer = lax.ppermute(part, "dp", [(1, 0), (2, 3)])
    place = lax.axis_index("dp")
    return jnp.where((place == 1) | (place == 2), part, outer).astype(F32)


def sum_to_owner(halves, first):
    if not direct_mesh():
        whole = halves[0].reshape(-1, halves[0].shape[-1])
        part = lax.psum_scatter(whole, "shard", scatter_dimension=0, tiled=True)
        return lax.psum(part, "dp").astype(F32)
    return line_sum(plane_sum(*halves, first))


def dot(left, right, left_dim=1, right_dim=0):
    return lax.dot_general(
        left, right, (((left_dim,), (right_dim,)), ((), ())), preferred_element_type=F32
    )


def wait_all(copies):
    for copy in copies:
        copy.wait()


def start_all(copies):
    for copy in copies:
        copy.start()
    return copies


def piece_copies(pieces, places, target, sems, columns=None):
    copies = []
    for i, piece in enumerate(pieces):
        rows = piece.shape[0]
        source = piece if columns is None else piece.at[:, pl.ds(columns[0], columns[1])]
        at = pl.ds(pl.multiple_of(places[i] * rows, rows), rows) if len(pieces) > 1 else pl.ds(0, rows)
        copies.append(pltpu.make_async_copy(source, target.at[at], sems.at[i]))
    return copies


def up_copies(packed, rows, target, sems):
    width = packed.shape[2]
    copies = []
    for column in range(4):
        for s in range(packed.shape[0]):
            source = packed.at[s, pl.ds((4 + column) * rows, rows), :]
            at = target.at[pl.ds(s * rows, rows), pl.ds(column * width, width)]
            copies.append(pltpu.make_async_copy(source, at, sems.at[len(copies)]))
    return copies


def down_copies(packed, rows, target, sems):
    copies = []
    for s in range(packed.shape[0]):
        source = packed.at[s, pl.ds(0, 4 * rows), :]
        copies.append(pltpu.make_async_copy(source, target.at[pl.ds(s * 4 * rows, 4 * rows)], sems.at[s]))
    return copies


def put_blocks(stage, places, values, first_row, columns):
    cores, _, rows, _ = stage.shape
    values = values.astype(stage.dtype)
    if cores == 1:
        stage[0, 0, first_row : first_row + values.shape[0], columns] = values
        return
    for at in range(0, values.shape[0], rows):
        rel = places[(first_row + at) // rows]
        stage[rel & 1, rel >> 1, :, columns] = values[at : at + rows]


def stage_copies(stage, outs, sems, first=0):
    return [pltpu.make_async_copy(stage.at[k], outs[k], sems.at[first + k]) for k in range(len(outs))]


def batch_scale(sums_ref, tokens):
    mean = sums_ref[0:1, :] * (1.0 / tokens)
    var = sums_ref[1:2, :] * (1.0 / tokens) - mean * mean
    return mean, var, lax.rsqrt(var + EPSILON)


def embed(projected_ref, sums_ref, tokens):
    mean, _, inv = batch_scale(sums_ref, tokens)
    return (projected_ref[...] - mean) * inv * sums_ref[2:3, :] + sums_ref[3:4, :]


def normalize(values):
    center = values - jnp.mean(values, axis=-1, keepdims=True)
    inv = lax.rsqrt(jnp.mean(center * center, axis=-1, keepdims=True) + EPSILON)
    return center * inv, inv


def normalize_back(scaled, normed, inv):
    return inv * (
        scaled
        - jnp.mean(scaled, axis=-1, keepdims=True)
        - normed * jnp.mean(scaled * normed, axis=-1, keepdims=True)
    )


def gelu_pair(values):
    z = jnp.abs(values) * 0.7071067811865476
    t = 1.0 / (1.0 + ERFC_RATE * z)
    poly = 0.5 * ERFC[-1]
    for factor in ERFC[-2::-1]:
        poly = poly * t + 0.5 * factor
    bell = jnp.exp(values * values * -0.5)
    tail = poly * t * bell
    share = jnp.where(values < 0, tail, 1.0 - tail)
    return values * share, share + values * bell * 0.3989422804014327


def call(kernel, args, outs, scratch, name, flops, smem=(), hbm_in=(), hbm_out=()):
    space = lambda i, far: pl.BlockSpec(memory_space=pl.ANY if i in far else pltpu.VMEM)
    in_specs = [
        pl.BlockSpec(memory_space=pltpu.SMEM) if i in smem else space(i, hbm_in) for i in range(len(args))
    ]
    moved = sum(a.size * a.dtype.itemsize for a in args) + sum(a.size * a.dtype.itemsize for a in outs)
    return pl.pallas_call(
        kernel,
        in_specs=in_specs,
        out_specs=[space(i, hbm_out) for i in range(len(outs))],
        out_shape=outs,
        scratch_shapes=scratch,
        compiler_params=pltpu.CompilerParams(vmem_limit_bytes=VMEM_LIMIT),
        cost_estimate=pl.CostEstimate(flops=flops, bytes_accessed=moved, transcendentals=0),
        name=name,
    )(*args)


def shape(dims, kind=F32):
    return jax.ShapeDtypeStruct(tuple(dims), kind)


def dma(count):
    return pltpu.SemaphoreType.DMA((count,))


def column_sum(values):
    return jnp.sum(values, axis=0, keepdims=True)


def project_kernel(count, places, x_ref, params_ref, *refs):
    pieces, (out_ref, sums_ref, weight, sems) = refs[:count], refs[count:]
    wait_all(start_all(piece_copies(pieces, places, weight, sems)))
    sums_ref[...] = params_ref[...]

    @pl.loop(0, out_ref.shape[1] // TILE)
    def _(n):
        cols = pl.ds(pl.multiple_of(n * TILE, TILE), TILE)
        part = dot(x_ref[...], weight[:, cols])
        out_ref[:, cols] = part
        sums_ref[0:1, cols] = column_sum(part)
        sums_ref[1:2, cols] = column_sum(part * part)


def attend_kernel(count, tokens, places, projected_ref, sums_ref, doc_row, doc_col, *refs):
    pieces = refs[:count]
    packed_out, mixed_out, lse_out, weight, sems = refs[count:]
    width = projected_ref.shape[1]
    copies = start_all(piece_copies(pieces, places, weight, sems, (0, 3 * width)))
    embedded = embed(projected_ref, sums_ref, tokens).astype(LOW)
    wait_all(copies)

    @pl.loop(0, 3 * width // TILE)
    def _(n):
        at = pl.multiple_of(n * TILE, TILE)
        part = dot(embedded, weight[:, pl.ds(at, TILE)])
        packed_out[pl.ds(at, TILE), :] = part.T.astype(LOW)

    same = doc_col[...] == doc_row[...]

    @pl.loop(0, width // HEAD_DIM)
    def _(h):
        at = pl.multiple_of(h * HEAD_DIM, HEAD_DIM)
        queries = packed_out[pl.ds(at, HEAD_DIM), :]
        keys = packed_out[pl.ds(width + at, HEAD_DIM), :]
        values = packed_out[pl.ds(2 * width + at, HEAD_DIM), :]
        scores = jnp.where(same, dot(keys, queries, 0, 0) * SCORE_SCALE, MASKED)
        top = jnp.max(scores, axis=0, keepdims=True)
        expo = jnp.exp(scores - top)
        total = jnp.sum(expo, axis=0, keepdims=True)
        probs = (expo * (1.0 / total)).astype(LOW)
        mixed_out[pl.ds(at, HEAD_DIM), :] = dot(values, probs).astype(LOW)
        lse_out[pl.ds(h, 1), :] = top + jnp.log(total)


def expand_kernel(count, packed, rows, tokens, places, projected_ref, sums_ref, mixed_ref, *refs):
    pieces, up_ref = refs[:count], refs[count]
    hat_out, inv_out, active_out, slope_out, weight_out, weight_up, low_one, sems_out, sems_up = refs[count + 1 :]
    width = projected_ref.shape[1]
    copies_out = start_all(piece_copies(pieces, places, weight_out, sems_out, (3 * width, width)))
    if packed:
        copies_up = up_copies(up_ref, rows, weight_up, sems_up)
    else:
        copies_up = [pltpu.make_async_copy(up_ref, weight_up, sems_up.at[0])]
    start_all(copies_up)
    embedded = embed(projected_ref, sums_ref, tokens)
    wait_all(copies_out)
    branch = dot(mixed_ref[...], weight_out[...], 0, 0)
    hat, inv = normalize(embedded + branch)
    hat_out[...] = hat
    inv_out[...] = inv
    low_one[...] = (hat * sums_ref[4:5, :] + sums_ref[5:6, :]).astype(LOW)
    wait_all(copies_up)

    @pl.loop(0, weight_up.shape[1] // TILE)
    def _(n):
        cols = pl.ds(pl.multiple_of(n * TILE, TILE), TILE)
        active, slope = gelu_pair(dot(low_one[...], weight_up[:, cols]))
        active_out[:, cols] = active.astype(LOW)
        slope_out[:, cols] = slope.astype(LOW)


def contract_kernel(packed, rows, places, active_ref, hat_ref, sums_ref, grad_ref, down_ref, *refs):
    halves = refs[: -8]
    layer_out, back_out, grads_out, weight, branch, low_back, stage, sems = refs[-8:]
    if packed:
        copies = down_copies(down_ref, rows, weight, sems)
    else:
        copies = [pltpu.make_async_copy(down_ref, weight, sems.at[0])]
    start_all(copies)
    wait_all(copies)

    @pl.loop(0, branch.shape[1] // TILE)
    def _(n):
        cols = pl.ds(pl.multiple_of(n * TILE, TILE), TILE)
        branch[:, cols] = dot(active_ref[...], weight[:, cols])

    normed_one = hat_ref[...] * sums_ref[4:5, :] + sums_ref[5:6, :]
    hat, inv = normalize(normed_one + branch[...])
    layer_out[...] = (hat * sums_ref[6:7, :] + sums_ref[7:8, :]).astype(LOW)
    gradient = grad_ref[...].astype(F32)
    grads_out[0:1, :] = column_sum(gradient * hat)
    grads_out[1:2, :] = column_sum(gradient)
    back = normalize_back(gradient * sums_ref[6:7, :], hat, inv)
    back_out[...] = back
    low_back[...] = back.astype(LOW)

    tall = 384

    for m in range(active_ref.shape[1] // tall):
        part = dot(active_ref[:, m * tall : (m + 1) * tall], low_back[...], 0, 0)
        put_blocks(stage, places, part, m * tall, slice(None))
    wait_all(start_all(stage_copies(stage, halves, sems)))


def expand_back_kernel(count, packed, rows, places, back_ref, slope_ref, hat_ref, inv_ref, sums_ref, mixed_ref, *refs):
    pieces, refs = refs[:count], refs[count:]
    weights, refs = refs[: (1 if packed else 2)], refs[(1 if packed else 2) :]
    (
        first_out, mixed_back_out, grads_out, weight_out, weight_up, weight_down, low_back, hidden, total,
        low_one, stage_up, stage_out, sems_out, sems_up, sems_down,
    ) = refs[-15:]
    halves = refs[:-15]
    up_halves, out_halves = halves[: len(halves) // 2], halves[len(halves) // 2 :]
    width = hat_ref.shape[1]
    if packed:
        copies_down = down_copies(weights[0], rows, weight_down, sems_down)
        copies_up = up_copies(weights[0], rows, weight_up, sems_up)
    else:
        copies_down = [pltpu.make_async_copy(weights[1], weight_down, sems_down.at[0])]
        copies_up = [pltpu.make_async_copy(weights[0], weight_up, sems_up.at[0])]
    copies_out = piece_copies(pieces, places, weight_out, sems_out, (3 * width, width))
    start_all(copies_down)
    start_all(copies_up)
    start_all(copies_out)
    low_back[...] = back_ref[...].astype(LOW)
    low_one[...] = (hat_ref[...] * sums_ref[4:5, :] + sums_ref[5:6, :]).T.astype(LOW)
    wait_all(copies_down)

    @pl.loop(0, hidden.shape[1] // TILE)
    def _(n):
        cols = pl.ds(pl.multiple_of(n * TILE, TILE), TILE)
        part = dot(low_back[...], weight_down[cols, :], 1, 1) * slope_ref[:, cols].astype(F32)
        part = part.astype(LOW)
        hidden[:, cols] = part
        put_blocks(stage_up, places, dot(low_one[...], part), 0, cols)

    up_sends = start_all(stage_copies(stage_up, up_halves, sems_down, 0))
    wait_all(copies_up)

    @pl.loop(0, width // TILE)
    def _(n):
        cols = pl.ds(pl.multiple_of(n * TILE, TILE), TILE)
        total[:, cols] = back_ref[:, cols] + dot(hidden[...], weight_up[cols, :], 1, 1)

    gradient = total[...]
    hat = hat_ref[...]
    grads_out[0:1, :] = column_sum(gradient * hat)
    grads_out[1:2, :] = column_sum(gradient)
    first = normalize_back(gradient * sums_ref[4:5, :], hat, inv_ref[...])
    first_out[...] = first
    low_first = first.astype(LOW)
    wait_all(copies_out)
    mixed_back_out[...] = dot(weight_out[...], low_first, 1, 1).astype(LOW)
    put_blocks(stage_out, places, dot(mixed_ref[...], low_first), 0, slice(None))
    out_sends = start_all(stage_copies(stage_out, out_halves, sems_out, 0))
    wait_all(up_sends)
    wait_all(out_sends)


def attend_back_kernel(
    count, tokens, places, packed_ref, mixed_back_ref, lse_ref, doc_row, doc_col, projected_ref, sums_ref, first_ref, *refs
):
    pieces = refs[:count]
    grad_packed_out, embedded_out, grads_out, weight, sems = refs[count:]
    width = projected_ref.shape[1]
    copies = start_all(piece_copies(pieces, places, weight, sems, (0, 3 * width)))
    same = doc_col[...] == doc_row[...]

    @pl.loop(0, width // HEAD_DIM)
    def _(h):
        at = pl.multiple_of(h * HEAD_DIM, HEAD_DIM)
        queries = packed_ref[pl.ds(at, HEAD_DIM), :]
        keys = packed_ref[pl.ds(width + at, HEAD_DIM), :]
        values = packed_ref[pl.ds(2 * width + at, HEAD_DIM), :]
        mixed_back = mixed_back_ref[pl.ds(at, HEAD_DIM), :]
        scores = jnp.where(same, dot(keys, queries, 0, 0) * SCORE_SCALE, MASKED)
        probs = jnp.exp(scores - lse_ref[pl.ds(h, 1), :])
        grad_probs = dot(values, mixed_back, 0, 0)
        grad_values = dot(mixed_back, probs.astype(LOW), 1, 1)
        inner = jnp.sum(probs * grad_probs, axis=0, keepdims=True)
        grad_scores = (probs * (grad_probs - inner)).astype(LOW)
        grad_queries = dot(keys, grad_scores) * SCORE_SCALE
        grad_keys = dot(queries, grad_scores, 1, 1) * SCORE_SCALE
        grad_packed_out[pl.ds(at, HEAD_DIM), :] = grad_queries.astype(LOW)
        grad_packed_out[pl.ds(width + at, HEAD_DIM), :] = grad_keys.astype(LOW)
        grad_packed_out[pl.ds(2 * width + at, HEAD_DIM), :] = grad_values.astype(LOW)

    wait_all(copies)
    mean, _, inv = batch_scale(sums_ref, tokens)
    for n in range(width // TILE):
        cols = slice(n * TILE, (n + 1) * TILE)
        part = first_ref[:, cols] + dot(weight[cols, :], grad_packed_out[...]).T
        embedded_out[:, cols] = part
        normed = (projected_ref[:, cols] - mean[:, cols]) * inv[:, cols]
        grads_out[0:1, cols] = column_sum(part)
        grads_out[1:2, cols] = column_sum(part * normed)


def packed_gradient_kernel(tokens, places, grad_packed_ref, projected_ref, sums_ref, *refs):
    halves, (stage, low, sems) = refs[:-3], refs[-3:]
    low[...] = embed(projected_ref, sums_ref, tokens).T.astype(LOW)

    @pl.loop(0, grad_packed_ref.shape[0] // TILE)
    def _(n):
        cols = pl.ds(pl.multiple_of(n * TILE, TILE), TILE)
        put_blocks(stage, places, dot(low[...], grad_packed_ref[cols, :], 1, 1), 0, cols)

    wait_all(start_all(stage_copies(stage, halves, sems)))


def project_back_kernel(tokens, places, embedded_ref, projected_ref, sums_ref, grads_ref, x_ref, *refs):
    halves, (low_out, stage, sems) = refs[:-3], refs[-3:]
    mean, _, inv = batch_scale(sums_ref, tokens)
    normed = (projected_ref[...] - mean) * inv
    gradient = embedded_ref[...] - grads_ref[0:1, :] * (1.0 / tokens) - normed * (grads_ref[1:2, :] * (1.0 / tokens))
    low_out[...] = (sums_ref[2:3, :] * inv * gradient).astype(LOW)
    for m in range(x_ref.shape[1] // TILE):
        part = dot(x_ref[:, m * TILE : (m + 1) * TILE], low_out[...], 0, 0)
        put_blocks(stage, places, part, m * TILE, slice(None))
    wait_all(start_all(stage_copies(stage, halves, sems)))


def input_gradient_kernel(count, places, low_ref, *refs):
    pieces, (out_ref, weight, sems) = refs[:count], refs[count:]
    wait_all(start_all(piece_copies(pieces, places, weight, sems)))

    @pl.loop(0, weight.shape[0] // TILE)
    def _(n):
        cols = pl.ds(pl.multiple_of(n * TILE, TILE), TILE)
        out_ref[:, cols] = dot(low_ref[...], weight[cols, :], 1, 1)


def gather_pieces(own):
    across, along = swap(own, ACROSS), swap(own, ALONG)
    half = own.shape[0] // 2
    corner = jnp.concatenate([swap(along[:half], ACROSS), swap(across[half:], ALONG)])
    pieces = []
    for near in (own, across, along, corner):
        pieces += [near, swap(near, CORE)]
    return pieces


def per_device(
    roi_features, doc_ids, w_roi, bn_gain, bn_beta, w_qkv, w_out, ln1_gain, ln1_beta,
    w_up, w_down, ln2_gain, ln2_beta, cotangent,
):
    _, length, roi_width = roi_features.shape
    width, hidden = w_roi.shape[1], w_up.shape[1]
    devices = lax.axis_size("dp") * lax.axis_size("shard")
    tokens = length * devices
    me = lax.axis_index("shard")
    direct = direct_mesh()
    rows = w_up.shape[0]
    shards = 8 if direct else 1
    cores, chips = (2, 4) if direct else (1, 1)
    places = (me ^ jnp.arange(8)).astype(jnp.int32) if direct else jnp.zeros((8,), jnp.int32)

    x = roi_features.reshape(length, roi_width)
    doc_row, doc_col = doc_ids.reshape(1, length), doc_ids.reshape(length, 1)
    own_params = jnp.stack([bn_gain, bn_beta, ln1_gain, ln1_beta, ln2_gain, ln2_beta]).astype(F32)
    own_params = jnp.where(lax.axis_index("dp") == 0, own_params, 0.0)
    own_start = me * bn_gain.shape[0]
    params = lax.dynamic_update_slice(jnp.zeros((8, width), F32), own_params, (2, own_start))

    whole = functools.partial(lax.all_gather, axis_name="shard", axis=0, tiled=True)
    wide = jnp.concatenate([w_qkv, w_out], axis=1)
    if direct:
        roi_pieces = gather_pieces(w_roi)
        wide, _ = lax.optimization_barrier((wide, roi_pieces[-1]))
        wide_pieces = gather_pieces(wide)
        packed = jnp.concatenate([w_down, w_up.reshape(rows, 4, width).swapaxes(0, 1).reshape(4 * rows, width)])
        packed, _ = lax.optimization_barrier((packed, wide_pieces[-1]))
        packed = lax.all_gather(packed, "shard", axis=0, tiled=False)
        up_in, down_in, both_in = packed, packed, [packed]
    else:
        roi_pieces, wide_pieces = [whole(w_roi)], [whole(wide)]
        up_in, down_in = whole(w_up), whole(w_down)
        both_in = [up_in, down_in]
    count = len(roi_pieces)
    spaces = range(100)

    def blocks(r, c):
        return [shape((chips, r, c), LOW)] * cores

    def staging(r, c):
        return pltpu.VMEM((cores, chips, r, c), LOW)

    projected, sums = call(
        functools.partial(project_kernel, count),
        [places, x, params, *roi_pieces],
        [shape((length, width)), shape((8, width))],
        [pltpu.VMEM((roi_width, width), LOW), dma(8)],
        "project",
        2 * length * roi_width * width,
        smem=(0,),
        hbm_in=spaces[3:],
    )
    sums = sum_everywhere(sums)

    packed_qkv, mixed, lse = call(
        functools.partial(attend_kernel, count, tokens),
        [places, projected, sums, doc_row, doc_col, *wide_pieces],
        [shape((3 * width, length), LOW), shape((width, length), LOW), shape((width // HEAD_DIM, length))],
        [pltpu.VMEM((width, 3 * width), LOW), dma(8)],
        "attend",
        2 * length * width * (3 * width + 2 * length),
        smem=(0,),
        hbm_in=spaces[5:],
    )
    hat, inv, active, slope = call(
        functools.partial(expand_kernel, count, direct, rows, tokens),
        [places, projected, sums, mixed, *wide_pieces, up_in],
        [shape((length, width)), shape((length, 1)), shape((length, hidden), LOW), shape((length, hidden), LOW)],
        [pltpu.VMEM((width, width), LOW), pltpu.VMEM((width, hidden), LOW), pltpu.VMEM((length, width), LOW), dma(8), dma(32)],
        "expand",
        2 * length * width * (width + hidden),
        smem=(0,),
        hbm_in=spaces[4:],
    )
    *down_halves, layer_out, back, grads_two = call(
        functools.partial(contract_kernel, direct, rows),
        [places, active, hat, sums, cotangent.reshape(length, width), down_in],
        blocks(hidden // shards, width) + [shape((length, width), LOW), shape((length, width)), shape((2, width))],
        [
            pltpu.VMEM((hidden, width), LOW), pltpu.VMEM((length, width), F32), pltpu.VMEM((length, width), LOW),
            staging(hidden // shards, width), dma(8),
        ],
        "contract",
        4 * length * width * hidden,
        smem=(0,),
        hbm_in=(5,),
        hbm_out=range(cores),
    )
    *both_halves, first, mixed_back, grads_one = call(
        functools.partial(expand_back_kernel, count, direct, rows),
        [places, back, slope, hat, inv, sums, mixed, *wide_pieces, *both_in],
        blocks(width // shards, hidden)
        + blocks(width // shards, width)
        + [shape((length, width)), shape((width, length), LOW), shape((2, width))],
        [
            pltpu.VMEM((width, width), LOW), pltpu.VMEM((width, hidden), LOW), pltpu.VMEM((hidden, width), LOW),
            pltpu.VMEM((length, width), LOW), pltpu.VMEM((length, hidden), LOW), pltpu.VMEM((length, width), F32),
            pltpu.VMEM((width, length), LOW), staging(width // shards, hidden), staging(width // shards, width),
            dma(8), dma(32), dma(8),
        ],
        "expand_back",
        2 * length * width * (3 * hidden + 2 * width),
        smem=(0,),
        hbm_in=spaces[7:],
        hbm_out=range(2 * cores),
    )
    up_halves, out_halves = both_halves[:cores], both_halves[cores:]
    grad_packed, grad_embedded, grads_bn = call(
        functools.partial(attend_back_kernel, count, tokens),
        [places, packed_qkv, mixed_back, lse, doc_row, doc_col, projected, sums, first, *wide_pieces],
        [shape((3 * width, length), LOW), shape((length, width)), shape((2, width))],
        [pltpu.VMEM((width, 3 * width), LOW), dma(8)],
        "attend_back",
        2 * length * width * (3 * width + 5 * length),
        smem=(0,),
        hbm_in=spaces[9:],
    )
    second = sum_everywhere(jnp.concatenate([grads_bn, grads_one, grads_two, jnp.zeros((2, width), F32)]))
    qkv_halves = call(
        functools.partial(packed_gradient_kernel, tokens),
        [places, grad_packed, projected, sums],
        blocks(width // shards, 3 * width),
        [staging(width // shards, 3 * width), pltpu.VMEM((width, length), LOW), dma(8)],
        "packed_gradient",
        2 * length * width * 3 * width,
        smem=(0,),
        hbm_out=range(cores),
    )
    *roi_halves, low_projected = call(
        functools.partial(project_back_kernel, tokens),
        [places, grad_embedded, projected, sums, second, x],
        blocks(roi_width // shards, width) + [shape((length, width), LOW)],
        [staging(roi_width // shards, width), dma(8)],
        "project_back",
        2 * length * width * roi_width,
        smem=(0,),
        hbm_out=range(cores),
    )
    (roi_grad,) = call(
        functools.partial(input_gradient_kernel, count),
        [places, low_projected, *roi_pieces],
        [shape((length, roi_width))],
        [pltpu.VMEM((roi_width, width), LOW), dma(8)],
        "input_gradient",
        2 * length * width * roi_width,
        smem=(0,),
        hbm_in=spaces[2:],
    )
    sum_down = sum_to_owner(down_halves, ACROSS)
    sum_up = sum_to_owner(up_halves, ALONG)
    sum_qkv = sum_to_owner(qkv_halves, ACROSS)
    sum_out = sum_to_owner(out_halves, ALONG)
    sum_roi = sum_to_owner(roi_halves, ALONG)
    own = lax.dynamic_slice_in_dim(second, own_start, bn_gain.shape[0], 1)
    mean = sums[0] / tokens
    return (
        layer_out[None], roi_grad[None], sum_roi, own[1], own[0], sum_qkv, sum_out, own[2], own[3],
        sum_up, sum_down, own[4], own[5], mean, sums[1] / tokens - mean * mean,
    )


def solution(mesh):
    rows3, rows2, split2, split1 = P(("dp", "shard"), None, None), P(("dp", "shard"), None), P("shard", None), P("shard")
    return jax.shard_map(
        per_device,
        mesh=mesh,
        in_specs=(
            rows3, rows2, split2, split1, split1, split2, split2, split1, split1, split2, split2, split1, split1, rows3,
        ),
        out_specs=(
            rows3, rows3, split2, split1, split1, split2, split2, split1, split1, split2, split2, split1, split1, P(), P(),
        ),
        check_vma=False,
    )
```

```python
import functools

import jax
import jax.numpy as jnp
from jax import lax
from jax.experimental import pallas as pl
from jax.experimental.pallas import tpu as pltpu
from jax.sharding import PartitionSpec as P

HEAD_DIM = 64
EPSILON = 1e-05
SCORE_SCALE = 0.125
MASKED = -1000000000.0
CORE, ACROSS, ALONG = 1, 2, 4
TILE = 256
VMEM_LIMIT = 56 * 2**20
F32, LOW = jnp.float32, jnp.bfloat16

ERFC_RATE = 0.33
ERFC = (
    0.18636612594127655,
    0.18283699452877045,
    0.20192526280879974,
    0.04500619322061539,
    0.4125494658946991,
    -0.3554469347000122,
    0.46269258856773376,
    -0.13592977821826935,
)


def direct_mesh():
    return lax.axis_size("shard") == 8 and lax.axis_size("dp") == 4


def swap(values, step, axis="shard"):
    size = lax.axis_size(axis)
    return lax.ppermute(values, axis, [(i, i ^ step) for i in range(size)])


def add_low(*terms):
    total = terms[0].astype(F32)
    for term in terms[1:]:
        total = total + term.astype(F32)
    return total.astype(LOW)


def sum_everywhere(part):
    if not direct_mesh():
        return lax.psum(part, ("dp", "shard"))
    part = part + swap(part, CORE)
    part = (part + swap(part, 1, "dp")) + (swap(part, 2, "dp") + swap(part, 3, "dp"))
    return (part + swap(part, ACROSS)) + (swap(part, ALONG) + swap(part, ACROSS | ALONG))


def tie(values, *after):
    return lax.optimization_barrier((values, after))[0]


class OwnedSum:
    def __init__(self, halves):
        self.direct = direct_mesh()
        if self.direct:
            self.mine, self.got = halves[0], swap(halves[1], CORE)
            rows = self.mine.shape[1] // 2
            self.cuts = ((slice(0, rows), 1, 2), (slice(rows, None), 2, 1))
        else:
            whole = halves[0].reshape(-1, halves[0].shape[-1])
            self.part = lax.psum_scatter(whole, "shard", scatter_dimension=0, tiled=True)

    def plane_one(self, *after):
        if not self.direct:
            return self.part
        self.mine, self.got = tie((self.mine, self.got), *after)
        mine, got = self.mine, self.got
        sent = [
            add_low(jnp.stack([mine[near, cut], mine[3, cut]]), jnp.stack([got[near, cut], got[3, cut]]))
            for cut, near, _ in self.cuts
        ]
        self.came = [swap(part, 2 * near) for part, (_, near, _) in zip(sent, self.cuts)]
        return sent

    def plane_two(self, *after):
        if not self.direct:
            return self.part
        self.mine, self.got, self.came = tie((self.mine, self.got, self.came), *after)
        passed = [
            add_low(self.mine[far, cut], self.got[far, cut], came[1]) for came, (cut, _, far) in zip(self.came, self.cuts)
        ]
        self.back = [swap(part, 2 * far) for part, (_, _, far) in zip(passed, self.cuts)]
        return passed

    def line_in(self, *after):
        if not self.direct:
            return self.part
        mine, got, came, back = tie((self.mine, self.got, self.came, self.back), *after)
        self.part = jnp.concatenate(
            [add_low(mine[0, cut], got[0, cut], c[0], b) for c, b, (cut, _, _) in zip(came, back, self.cuts)]
        )
        self.inward = lax.ppermute(self.part, "dp", [(0, 1), (3, 2)])
        return self.part

    def line_middle(self, *after):
        if not self.direct:
            return self.part
        part, inward = tie((self.part, self.inward), *after)
        self.part = add_low(part, inward)
        self.middle = lax.ppermute(self.part, "dp", [(1, 2), (2, 1)])
        return self.part

    def line_out(self, *after):
        if not self.direct:
            return self.part
        part, middle = tie((self.part, self.middle), *after)
        self.part = add_low(part, middle)
        self.outer = lax.ppermute(self.part, "dp", [(1, 0), (2, 3)])
        return self.part

    def owned(self, *after):
        if not self.direct:
            return lax.psum(self.part, "dp").astype(F32)
        part, outer = tie((self.part, self.outer), *after)
        place = lax.axis_index("dp")
        return jnp.where((place == 1) | (place == 2), part, outer).astype(F32)


def dot(left, right, left_dim=1, right_dim=0):
    return lax.dot_general(
        left, right, (((left_dim,), (right_dim,)), ((), ())), preferred_element_type=F32
    )


def wait_all(copies):
    for copy in copies:
        copy.wait()


def start_all(copies):
    for copy in copies:
        copy.start()
    return copies


def span(index, size):
    return slice(index * size, (index + 1) * size)


def piece_copies(pieces, places, target, sems, source_columns=None, columns=slice(None)):
    copies = []
    for i, piece in enumerate(pieces):
        rows = piece.shape[0]
        source = piece if source_columns is None else piece.at[:, source_columns]
        at = pl.ds(pl.multiple_of(places[i] * rows, rows), rows) if len(pieces) > 1 else pl.ds(0, rows)
        copies.append(pltpu.make_async_copy(source, target.at[at, columns], sems.at[i]))
    return copies


def put_blocks(stage, places, values, first_row, columns):
    cores, _, rows, _ = stage.shape
    values = values.astype(stage.dtype)
    if cores == 1:
        stage[0, 0, first_row : first_row + values.shape[0], columns] = values
        return
    for at in range(0, values.shape[0], rows):
        rel = places[(first_row + at) // rows]
        stage[rel & 1, rel >> 1, :, columns] = values[at : at + rows]


def send_columns(stage, outs, sems, columns=slice(None)):
    return start_all(
        [
            pltpu.make_async_copy(stage.at[k, :, :, columns], out.at[:, :, columns], sems.at[k])
            for k, out in enumerate(outs)
        ]
    )


def row_blocks(stage, outs, places, sems, make):
    cores, chips, rows, _ = stage.shape
    sends = []
    for rel in range(cores * chips):
        first = places[rel] * rows if cores > 1 else 0
        if cores == 1:
            step = min(rows, 512)
            for at in range(0, rows, step):
                stage[0, 0, at : at + step] = make(at, step).astype(stage.dtype)
        else:
            stage[rel & 1, rel >> 1] = make(first, rows).astype(stage.dtype)
        sends += start_all(
            [pltpu.make_async_copy(stage.at[rel & 1, rel >> 1], outs[rel & 1].at[rel >> 1], sems.at[rel])]
        )
    return sends


def lanes(first, size):
    return pl.ds(first if isinstance(first, int) else pl.multiple_of(first, 128), size)


def batch_scale(sums_ref, tokens):
    mean = sums_ref[0:1, :] * (1.0 / tokens)
    var = sums_ref[1:2, :] * (1.0 / tokens) - mean * mean
    return mean, var, lax.rsqrt(var + EPSILON)


def embed(projected_ref, sums_ref, tokens):
    mean, _, inv = batch_scale(sums_ref, tokens)
    return (projected_ref[...] - mean) * inv * sums_ref[2:3, :] + sums_ref[3:4, :]


def normalize(values):
    center = values - jnp.mean(values, axis=-1, keepdims=True)
    inv = lax.rsqrt(jnp.mean(center * center, axis=-1, keepdims=True) + EPSILON)
    return center * inv, inv


def normalize_back(scaled, normed, inv):
    return inv * (
        scaled
        - jnp.mean(scaled, axis=-1, keepdims=True)
        - normed * jnp.mean(scaled * normed, axis=-1, keepdims=True)
    )


def gelu_pair(values):
    t = 1.0 / (1.0 + (ERFC_RATE * 0.7071067811865476) * jnp.abs(values))
    poly = 0.5 * ERFC[-1]
    for factor in ERFC[-2::-1]:
        poly = poly * t + 0.5 * factor
    bell = jnp.exp(values * values * -0.5)
    tail = poly * t * bell
    share = jnp.where(values < 0, tail, 1.0 - tail)
    return values * share, share + values * bell * 0.3989422804014327


def call(kernel, args, outs, scratch, name, smem=(0,), hbm_in=(), hbm_out=()):
    space = lambda i, far: pl.BlockSpec(memory_space=pl.ANY if i in far else pltpu.VMEM)
    in_specs = [
        pl.BlockSpec(memory_space=pltpu.SMEM) if i in smem else space(i, hbm_in) for i in range(len(args))
    ]
    return pl.pallas_call(
        kernel,
        in_specs=in_specs,
        out_specs=[space(i, hbm_out) for i in range(len(outs))],
        out_shape=outs,
        scratch_shapes=scratch,
        compiler_params=pltpu.CompilerParams(vmem_limit_bytes=VMEM_LIMIT),
        cost_estimate=pl.CostEstimate(flops=1024, bytes_accessed=1024, transcendentals=0),
        name=name,
    )(*args)


def shape(dims, kind=F32):
    return jax.ShapeDtypeStruct(tuple(dims), kind)


def dma(*counts):
    return pltpu.SemaphoreType.DMA(counts)


def column_sum(values):
    return jnp.sum(values, axis=0, keepdims=True)


def project_kernel(count, places, x_ref, params_ref, *refs):
    pieces, (out_ref, sums_ref, weight, sems) = refs[:count], refs[count:]
    wait_all(start_all(piece_copies(pieces, places, weight, sems)))
    sums_ref[...] = params_ref[...]
    for n in range(out_ref.shape[1] // TILE):
        cols = span(n, TILE)
        part = dot(x_ref[...], weight[:, cols])
        out_ref[:, cols] = part
        sums_ref[0:1, cols] = column_sum(part)
        sums_ref[1:2, cols] = column_sum(part * part)


def attend_head(head, first_head, width, packed_ref, same, mixed_out, lse_out):
    at = pl.multiple_of((head + first_head) * HEAD_DIM, HEAD_DIM)
    queries = packed_ref[pl.ds(at, HEAD_DIM), :] * jnp.asarray(SCORE_SCALE, LOW)
    keys = packed_ref[pl.ds(width + at, HEAD_DIM), :]
    values = packed_ref[pl.ds(2 * width + at, HEAD_DIM), :]
    scores = jnp.where(same, dot(keys, queries, 0, 0), MASKED)
    top = jnp.max(scores, axis=0, keepdims=True)
    expo = jnp.exp(scores - top)
    total = jnp.sum(expo, axis=0, keepdims=True)
    mixed = dot(values, expo.astype(LOW)) * (1.0 / total)
    mixed_out[pl.ds(pl.multiple_of(head * HEAD_DIM, HEAD_DIM), HEAD_DIM), :] = mixed.astype(LOW)
    lse_out[pl.ds(head, 1), :] = top + jnp.log(total)


def attend_kernel(count, tokens, places, projected_ref, sums_ref, doc_row, doc_col, *refs):
    pieces = refs[:count]
    packed_out, mixed_out, lse_out, weight, sems = refs[count:]
    width = projected_ref.shape[1]
    copies = [
        start_all(piece_copies(pieces, places, weight, sems.at[c], pl.ds(c * width, width), pl.ds(c * width, width)))
        for c in range(3)
    ]
    embedded = embed(projected_ref, sums_ref, tokens).astype(LOW)
    for c in range(3):
        wait_all(copies[c])
        for n in range(c * width // TILE, (c + 1) * width // TILE):
            packed_out[span(n, TILE), :] = dot(embedded, weight[:, span(n, TILE)]).T.astype(LOW)
    same = doc_col[...] == doc_row[...]

    @pl.loop(0, lse_out.shape[0], unroll=3)
    def _(head):
        attend_head(head, 0, width, packed_out, same, mixed_out, lse_out)


def attend_rest_kernel(places, packed_ref, doc_row, doc_col, mixed_out, lse_out):
    width = packed_ref.shape[0] // 3
    first_head = width // HEAD_DIM - lse_out.shape[0]
    same = doc_col[...] == doc_row[...]

    @pl.loop(0, lse_out.shape[0], unroll=3)
    def _(head):
        attend_head(head, first_head, width, packed_ref, same, mixed_out, lse_out)


def expand_kernel(count, tokens, places, projected_ref, sums_ref, mixed_ref, rest_ref, *refs):
    pieces, ups, refs = refs[:count], refs[count : 2 * count], refs[2 * count :]
    hat_out, inv_out, active_out, slope_out, weight_out, weight_up, hat, active, slope, sems_out, sems_up, sems = refs
    width = projected_ref.shape[1]
    copies_out = start_all(piece_copies(pieces, places, weight_out, sems_out, pl.ds(3 * width, width)))
    copies_up = [
        start_all(piece_copies(ups, places, weight_up, sems_up.at[c], pl.ds(c * width, width), pl.ds(c * width, width)))
        for c in range(4)
    ]
    embedded = embed(projected_ref, sums_ref, tokens)
    wait_all(copies_out)
    split = mixed_ref.shape[0]
    branch = dot(mixed_ref[...], weight_out[:split, :], 0, 0) + dot(rest_ref[...], weight_out[split:, :], 0, 0)
    normed, inv = normalize(embedded + branch)
    hat[...] = normed
    sends = start_all([pltpu.make_async_copy(hat, hat_out, sems.at[8])])
    inv_out[...] = inv
    low_one = (normed * sums_ref[4:5, :] + sums_ref[5:6, :]).astype(LOW)
    for c in range(4):
        wait_all(copies_up[c])
        for n in range(c * width // TILE, (c + 1) * width // TILE):
            cols = span(n, TILE)
            one, two = gelu_pair(dot(low_one, weight_up[:, cols]))
            active[:, cols] = one.astype(LOW)
            slope[:, cols] = two.astype(LOW)
        cols = pl.ds(c * width, width)
        sends += start_all(
            [
                pltpu.make_async_copy(active.at[:, cols], active_out.at[:, cols], sems.at[c]),
                pltpu.make_async_copy(slope.at[:, cols], slope_out.at[:, cols], sems.at[4 + c]),
            ]
        )
    wait_all(sends)


def contract_kernel(places, hat_ref, sums_ref, grad_ref, active_ref, down_ref, *refs):
    halves, refs = refs[:-9], refs[-9:]
    layer_out, back_out, grads_out, active, weight, branch, stage, sems, sems_out = refs
    width = hat_ref.shape[1]
    copies = []
    for c in range(4):
        cols = pl.ds(c * width, width)
        copies.append(
            start_all(
                [
                    pltpu.make_async_copy(active_ref.at[:, cols], active.at[:, cols], sems.at[c]),
                    pltpu.make_async_copy(down_ref.at[cols], weight.at[cols], sems.at[4 + c]),
                ]
            )
        )
    branch[...] = hat_ref[...] * sums_ref[4:5, :] + sums_ref[5:6, :]
    for c in range(4):
        wait_all(copies[c])
        branch[...] += dot(active[:, span(c, width)], weight[span(c, width), :])
    hat, inv = normalize(branch[...])
    layer_out[...] = (hat * sums_ref[6:7, :] + sums_ref[7:8, :]).astype(LOW)
    gradient = grad_ref[...].astype(F32)
    grads_out[0:1, :] = column_sum(gradient * hat)
    grads_out[1:2, :] = column_sum(gradient)
    back = normalize_back(gradient * sums_ref[6:7, :], hat, inv)
    back_out[...] = back
    low_back = back.astype(LOW)
    wait_all(row_blocks(stage, halves, places, sems_out, lambda at, n: dot(active[:, lanes(at, n)], low_back, 0, 0)))


def hidden_back_kernel(places, back_ref, hat_ref, sums_ref, slope_ref, down_ref, *refs):
    halves, refs = refs[:-8], refs[-8:]
    hidden_out, hidden, slope, weight, stage, sems, sems_out, sems_hidden = refs
    width = hat_ref.shape[1]
    copies = []
    for c in range(4):
        cols = pl.ds(c * width, width)
        copies.append(
            start_all(
                [
                    pltpu.make_async_copy(slope_ref.at[:, cols], slope.at[:, cols], sems.at[c]),
                    pltpu.make_async_copy(down_ref.at[cols], weight.at[cols], sems.at[4 + c]),
                ]
            )
        )
    low_back = back_ref[...].astype(LOW)
    low_one = (hat_ref[...] * sums_ref[4:5, :] + sums_ref[5:6, :]).T.astype(LOW)
    sends = []
    for c in range(4):
        wait_all(copies[c])
        for n in range(c * width // TILE, (c + 1) * width // TILE):
            cols = span(n, TILE)
            part = (dot(low_back, weight[cols, :], 1, 1) * slope[:, cols].astype(F32)).astype(LOW)
            hidden[:, cols] = part
            put_blocks(stage, places, dot(low_one, part), 0, cols)
        cols = pl.ds(c * width, width)
        sends += send_columns(stage, halves, sems_out.at[c], cols)
        sends += start_all([pltpu.make_async_copy(hidden.at[:, cols], hidden_out.at[:, cols], sems_hidden.at[c])])
    wait_all(sends)


def expand_back_kernel(count, places, back_ref, hat_ref, inv_ref, sums_ref, hidden_ref, *refs):
    pieces, ups, refs = refs[:count], refs[count : 2 * count], refs[2 * count :]
    first_out, low_out, mixed_back_out, grads_out, hidden, weight_out, weight_up, total, sems_out, sems_up, sems = refs
    width = hat_ref.shape[1]
    copies = []
    for c in range(4):
        cols = pl.ds(c * width, width)
        copies.append(
            start_all(
                [pltpu.make_async_copy(hidden_ref.at[:, cols], hidden.at[:, cols], sems.at[c])]
                + piece_copies(ups, places, weight_up, sems_up.at[c], cols, cols)
            )
        )
    copies_out = start_all(piece_copies(pieces, places, weight_out, sems_out, pl.ds(3 * width, width)))
    for c in range(4):
        wait_all(copies[c])
        part = dot(hidden[:, span(c, width)], weight_up[:, span(c, width)], 1, 1)
        total[...] = (back_ref[...] if c == 0 else total[...]) + part
    gradient = total[...]
    hat = hat_ref[...]
    grads_out[0:1, :] = column_sum(gradient * hat)
    grads_out[1:2, :] = column_sum(gradient)
    first = normalize_back(gradient * sums_ref[4:5, :], hat, inv_ref[...])
    first_out[...] = first
    low_first = first.astype(LOW)
    low_out[...] = low_first
    wait_all(copies_out)
    mixed_back_out[...] = dot(weight_out[...], low_first, 1, 1).astype(LOW)


def attend_back_kernel(
    count, tokens, places, packed_ref, mixed_back_ref, lse_ref, lse_rest, doc_row, doc_col, projected_ref, sums_ref,
    first_ref, *refs
):
    pieces = refs[:count]
    grad_packed_out, embedded_out, grads_out, weight, lse, sems = refs[count:]
    width = projected_ref.shape[1]
    copies = start_all(piece_copies(pieces, places, weight, sems, pl.ds(0, 3 * width)))
    split = lse_ref.shape[0]
    lse[:split, :] = lse_ref[...]
    lse[split:, :] = lse_rest[...]
    same = doc_col[...] == doc_row[...]

    @pl.loop(0, width // HEAD_DIM, unroll=3)
    def _(h):
        at = pl.multiple_of(h * HEAD_DIM, HEAD_DIM)
        queries = packed_ref[pl.ds(at, HEAD_DIM), :] * jnp.asarray(SCORE_SCALE, LOW)
        keys = packed_ref[pl.ds(width + at, HEAD_DIM), :]
        values = packed_ref[pl.ds(2 * width + at, HEAD_DIM), :]
        mixed_back = mixed_back_ref[pl.ds(at, HEAD_DIM), :]
        scores = jnp.where(same, dot(keys, queries, 0, 0), MASKED)
        probs = jnp.exp(scores - lse[pl.ds(h, 1), :])
        grad_probs = dot(values, mixed_back, 0, 0)
        grad_values = dot(mixed_back, probs.astype(LOW), 1, 1)
        inner = jnp.sum(probs * grad_probs, axis=0, keepdims=True)
        grad_scores = (probs * (grad_probs - inner)).astype(LOW)
        grad_queries = dot(keys, grad_scores) * SCORE_SCALE
        grad_keys = dot(queries, grad_scores, 1, 1)
        grad_packed_out[pl.ds(at, HEAD_DIM), :] = grad_queries.astype(LOW)
        grad_packed_out[pl.ds(width + at, HEAD_DIM), :] = grad_keys.astype(LOW)
        grad_packed_out[pl.ds(2 * width + at, HEAD_DIM), :] = grad_values.astype(LOW)

    wait_all(copies)
    mean, _, inv = batch_scale(sums_ref, tokens)
    for n in range(width // TILE):
        cols = span(n, TILE)
        part = first_ref[:, cols] + dot(weight[cols, :], grad_packed_out[...]).T
        embedded_out[:, cols] = part
        normed = (projected_ref[:, cols] - mean[:, cols]) * inv[:, cols]
        grads_out[0:1, cols] = column_sum(part)
        grads_out[1:2, cols] = column_sum(part * normed)


def wide_gradient_kernel(tokens, places, grad_packed_ref, projected_ref, sums_ref, mixed_ref, rest_ref, low_ref, *refs):
    halves, (stage, low, sems) = refs[:-3], refs[-3:]
    low[...] = embed(projected_ref, sums_ref, tokens).T.astype(LOW)
    packed, width = grad_packed_ref.shape[0], projected_ref.shape[1]
    sends = []
    for c in range(3):
        for n in range(c * width // TILE, (c + 1) * width // TILE):
            cols = span(n, TILE)
            put_blocks(stage, places, dot(low[...], grad_packed_ref[cols, :], 1, 1), 0, cols)
        sends += send_columns(stage, halves, sems.at[c], pl.ds(c * width, width))
    split = mixed_ref.shape[0]
    for n in range(width // TILE):
        cols = slice(packed + n * TILE, packed + (n + 1) * TILE)
        put_blocks(stage, places, dot(mixed_ref[...], low_ref[:, span(n, TILE)]), 0, cols)
        put_blocks(stage, places, dot(rest_ref[...], low_ref[:, span(n, TILE)]), split, cols)
    sends += send_columns(stage, halves, sems.at[3], pl.ds(3 * width, width))
    wait_all(sends)


def project_back_kernel(tokens, places, embedded_ref, projected_ref, sums_ref, grads_ref, x_ref, *refs):
    halves, (low_out, stage, sems) = refs[:-3], refs[-3:]
    mean, _, inv = batch_scale(sums_ref, tokens)
    normed = (projected_ref[...] - mean) * inv
    gradient = embedded_ref[...] - grads_ref[0:1, :] * (1.0 / tokens) - normed * (grads_ref[1:2, :] * (1.0 / tokens))
    low = (sums_ref[2:3, :] * inv * gradient).astype(LOW)
    low_out[...] = low
    wait_all(row_blocks(stage, halves, places, sems, lambda at, n: dot(x_ref[:, lanes(at, n)], low, 0, 0)))


def input_gradient_kernel(count, places, low_ref, *refs):
    pieces, (out_ref, weight, out, sems, sems_out) = refs[:count], refs[count:]
    copies = start_all(piece_copies(pieces, places, weight, sems))
    sends = []
    rows = weight.shape[0] // len(pieces)
    step = min(rows, 512)
    for i, copy in enumerate(copies):
        copy.wait()
        for part in range(rows // step):
            first = part * step if len(pieces) == 1 else places[i] * rows
            cols = lanes(first, step)
            at = pl.ds(first, step) if len(pieces) == 1 else pl.ds(pl.multiple_of(first, rows), rows)
            out[:, cols] = dot(low_ref[...], weight[at, :], 1, 1)
            sends += start_all([pltpu.make_async_copy(out.at[:, cols], out_ref.at[:, cols], sems_out.at[len(sends)])])
    wait_all(sends)


def corner(across, along):
    half = across.shape[0] // 2
    return jnp.concatenate([swap(along[:half], ACROSS), swap(across[half:], ALONG)])


def with_cores(chips):
    pieces = []
    for shard in chips:
        pieces += [shard, swap(shard, CORE)]
    return pieces


def per_device(
    roi_features, doc_ids, w_roi, bn_gain, bn_beta, w_qkv, w_out, ln1_gain, ln1_beta,
    w_up, w_down, ln2_gain, ln2_beta, cotangent,
):
    _, length, roi_width = roi_features.shape
    width, hidden = w_roi.shape[1], w_up.shape[1]
    devices = lax.axis_size("dp") * lax.axis_size("shard")
    tokens = length * devices
    me = lax.axis_index("shard")
    direct = direct_mesh()
    shards = 8 if direct else 1
    cores, chips = (2, 4) if direct else (1, 1)
    places = (me ^ jnp.arange(8)).astype(jnp.int32) if direct else jnp.zeros((8,), jnp.int32)

    x = roi_features.reshape(length, roi_width)
    doc_row, doc_col = doc_ids.reshape(1, length), doc_ids.reshape(length, 1)
    own_params = jnp.stack([bn_gain, bn_beta, ln1_gain, ln1_beta, ln2_gain, ln2_beta]).astype(F32)
    own_params = jnp.where(lax.axis_index("dp") == 0, own_params, 0.0)
    own_start = me * bn_gain.shape[0]
    params = lax.dynamic_update_slice(jnp.zeros((8, width), F32), own_params, (2, own_start))

    gather = functools.partial(lax.all_gather, axis_name="shard", axis=0, tiled=True)
    wide = jnp.concatenate([w_qkv, w_out], axis=1)
    if direct:
        roi_pieces = with_cores([w_roi, swap(w_roi, ACROSS), swap(w_roi, ALONG), swap(w_roi, ACROSS | ALONG)])
        wide = tie(wide, params)
        wide_sides = [swap(wide, ACROSS), swap(wide, ALONG)]
    else:
        roi_pieces = [gather(w_roi)]
    count = len(roi_pieces)
    spaces = range(100)

    def blocks(r, c):
        return [shape((chips, r, c), LOW)] * cores

    def staging(r, c):
        return pltpu.VMEM((cores, chips, r, c), LOW)

    def low(r, c):
        return pltpu.VMEM((r, c), LOW)

    projected, sums = call(
        functools.partial(project_kernel, count),
        [places, x, params, *roi_pieces],
        [shape((length, width)), shape((8, width))],
        [low(roi_width, width), dma(8)],
        "project",
        hbm_in=spaces[3:],
    )
    if direct:
        sums = sums + swap(sums, CORE)
        wide_corner = corner(*wide_sides)
        sums = tie(sums, *wide_sides)
        sums = (sums + swap(sums, 1, "dp")) + (swap(sums, 2, "dp") + swap(sums, 3, "dp"))
        sums = (sums + swap(sums, ACROSS)) + (swap(sums, ALONG) + swap(sums, ACROSS | ALONG))
        wide_pieces = with_cores([wide, *wide_sides, wide_corner])
        w_up = tie(w_up, sums)
        up_sides = [swap(w_up, ACROSS), swap(w_up, ALONG)]
    else:
        sums = lax.psum(sums, ("dp", "shard"))
        wide_pieces = [gather(wide)]

    heads = width // HEAD_DIM
    part_heads = heads // 2
    part_width = part_heads * HEAD_DIM
    packed_qkv, mixed, lse = call(
        functools.partial(attend_kernel, count, tokens),
        [places, projected, sums, doc_row, doc_col, *wide_pieces],
        [shape((3 * width, length), LOW), shape((part_width, length), LOW), shape((part_heads, length))],
        [low(width, 3 * width), dma(3, 8)],
        "attend",
        hbm_in=spaces[5:],
    )
    if direct:
        up_sides = tie(up_sides, mixed)
        up_corner = corner(*up_sides)
        down_whole = gather(tie(w_down, up_sides))
        start_rest = tie(places, up_sides)
    else:
        down_whole, start_rest = gather(w_down), places
    mixed_rest, lse_rest = call(
        attend_rest_kernel,
        [start_rest, packed_qkv, doc_row, doc_col],
        [shape((width - part_width, length), LOW), shape((heads - part_heads, length))],
        [],
        "attend_rest",
    )
    if direct:
        up_pieces = with_cores([w_up, *up_sides, up_corner])
    else:
        up_pieces = [gather(w_up)]
    hat, inv, active, slope = call(
        functools.partial(expand_kernel, count, tokens),
        [places, projected, sums, mixed, mixed_rest, *wide_pieces, *up_pieces],
        [shape((length, width)), shape((length, 1)), shape((length, hidden), LOW), shape((length, hidden), LOW)],
        [
            low(width, width), low(width, hidden), pltpu.VMEM((length, width), F32), low(length, hidden),
            low(length, hidden), dma(8), dma(4, 8), dma(9),
        ],
        "expand",
        hbm_in=spaces[5:],
        hbm_out=(0, 2, 3),
    )
    *down_halves, layer_out, back, grads_two = call(
        contract_kernel,
        [places, hat, sums, cotangent.reshape(length, width), active, down_whole],
        blocks(hidden // shards, width) + [shape((length, width), LOW), shape((length, width)), shape((2, width))],
        [
            low(length, hidden), low(hidden, width), pltpu.VMEM((length, width), F32), staging(hidden // shards, width),
            dma(8), dma(8),
        ],
        "contract",
        hbm_in=(4, 5),
        hbm_out=range(cores),
    )
    down = OwnedSum(down_halves)
    *up_halves, grad_hidden = call(
        hidden_back_kernel,
        [places, back, hat, sums, slope, down_whole],
        blocks(width // shards, hidden) + [shape((length, hidden), LOW)],
        [
            low(length, hidden), low(length, hidden), low(hidden, width), staging(width // shards, hidden),
            dma(8), dma(4, 2), dma(4),
        ],
        "hidden_back",
        hbm_in=(4, 5),
        hbm_out=range(cores + 1),
    )
    up = OwnedSum(up_halves)
    sent = down.plane_one(grad_hidden)
    first, low_first, mixed_back, grads_one = call(
        functools.partial(expand_back_kernel, count),
        [tie(places, sent), back, hat, inv, sums, grad_hidden, *wide_pieces, *up_pieces],
        [shape((length, width)), shape((length, width), LOW), shape((width, length), LOW), shape((2, width))],
        [
            low(length, hidden), low(width, width), low(width, hidden), pltpu.VMEM((length, width), F32),
            dma(8), dma(4, 8), dma(4),
        ],
        "expand_back",
        hbm_in=spaces[5:],
    )
    sent = down.plane_two(first)
    sent = up.plane_one(first, sent)
    grad_packed, grad_embedded, grads_bn = call(
        functools.partial(attend_back_kernel, count, tokens),
        [tie(places, sent), packed_qkv, mixed_back, lse, lse_rest, doc_row, doc_col, projected, sums, first, *wide_pieces],
        [shape((3 * width, length), LOW), shape((length, width)), shape((2, width))],
        [low(width, 3 * width), pltpu.VMEM((heads, length), F32), dma(8)],
        "attend_back",
        hbm_in=spaces[10:],
    )
    second = jnp.concatenate([grads_bn, grads_one, grads_two, jnp.zeros((2, width), F32)])
    if direct:
        second = tie(second, up.came, down.back)
        second = second + swap(second, CORE)
        second = (second + swap(second, 1, "dp")) + (swap(second, 2, "dp") + swap(second, 3, "dp"))
        start_wide = tie(places, second)
        second = (second + swap(second, ACROSS)) + (swap(second, ALONG) + swap(second, ACROSS | ALONG))
    else:
        second, start_wide = lax.psum(second, ("dp", "shard")), places
    wide_halves = call(
        functools.partial(wide_gradient_kernel, tokens),
        [start_wide, grad_packed, projected, sums, mixed, mixed_rest, low_first],
        blocks(width // shards, 4 * width),
        [staging(width // shards, 4 * width), low(width, length), dma(4, 2)],
        "wide_gradient",
        hbm_out=range(cores),
    )
    wide_sum = OwnedSum(wide_halves)
    sent = up.plane_two(second, wide_halves)
    sent = down.line_in(sent)
    *roi_halves, low_projected = call(
        functools.partial(project_back_kernel, tokens),
        [tie(places, sent), grad_embedded, projected, sums, second, x],
        blocks(roi_width // shards, width) + [shape((length, width), LOW)],
        [staging(roi_width // shards, width), dma(8)],
        "project_back",
        hbm_out=range(cores),
    )
    roi = OwnedSum(roi_halves)
    sent = wide_sum.plane_one(low_projected)
    sent = down.line_middle(sent)
    sent = up.line_in(sent)
    (roi_grad,) = call(
        functools.partial(input_gradient_kernel, count),
        [tie(places, sent), low_projected, *roi_pieces],
        [shape((length, roi_width))],
        [low(roi_width, width), pltpu.VMEM((length, roi_width), F32), dma(8), dma(8)],
        "input_gradient",
        hbm_in=spaces[2:],
        hbm_out=(0,),
    )
    sent = roi.plane_one(roi_grad)
    sent = wide_sum.plane_two(sent)
    sent = down.line_out(sent)
    sent = up.line_middle(sent)
    sent = roi.plane_two(sent)
    sent = wide_sum.line_in(sent)
    sent = up.line_out(sent)
    sent = roi.line_in(sent)
    sent = wide_sum.line_middle(sent)
    sent = roi.line_middle(sent)
    sent = wide_sum.line_out(sent)
    sent = roi.line_out(sent)
    sum_down, sum_up, sum_wide, sum_roi = [g.owned() for g in (down, up, wide_sum, roi)]
    sum_qkv, sum_out = sum_wide[:, : 3 * width], sum_wide[:, 3 * width :]
    own = lax.dynamic_slice_in_dim(second, own_start, bn_gain.shape[0], 1)
    mean = sums[0] / tokens
    return (
        layer_out[None], roi_grad[None], sum_roi, own[1], own[0], sum_qkv, sum_out, own[2], own[3],
        sum_up, sum_down, own[4], own[5], mean, sums[1] / tokens - mean * mean,
    )


def solution(mesh):
    rows3, rows2, split2, split1 = P(("dp", "shard"), None, None), P(("dp", "shard"), None), P("shard", None), P("shard")
    return jax.shard_map(
        per_device,
        mesh=mesh,
        in_specs=(
            rows3, rows2, split2, split1, split1, split2, split2, split1, split1, split2, split2, split1, split1, rows3,
        ),
        out_specs=(
            rows3, rows3, split2, split1, split1, split2, split2, split1, split1, split2, split2, split1, split1, P(), P(),
        ),
        check_vma=False,
    )
```

```python
import functools
import math

import jax
import jax.numpy as jnp
from jax import lax
from jax.experimental import pallas as pl
from jax.experimental.pallas import tpu as pltpu
from jax.sharding import PartitionSpec as P

HEAD_DIM = 64
EPSILON = 1e-05
SCORE_SCALE = 0.125
MASKED = -1000000000.0
CORE, ACROSS, ALONG = 1, 2, 4
TILE = 256
F32, LOW = jnp.float32, jnp.bfloat16

ERFC_RATE = 0.33
ERFC = (
    0.18636612594127655,
    0.18283699452877045,
    0.20192526280879974,
    0.04500619322061539,
    0.4125494658946991,
    -0.3554469347000122,
    0.46269258856773376,
    -0.13592977821826935,
)


def direct_mesh():
    return lax.axis_size("shard") == 8 and lax.axis_size("dp") == 4


def swap(values, step, axis="shard"):
    size = lax.axis_size(axis)
    return lax.ppermute(values, axis, [(i, i ^ step) for i in range(size)])


def add_low(*terms):
    total = terms[0].astype(F32)
    for term in terms[1:]:
        total = total + term.astype(F32)
    return total.astype(LOW)


def sum_everywhere(part):
    if not direct_mesh():
        return lax.psum(part, ("dp", "shard"))
    part = part + swap(part, CORE)
    part = (part + swap(part, 1, "dp")) + (swap(part, 2, "dp") + swap(part, 3, "dp"))
    return (part + swap(part, ACROSS)) + (swap(part, ALONG) + swap(part, ACROSS | ALONG))


def tie(values, *after):
    return lax.optimization_barrier((values, after))[0]


class OwnedSum:
    def __init__(self, halves):
        self.direct = direct_mesh()
        if self.direct:
            self.mine, self.got = halves[0], swap(halves[1], CORE)
            rows = self.mine.shape[1] // 2
            self.cuts = ((slice(0, rows), 1, 2), (slice(rows, None), 2, 1))
        else:
            whole = halves[0].reshape(-1, halves[0].shape[-1])
            self.part = lax.psum_scatter(whole, "shard", scatter_dimension=0, tiled=True)

    def plane_one(self, *after):
        if not self.direct:
            return self.part
        self.mine, self.got = tie((self.mine, self.got), *after)
        mine, got = self.mine, self.got
        sent = [
            add_low(jnp.stack([mine[near, cut], mine[3, cut]]), jnp.stack([got[near, cut], got[3, cut]]))
            for cut, near, _ in self.cuts
        ]
        self.came = [swap(part, 2 * near) for part, (_, near, _) in zip(sent, self.cuts)]
        return sent

    def plane_two(self, *after):
        if not self.direct:
            return self.part
        self.mine, self.got, self.came = tie((self.mine, self.got, self.came), *after)
        passed = [
            add_low(self.mine[far, cut], self.got[far, cut], came[1]) for came, (cut, _, far) in zip(self.came, self.cuts)
        ]
        self.back = [swap(part, 2 * far) for part, (_, _, far) in zip(passed, self.cuts)]
        return passed

    def plane_done(self, *after):
        if not self.direct:
            return self.part
        mine, got, came, back = tie((self.mine, self.got, self.came, self.back), *after)
        return jnp.concatenate(
            [add_low(mine[0, cut], got[0, cut], c[0], b) for c, b, (cut, _, _) in zip(came, back, self.cuts)]
        )


class LineSum:
    def __init__(self, part):
        self.part = part
        self.pairs = ([(0, 1), (3, 2)], [(1, 2), (2, 1)], [(1, 0), (2, 3)])
        self.number = 0

    def step(self, *after):
        if not direct_mesh():
            return self.part
        if self.number == 0:
            self.part = tie(self.part, *after)
        else:
            self.part = add_low(*tie((self.part, self.came), *after))
        self.came = lax.ppermute(self.part, "dp", self.pairs[self.number])
        self.number += 1
        return self.part

    def total(self):
        if not direct_mesh():
            return lax.psum(self.part, "dp").astype(F32)
        place = lax.axis_index("dp")
        return jnp.where((place == 1) | (place == 2), self.part, self.came).astype(F32)


def dot(left, right, left_dim=1, right_dim=0):
    return lax.dot_general(
        left, right, (((left_dim,), (right_dim,)), ((), ())), preferred_element_type=F32
    )


def wait_all(copies):
    for copy in copies:
        copy.wait()


def start_all(copies):
    for copy in copies:
        copy.start()
    return copies


def part(index, size):
    return pl.ds(pl.multiple_of(index * size, size), size)


def by_rows(count, body):
    @pl.loop(0, count // 128)
    def _(i):
        body(part(i, 128))


def piece_copies(pieces, places, target, sems, source_columns=None, columns=slice(None)):
    copies = []
    for i, piece in enumerate(pieces):
        rows = piece.shape[0]
        source = piece if source_columns is None else piece.at[:, source_columns]
        at = part(places[i], rows) if len(pieces) > 1 else pl.ds(0, rows)
        copies.append(pltpu.make_async_copy(source, target.at[at, columns], sems.at[i]))
    return copies


def put_blocks(halves, places, values, columns, work, section=0):
    if len(halves) == 1:
        halves[0][0, part(section, values.shape[0]), columns] = values.astype(LOW)
        return
    rows = values.shape[0] // 8
    work[...] = values.astype(LOW)
    for rel in range(8):
        halves[rel & 1][rel >> 1, part(section, rows), columns] = work[part(places[rel], rows), :]


def row_blocks(halves, places, make, rows=None):
    chips = halves[0].shape[0]
    rows = rows or halves[0].shape[1]
    if len(halves) == 1:
        step = min(rows, 512)

        @pl.loop(0, rows // step)
        def _(i):
            at = pl.multiple_of(i * step, step)
            halves[0][0, pl.ds(at, step)] = make(at, step).astype(LOW)

        return

    @pl.loop(0, chips)
    def _(j):
        for k in range(2):
            halves[k][j, :rows] = make(places[2 * j + k] * rows, rows).astype(LOW)


def lanes(first, size):
    return pl.ds(pl.multiple_of(first, 128), size)


def batch_scale(sums_ref, tokens):
    mean = sums_ref[0:1, :] * (1.0 / tokens)
    var = sums_ref[1:2, :] * (1.0 / tokens) - mean * mean
    return mean, var, lax.rsqrt(var + EPSILON)


def embed(projected_ref, sums_ref, tokens, rows=slice(None)):
    mean, _, inv = batch_scale(sums_ref, tokens)
    return (projected_ref[rows, :] - mean) * inv * sums_ref[2:3, :] + sums_ref[3:4, :]


def normalize(values):
    center = values - jnp.mean(values, axis=-1, keepdims=True)
    inv = lax.rsqrt(jnp.mean(center * center, axis=-1, keepdims=True) + EPSILON)
    return center * inv, inv


def normalize_back(scaled, normed, inv):
    return inv * (
        scaled
        - jnp.mean(scaled, axis=-1, keepdims=True)
        - normed * jnp.mean(scaled * normed, axis=-1, keepdims=True)
    )


def gelu_pair(values):
    t = 1.0 / (1.0 + (ERFC_RATE * 0.7071067811865476) * jnp.abs(values))
    poly = 0.5 * ERFC[-1]
    for factor in ERFC[-2::-1]:
        poly = poly * t + 0.5 * factor
    bell = jnp.exp(values * values * -0.5)
    tail = poly * t * bell
    share = jnp.where(values < 0, tail, 1.0 - tail)
    return values * share, share + values * bell * 0.3989422804014327


def size_of(array):
    return math.prod(array.shape) * jnp.dtype(array.dtype).itemsize


def call(kernel, args, outs, scratch, name, spare=6, far=(), near=(), out_near=(), sems=()):
    spaces = [pltpu.HBM if i in far else pltpu.VMEM for i in range(len(args))]
    spaces[0] = pltpu.SMEM
    held = [a for i, a in enumerate(args) if i and i not in far and i not in near]
    held += [a for i, a in enumerate(outs) if i not in out_near] + list(scratch)
    args = [
        pltpu.with_memory_space_constraint(a, pltpu.HBM if i in far else pltpu.VMEM) if i in far or i in near else a
        for i, a in enumerate(args)
    ]
    return pl.pallas_call(
        kernel,
        in_specs=[pl.BlockSpec(memory_space=space) for space in spaces],
        out_specs=[pl.BlockSpec(memory_space=pltpu.VMEM)] * len(outs),
        out_shape=[pltpu.VMEM(a.shape, a.dtype) if i in out_near else a for i, a in enumerate(outs)],
        scratch_shapes=list(scratch) + [pltpu.SemaphoreType.DMA(count) for count in sems],
        compiler_params=pltpu.CompilerParams(vmem_limit_bytes=sum(map(size_of, held)) + spare * 2**20),
        cost_estimate=pl.CostEstimate(flops=1024, bytes_accessed=1024, transcendentals=0),
        name=name,
    )(*args)


def shape(dims, kind=F32):
    return jax.ShapeDtypeStruct(tuple(dims), kind)


def column_sum(values):
    return jnp.sum(values, axis=0, keepdims=True)


def project_kernel(count, places, x_ref, params_ref, *refs):
    pieces, (out_ref, sums_ref, weight, sems) = refs[:count], refs[count:]
    wait_all(start_all(piece_copies(pieces, places, weight, sems)))
    sums_ref[...] = params_ref[...]

    @pl.loop(0, out_ref.shape[1] // TILE)
    def _(n):
        cols = part(n, TILE)
        values = dot(x_ref[...], weight[:, cols])
        out_ref[:, cols] = values
        sums_ref[0:1, cols] = column_sum(values)
        sums_ref[1:2, cols] = column_sum(values * values)


def attend_kernel(count, tokens, places, projected_ref, sums_ref, doc_row, doc_col, *refs):
    pieces = refs[:count]
    packed_out, mixed_out, lse_out, weight, embedded, sems = refs[count:]
    length, width = projected_ref.shape

    def fetch(c):
        return piece_copies(pieces, places, weight, sems.at[c], part(c, width), part(c, width))

    for c in range(3):
        start_all(fetch(c))

    @functools.partial(by_rows, length)
    def _(rows):
        embedded[rows, :] = embed(projected_ref, sums_ref, tokens, rows).astype(LOW)

    @pl.loop(0, 3)
    def _(c):
        wait_all(fetch(c))
        for n in range(width // TILE):
            cols = part(c * (width // TILE) + n, TILE)
            packed_out[cols, :] = dot(embedded[...], weight[:, cols]).T.astype(LOW)

    same = doc_col[...] == doc_row[...]
    heads = width // HEAD_DIM

    @pl.loop(0, heads, unroll=3)
    def _(head):
        queries = packed_out[part(head, HEAD_DIM), :] * jnp.asarray(SCORE_SCALE, LOW)
        keys = packed_out[part(head + heads, HEAD_DIM), :]
        values = packed_out[part(head + 2 * heads, HEAD_DIM), :]
        scores = jnp.where(same, dot(keys, queries, 0, 0), MASKED)
        top = jnp.max(scores, axis=0, keepdims=True)
        expo = jnp.exp(scores - top)
        total = jnp.sum(expo, axis=0, keepdims=True)
        mixed = dot(values, expo.astype(LOW)) * (1.0 / total)
        mixed_out[part(head, HEAD_DIM), :] = mixed.astype(LOW)
        lse_out[pl.ds(head, 1), :] = top + jnp.log(total)


def expand_kernel(count, tokens, places, projected_ref, sums_ref, mixed_ref, *refs):
    pieces, ups, refs = refs[:count], refs[count : 2 * count], refs[2 * count :]
    hat_out, inv_out, active_out, slope_out, weight_out, weight_up, low_one, sems_out, sems_up = refs
    length, width = projected_ref.shape
    copies_out = start_all(piece_copies(pieces, places, weight_out, sems_out, pl.ds(3 * width, width)))

    def fetch(c):
        return piece_copies(ups, places, weight_up, sems_up.at[c], part(c, width), part(c, width))

    for c in range(4):
        start_all(fetch(c))
    wait_all(copies_out)
    hat_out[...] = dot(mixed_ref[...], weight_out[...], 0, 0)

    @functools.partial(by_rows, length)
    def _(rows):
        hat, inv = normalize(embed(projected_ref, sums_ref, tokens, rows) + hat_out[rows, :])
        hat_out[rows, :] = hat
        inv_out[rows, :] = inv
        low_one[rows, :] = (hat * sums_ref[4:5, :] + sums_ref[5:6, :]).astype(LOW)

    @pl.loop(0, 4)
    def _(c):
        wait_all(fetch(c))
        for n in range(width // TILE):
            cols = part(c * (width // TILE) + n, TILE)
            active, slope = gelu_pair(dot(low_one[...], weight_up[:, cols]))
            active_out[:, cols] = active.astype(LOW)
            slope_out[:, cols] = slope.astype(LOW)


def contract_kernel(count, places, hat_ref, sums_ref, grad_ref, active_ref, *refs):
    pieces, refs = refs[:count], refs[count:]
    halves, (layer_out, back_out, grads_out, weight, branch, low_back, sems) = refs[:-7], refs[-7:]
    length, width = hat_ref.shape
    copies = start_all(piece_copies(pieces, places, weight, sems))

    @functools.partial(by_rows, length)
    def _(rows):
        branch[rows, :] = hat_ref[rows, :] * sums_ref[4:5, :] + sums_ref[5:6, :]

    wait_all(copies)

    @pl.loop(0, 4)
    def _(c):
        branch[...] += dot(active_ref[:, part(c, width)], weight[part(c, width), :])

    grads_out[...] = jnp.zeros_like(grads_out)

    @functools.partial(by_rows, length)
    def _(rows):
        hat, inv = normalize(branch[rows, :])
        layer_out[rows, :] = (hat * sums_ref[6:7, :] + sums_ref[7:8, :]).astype(LOW)
        gradient = grad_ref[rows, :].astype(F32)
        grads_out[0:1, :] += column_sum(gradient * hat)
        grads_out[1:2, :] += column_sum(gradient)
        back = normalize_back(gradient * sums_ref[6:7, :], hat, inv)
        back_out[rows, :] = back
        low_back[rows, :] = back.astype(LOW)

    row_blocks(halves, places, lambda at, n: dot(active_ref[:, lanes(at, n)], low_back[...], 0, 0))


def hidden_back_kernel(count, places, back_ref, hat_ref, sums_ref, slope_ref, *refs):
    pieces, refs = refs[:count], refs[count:]
    halves, (hidden_out, weight, low_back, low_one, work, sems) = refs[:-6], refs[-6:]
    length, width = hat_ref.shape
    copies = start_all(piece_copies(pieces, places, weight, sems))

    @functools.partial(by_rows, length)
    def _(rows):
        low_back[rows, :] = back_ref[rows, :].astype(LOW)
        low_one[:, rows] = (hat_ref[rows, :] * sums_ref[4:5, :] + sums_ref[5:6, :]).T.astype(LOW)

    wait_all(copies)

    @pl.loop(0, 4)
    def _(c):
        for n in range(width // TILE):
            cols = part(c * (width // TILE) + n, TILE)
            values = (dot(low_back[...], weight[cols, :], 1, 1) * slope_ref[:, cols].astype(F32)).astype(LOW)
            hidden_out[:, cols] = values
            put_blocks(halves, places, dot(low_one[...], values), slice(n * TILE, (n + 1) * TILE), work.at[n % 2], c)


def attend_back_head(head, first_head, packed_ref, mixed_back, lse_ref, same, out_ref, step, start):
    width = packed_ref.shape[0] // 3
    at = part(head + first_head, HEAD_DIM)
    queries = packed_ref[at, :] * jnp.asarray(SCORE_SCALE, LOW)
    at = part(head + first_head + width // HEAD_DIM, HEAD_DIM)
    keys = packed_ref[at, :]
    at = part(head + first_head + 2 * width // HEAD_DIM, HEAD_DIM)
    values = packed_ref[at, :]
    scores = jnp.where(same, dot(keys, queries, 0, 0), MASKED)
    probs = jnp.exp(scores - lse_ref[pl.ds(head + first_head, 1), :])
    grad_probs = dot(values, mixed_back, 0, 0)
    grad_values = dot(mixed_back, probs.astype(LOW), 1, 1)
    inner = jnp.sum(probs * grad_probs, axis=0, keepdims=True)
    grad_scores = (probs * (grad_probs - inner)).astype(LOW)
    grad_queries = dot(keys, grad_scores) * SCORE_SCALE
    grad_keys = dot(queries, grad_scores, 1, 1)
    for i, grad in enumerate((grad_queries, grad_keys, grad_values)):
        out_ref[part((i * step + start) // HEAD_DIM + head, HEAD_DIM), :] = grad.astype(LOW)


def expand_back_kernel(
    count, places, back_ref, hat_ref, inv_ref, sums_ref, hidden_ref, packed_ref, lse_ref, doc_row, doc_col, *refs
):
    pieces, ups, refs = refs[:count], refs[count : 2 * count], refs[2 * count :]
    (
        first_out, low_out, mixed_back_out, grads_out, grad_packed_out, weight_out, weight_up, total, sems_out, sems_up
    ) = refs
    length, width = hat_ref.shape

    def fetch(c):
        return piece_copies(ups, places, weight_up, sems_up.at[c], part(c, width), part(c, width))

    for c in range(4):
        start_all(fetch(c))
    copies_out = start_all(piece_copies(pieces, places, weight_out, sems_out, pl.ds(3 * width, width)))
    total[...] = back_ref[...]

    @pl.loop(0, 4)
    def _(c):
        wait_all(fetch(c))
        total[...] += dot(hidden_ref[:, part(c, width)], weight_up[:, part(c, width)], 1, 1)

    grads_out[...] = jnp.zeros_like(grads_out)

    @functools.partial(by_rows, length)
    def _(rows):
        gradient, hat = total[rows, :], hat_ref[rows, :]
        grads_out[0:1, :] += column_sum(gradient * hat)
        grads_out[1:2, :] += column_sum(gradient)
        first = normalize_back(gradient * sums_ref[4:5, :], hat, inv_ref[rows, :])
        first_out[rows, :] = first
        low_out[rows, :] = first.astype(LOW)

    wait_all(copies_out)
    mixed_back_out[...] = dot(weight_out[...], low_out[...], 1, 1).astype(LOW)
    same = doc_col[...] == doc_row[...]
    heads = grad_packed_out.shape[0] // (3 * HEAD_DIM)

    @pl.loop(0, heads, unroll=3)
    def _(head):
        mixed_back = mixed_back_out[part(head, HEAD_DIM), :]
        attend_back_head(head, 0, packed_ref, mixed_back, lse_ref, same, grad_packed_out, heads * HEAD_DIM, 0)


def attend_back_kernel(
    count, tokens, places, packed_ref, mixed_back_ref, lse_ref, doc_row, doc_col, projected_ref, sums_ref, first_ref,
    done_ref, *refs
):
    pieces = refs[:count]
    grad_packed_out, embedded_out, grads_out, weight, sems = refs[count:]
    length, width = projected_ref.shape
    copies = start_all(piece_copies(pieces, places, weight, sems, pl.ds(0, 3 * width)))
    same = doc_col[...] == doc_row[...]
    done = done_ref.shape[0] // 3

    @pl.loop(0, (width - done) // HEAD_DIM, unroll=3)
    def _(head):
        mixed_back = mixed_back_ref[part(head + done // HEAD_DIM, HEAD_DIM), :]
        attend_back_head(head, done // HEAD_DIM, packed_ref, mixed_back, lse_ref, same, grad_packed_out, width, done)

    for i in range(3):
        grad_packed_out[i * width : i * width + done, :] = done_ref[i * done : (i + 1) * done, :]
    wait_all(copies)
    mean, _, inv = batch_scale(sums_ref, tokens)
    for n in range(width // TILE):
        cols = slice(n * TILE, (n + 1) * TILE)
        values = first_ref[:, cols] + dot(weight[cols, :], grad_packed_out[...]).T
        embedded_out[:, cols] = values
        normed = (projected_ref[:, cols] - mean[:, cols]) * inv[:, cols]
        grads_out[0:1, cols] = column_sum(values)
        grads_out[1:2, cols] = column_sum(values * normed)


def packed_gradient_kernel(tokens, places, grad_packed_ref, projected_ref, sums_ref, *refs):
    halves, (low, work) = refs[:-2], refs[-2:]
    length, width = projected_ref.shape

    @functools.partial(by_rows, length)
    def _(rows):
        low[:, rows] = embed(projected_ref, sums_ref, tokens, rows).T.astype(LOW)

    @pl.loop(0, 3)
    def _(c):
        for n in range(width // TILE):
            cols = part(c * (width // TILE) + n, TILE)
            put_blocks(halves, places, dot(low[...], grad_packed_ref[cols, :], 1, 1), cols, work.at[n % 2])


def project_back_kernel(tokens, places, embedded_ref, projected_ref, sums_ref, grads_ref, mixed_ref, low_ref, x_ref, *refs):
    halves, (low_out, work) = refs[:-2], refs[-2:]
    mean, _, inv = batch_scale(sums_ref, tokens)
    roi_rows = x_ref.shape[1] * halves[0].shape[1] // (x_ref.shape[1] + low_ref.shape[1])

    @functools.partial(by_rows, projected_ref.shape[0])
    def _(rows):
        normed = (projected_ref[rows, :] - mean) * inv
        shift = grads_ref[0:1, :] * (1.0 / tokens) + normed * (grads_ref[1:2, :] * (1.0 / tokens))
        low_out[rows, :] = (sums_ref[2:3, :] * inv * (embedded_ref[rows, :] - shift)).astype(LOW)

    row_blocks(halves, places, lambda at, n: dot(x_ref[:, lanes(at, n)], low_out[...], 0, 0), roi_rows)
    work[...] = dot(mixed_ref[...], low_ref[...]).astype(LOW)
    if len(halves) == 1:
        halves[0][0, roi_rows:, :] = work[...]
    else:
        rows = halves[0].shape[1] - roi_rows
        for rel in range(8):
            halves[rel & 1][rel >> 1, roi_rows:, :] = work[part(places[rel], rows), :]


def input_gradient_kernel(count, places, low_ref, *refs):
    pieces, (out_ref, weight, sems) = refs[:count], refs[count:]
    wait_all(start_all(piece_copies(pieces, places, weight, sems)))

    @pl.loop(0, weight.shape[0] // 512)
    def _(i):
        out_ref[:, part(i, 512)] = dot(low_ref[...], weight[part(i, 512), :], 1, 1)


def sides(own):
    return [swap(own, ACROSS), swap(own, ALONG)]


def corner_halves(across, along):
    half = across.shape[0] // 2
    return [swap(along[:half], ACROSS), swap(across[half:], ALONG)]


def with_cores(chips):
    pieces = []
    for shard in chips:
        pieces += [shard, swap(shard, CORE)]
    return pieces


def per_device(
    roi_features, doc_ids, w_roi, bn_gain, bn_beta, w_qkv, w_out, ln1_gain, ln1_beta,
    w_up, w_down, ln2_gain, ln2_beta, cotangent,
):
    _, length, roi_width = roi_features.shape
    width, hidden = w_roi.shape[1], w_up.shape[1]
    devices = lax.axis_size("dp") * lax.axis_size("shard")
    tokens = length * devices
    me = lax.axis_index("shard")
    direct = direct_mesh()
    shards, rows = 8 if direct else 1, w_up.shape[0]
    cores, chips = (2, 4) if direct else (1, 1)
    places = (me ^ jnp.arange(8)).astype(jnp.int32) if direct else jnp.zeros((8,), jnp.int32)

    x = roi_features.reshape(length, roi_width)
    doc_row, doc_col = doc_ids.reshape(1, length), doc_ids.reshape(length, 1)
    own_params = jnp.stack([bn_gain, bn_beta, ln1_gain, ln1_beta, ln2_gain, ln2_beta]).astype(F32)
    own_params = jnp.where(lax.axis_index("dp") == 0, own_params, 0.0)
    own_start = me * bn_gain.shape[0]
    params = lax.dynamic_update_slice(jnp.zeros((8, width), F32), own_params, (2, own_start))

    gather = functools.partial(lax.all_gather, axis_name="shard", axis=0, tiled=True)
    wide = jnp.concatenate([w_qkv, w_out], axis=1)
    if direct:
        roi_chips = [w_roi, *sides(w_roi), swap(w_roi, ACROSS | ALONG)]
        wide = tie(wide, params)
        wide_chips = [wide, *sides(wide), swap(wide, ACROSS | ALONG)]
        roi_pieces = with_cores(tie(roi_chips, wide))
    else:
        roi_pieces = [gather(w_roi)]
    count = len(roi_pieces)

    def blocks(r, c):
        return [shape((chips, r, c), LOW)] * cores

    def low(r, c):
        return pltpu.VMEM((r, c), LOW)

    projected, sums = call(
        functools.partial(project_kernel, count),
        [places, x, params, *roi_pieces],
        [shape((length, width)), shape((8, width))],
        [low(roi_width, width)],
        "project",
        out_near=(0,),
        far=range(3, 100),
        sems=((8,),),
    )
    if direct:
        sums = sums + swap(sums, CORE)
        sums = sums + swap(sums, 1, "dp")
        sums = sums + swap(sums, 2, "dp")
        around = [swap(sums, ACROSS), swap(sums, ALONG), swap(sums, ACROSS | ALONG)]
        wide_chips = tie(wide_chips, sums)
        around = tie(around, wide_chips)
        sums = (sums + around[0]) + (around[1] + around[2])
        wide_pieces = with_cores(wide_chips)
        up_sides = sides(tie(w_up, sums))
    else:
        sums = lax.psum(sums, ("dp", "shard"))
        wide_pieces = [gather(wide)]

    heads = width // HEAD_DIM
    part_width = heads // 2 * HEAD_DIM
    packed_qkv, mixed, lse = call(
        functools.partial(attend_kernel, count, tokens),
        [places, projected, sums, doc_row, doc_col, *wide_pieces],
        [shape((3 * width, length), LOW), shape((width, length), LOW), shape((heads, length))],
        [low(width, 3 * width), low(length, width)],
        "attend",
        near=(1,), out_near=(0, 1, 2),
        far=range(5, 100),
        sems=((3, 8),),
    )
    if direct:
        up_sides = tie(up_sides, mixed)
        up_corner = jnp.concatenate(corner_halves(*up_sides))
        down_sides = sides(tie(w_down, up_sides))
        up_pieces = with_cores([w_up, *up_sides, up_corner])
    else:
        up_pieces, down_parts = [gather(w_up)], [gather(w_down)]
    hat, inv, active, slope = call(
        functools.partial(expand_kernel, count, tokens),
        [places, projected, sums, mixed, *wide_pieces, *up_pieces],
        [shape((length, width)), shape((length, 1)), shape((length, hidden), LOW), shape((length, hidden), LOW)],
        [low(width, width), low(width, hidden), low(length, width)],
        "expand",
        near=(1, 3), out_near=(0, 1, 2, 3),
        far=range(4, 100),
        sems=((8,), (4, 8)),
    )
    if direct:
        down_sides = tie(down_sides, active)
        down_parts = with_cores([w_down, *down_sides, jnp.concatenate(corner_halves(*down_sides))])
    *down_halves, layer_out, back, grads_two = call(
        functools.partial(contract_kernel, count),
        [places, hat, sums, cotangent.reshape(length, width), active, *down_parts],
        blocks(hidden // shards, width) + [shape((length, width), LOW), shape((length, width)), shape((2, width))],
        [low(hidden, width), pltpu.VMEM((length, width), F32), low(length, width)],
        "contract",
        near=(1, 4), out_near=(cores + 1,),
        far=range(5, 100),
        sems=((8,),),
    )
    down = OwnedSum(down_halves)
    *up_halves, grad_hidden = call(
        functools.partial(hidden_back_kernel, count),
        [places, back, hat, sums, slope, *down_parts],
        blocks(hidden // shards, width) + [shape((length, hidden), LOW)],
        [low(hidden, width), low(length, width), low(width, length), pltpu.VMEM((2, width, TILE), LOW)],
        "hidden_back",
        near=(1, 2, 4), out_near=(cores,),
        far=range(5, 100),
        sems=((8,),),
    )
    up = OwnedSum(up_halves)
    sent = down.plane_one(grad_hidden)
    first, low_first, mixed_back, grads_one, grad_part = call(
        functools.partial(expand_back_kernel, count),
        [
            tie(places, sent), back, hat, inv, sums, grad_hidden, packed_qkv, lse, doc_row, doc_col,
            *wide_pieces, *up_pieces,
        ],
        [
            shape((length, width)), shape((length, width), LOW), shape((width, length), LOW), shape((2, width)),
            shape((3 * part_width, length), LOW),
        ],
        [low(width, width), low(width, hidden), pltpu.VMEM((length, width), F32)],
        "expand_back",
        near=(1, 2, 3, 5, 6, 7), out_near=(0, 1, 2, 4),
        far=range(10, 100),
        sems=((8,), (4, 8)),
    )
    sent = down.plane_two(first)
    sent = up.plane_one(sent)
    grad_packed, grad_embedded, grads_bn = call(
        functools.partial(attend_back_kernel, count, tokens),
        [
            tie(places, sent), packed_qkv, mixed_back, lse, doc_row, doc_col, projected, sums, first, grad_part,
            *wide_pieces,
        ],
        [shape((3 * width, length), LOW), shape((length, width)), shape((2, width))],
        [low(width, 3 * width)],
        "attend_back",
        near=(1, 2, 3, 6, 8, 9), out_near=(0, 1),
        far=range(10, 100),
        sems=((8,),),
    )
    second = jnp.concatenate([grads_bn, grads_one, grads_two, jnp.zeros((2, width), F32)])
    if direct:
        second = second + swap(tie(second, down.back), CORE)
        second = second + swap(second, 1, "dp")
        second = second + swap(second, 2, "dp")
        second = tie(second, up.came)
        around = [swap(second, ACROSS), swap(second, ALONG), swap(second, ACROSS | ALONG)]
        sent = up.plane_two(second)
        down_sum = LineSum(down.plane_done(sent))
        around = tie(around, sent, down_sum.step())
        second = (second + around[0]) + (around[1] + around[2])
    else:
        second = lax.psum(second, ("dp", "shard"))
    roi_rows, out_rows = roi_width // shards, width // shards
    *roi_halves, low_projected = call(
        functools.partial(project_back_kernel, tokens),
        [places, grad_embedded, projected, sums, second, mixed, low_first, x],
        blocks(roi_rows + out_rows, width) + [shape((length, width), LOW)],
        [low(width, width)],
        "project_back",
        near=(1, 2, 5, 6), out_near=(cores,),
    )
    roi = OwnedSum(roi_halves)
    start_packed = tie(places, low_projected)
    qkv_halves = call(
        functools.partial(packed_gradient_kernel, tokens),
        [start_packed, grad_packed, projected, sums],
        blocks(width // shards, 3 * width),
        [low(width, length), pltpu.VMEM((2, width, TILE), LOW)],
        "packed_gradient",
        near=(1, 2),
    )
    qkv = OwnedSum(qkv_halves)
    sent = roi.plane_one(qkv_halves)
    if direct:
        up_sum = LineSum(up.plane_done(sent))
        sent = up_sum.step()
    (roi_grad,) = call(
        functools.partial(input_gradient_kernel, count),
        [tie(places, sent), low_projected, *roi_pieces],
        [shape((length, roi_width))],
        [low(roi_width, width)],
        "input_gradient",
        near=(1,),
        far=range(2, 100),
        sems=((8,),),
    )
    if direct:
        sent = roi.plane_two(down_sum.step(roi_grad))
        sent = qkv.plane_one(sent)
        sent = down_sum.step(up_sum.step(sent))
        roi_sum = LineSum(roi.plane_done(sent))
        sent = roi_sum.step()
        sent = qkv.plane_two(sent)
        sent = up_sum.step(sent)
        sent = roi_sum.step(sent)
        qkv_sum = LineSum(qkv.plane_done(sent))
        sent = qkv_sum.step()
        sent = roi_sum.step(sent)
        sent = qkv_sum.step(sent)
        sent = qkv_sum.step(sent)
        sum_roi, sum_down, sum_up, sum_qkv = [g.total() for g in (roi_sum, down_sum, up_sum, qkv_sum)]
        sum_roi, sum_out = sum_roi[:roi_rows], sum_roi[roi_rows:]
        sum_up = jnp.concatenate([sum_up[i * rows : (i + 1) * rows] for i in range(4)], axis=1)
    else:
        grads = [roi_halves[0][0, :roi_rows], roi_halves[0][0, roi_rows:], down_halves[0][0], qkv_halves[0][0]]
        grads.append(up_halves[0][0].reshape(4, width, width).swapaxes(0, 1).reshape(width, hidden))
        sum_roi, sum_out, sum_down, sum_qkv, sum_up = [
            lax.psum(lax.psum_scatter(grad, "shard", scatter_dimension=0, tiled=True), "dp").astype(F32) for grad in grads
        ]
    own = lax.dynamic_slice_in_dim(second, own_start, bn_gain.shape[0], 1)
    mean = sums[0] / tokens
    return (
        layer_out[None], roi_grad[None], sum_roi, own[1], own[0], sum_qkv, sum_out, own[2], own[3],
        sum_up, sum_down, own[4], own[5], mean, sums[1] / tokens - mean * mean,
    )


def solution(mesh):
    rows3, rows2, split2, split1 = P(("dp", "shard"), None, None), P(("dp", "shard"), None), P("shard", None), P("shard")
    return jax.shard_map(
        per_device,
        mesh=mesh,
        in_specs=(
            rows3, rows2, split2, split1, split1, split2, split2, split1, split1, split2, split2, split1, split1, rows3,
        ),
        out_specs=(
            rows3, rows3, split2, split1, split1, split2, split2, split1, split1, split2, split2, split1, split1, P(), P(),
        ),
        check_vma=False,
    )
```

```python
import functools
import math

import jax
import jax.numpy as jnp
from jax import lax
from jax.experimental import pallas as pl
from jax.experimental.pallas import tpu as pltpu
from jax.sharding import PartitionSpec as P

HEAD_DIM = 64
EPSILON = 1e-05
SCORE_SCALE = 0.125
MASKED = -1000000000.0
CORE, ACROSS, ALONG = 1, 2, 4
TILE = 256
F32, LOW = jnp.float32, jnp.bfloat16

ERFC_RATE = 0.33
ERFC = (
    0.18636612594127655,
    0.18283699452877045,
    0.20192526280879974,
    0.04500619322061539,
    0.4125494658946991,
    -0.3554469347000122,
    0.46269258856773376,
    -0.13592977821826935,
)


def direct_mesh():
    return lax.axis_size("shard") == 8 and lax.axis_size("dp") == 4


def swap(values, step, axis="shard"):
    size = lax.axis_size(axis)
    return lax.ppermute(values, axis, [(i, i ^ step) for i in range(size)])


def add_low(*terms):
    total = terms[0].astype(F32)
    for term in terms[1:]:
        total = total + term.astype(F32)
    return total.astype(LOW)


def sum_everywhere(part):
    if not direct_mesh():
        return lax.psum(part, ("dp", "shard"))
    part = part + swap(part, CORE)
    part = (part + swap(part, 1, "dp")) + (swap(part, 2, "dp") + swap(part, 3, "dp"))
    return (part + swap(part, ACROSS)) + (swap(part, ALONG) + swap(part, ACROSS | ALONG))


def tie(values, *after):
    return lax.optimization_barrier((values, after))[0]


class OwnedSum:
    def __init__(self, halves):
        self.direct = direct_mesh()
        if self.direct:
            self.mine, self.got = halves[0], swap(halves[1], CORE)
            rows = self.mine.shape[1] // 2
            self.cuts = ((slice(0, rows), 1, 2), (slice(rows, None), 2, 1))
        else:
            whole = halves[0].reshape(-1, halves[0].shape[-1])
            self.part = lax.psum_scatter(whole, "shard", scatter_dimension=0, tiled=True)

    def plane_one(self, *after):
        if not self.direct:
            return self.part
        self.mine, self.got = tie((self.mine, self.got), *after)
        mine, got = self.mine, self.got
        sent = [
            add_low(jnp.stack([mine[near, cut], mine[3, cut]]), jnp.stack([got[near, cut], got[3, cut]]))
            for cut, near, _ in self.cuts
        ]
        self.came = [swap(part, 2 * near) for part, (_, near, _) in zip(sent, self.cuts)]
        return sent

    def plane_two(self, *after):
        if not self.direct:
            return self.part
        self.mine, self.got, self.came = tie((self.mine, self.got, self.came), *after)
        passed = [
            add_low(self.mine[far, cut], self.got[far, cut], came[1]) for came, (cut, _, far) in zip(self.came, self.cuts)
        ]
        self.back = [swap(part, 2 * far) for part, (_, _, far) in zip(passed, self.cuts)]
        return passed

    def plane_done(self, *after):
        if not self.direct:
            return self.part
        mine, got, came, back = tie((self.mine, self.got, self.came, self.back), *after)
        return jnp.concatenate(
            [add_low(mine[0, cut], got[0, cut], c[0], b) for c, b, (cut, _, _) in zip(came, back, self.cuts)]
        )


class LineSum:
    def __init__(self, part):
        self.part = part
        self.pairs = ([(0, 1), (3, 2)], [(1, 2), (2, 1)], [(1, 0), (2, 3)])
        self.number = 0

    def step(self, *after):
        if not direct_mesh():
            return self.part
        if self.number == 0:
            self.part = tie(self.part, *after)
        else:
            self.part = add_low(*tie((self.part, self.came), *after))
        self.came = lax.ppermute(self.part, "dp", self.pairs[self.number])
        self.number += 1
        return self.part

    def total(self):
        if not direct_mesh():
            return lax.psum(self.part, "dp").astype(F32)
        place = lax.axis_index("dp")
        return jnp.where((place == 1) | (place == 2), self.part, self.came).astype(F32)


def dot(left, right, left_dim=1, right_dim=0):
    return lax.dot_general(
        left, right, (((left_dim,), (right_dim,)), ((), ())), preferred_element_type=F32
    )


def wait_all(copies):
    for copy in copies:
        copy.wait()


def start_all(copies):
    for copy in copies:
        copy.start()
    return copies


def part(index, size):
    return pl.ds(pl.multiple_of(index * size, size), size)


def by_rows(count, body):
    @pl.loop(0, count // 128)
    def _(i):
        body(part(i, 128))


def piece_copies(pieces, places, target, sems, source_columns=None, columns=slice(None)):
    copies = []
    for i, piece in enumerate(pieces):
        rows = piece.shape[0]
        source = piece if source_columns is None else piece.at[:, source_columns]
        at = part(places[i], rows) if len(pieces) > 1 else pl.ds(0, rows)
        copies.append(pltpu.make_async_copy(source, target.at[at, columns], sems.at[i]))
    return copies


def wait_chunk(count, copies, places, target, sems, c):
    if count == 1:
        return c
    rows = target.shape[0] // 8
    for k in range(2):
        at = target.at[part(places[2 * c + k], rows)]
        pltpu.make_async_copy(at, at, sems.at[2 * c + k]).wait()
    return places[2 * c] >> 1


def put_blocks(halves, places, values, columns, work, section=0):
    if len(halves) == 1:
        halves[0][0, part(section, values.shape[0]), columns] = values.astype(LOW)
        return
    rows = values.shape[0] // 8
    work[...] = values.astype(LOW)
    for rel in range(8):
        halves[rel & 1][rel >> 1, part(section, rows), columns] = work[part(places[rel], rows), :]


def row_blocks(halves, places, make, rows=None):
    chips = halves[0].shape[0]
    rows = rows or halves[0].shape[1]
    if len(halves) == 1:
        step = min(rows, 512)

        @pl.loop(0, rows // step)
        def _(i):
            at = pl.multiple_of(i * step, step)
            halves[0][0, pl.ds(at, step)] = make(at, step).astype(LOW)

        return

    @pl.loop(0, chips)
    def _(j):
        for k in range(2):
            halves[k][j, :rows] = make(places[2 * j + k] * rows, rows).astype(LOW)


def lanes(first, size):
    return pl.ds(pl.multiple_of(first, 128), size)


def batch_scale(sums_ref, tokens):
    mean = sums_ref[0:1, :] * (1.0 / tokens)
    var = sums_ref[1:2, :] * (1.0 / tokens) - mean * mean
    return mean, var, lax.rsqrt(var + EPSILON)


def embed(projected_ref, sums_ref, tokens, rows=slice(None)):
    mean, _, inv = batch_scale(sums_ref, tokens)
    return (projected_ref[rows, :] - mean) * inv * sums_ref[2:3, :] + sums_ref[3:4, :]


def normalize(values):
    center = values - jnp.mean(values, axis=-1, keepdims=True)
    inv = lax.rsqrt(jnp.mean(center * center, axis=-1, keepdims=True) + EPSILON)
    return center * inv, inv


def normalize_back(scaled, normed, inv):
    return inv * (
        scaled
        - jnp.mean(scaled, axis=-1, keepdims=True)
        - normed * jnp.mean(scaled * normed, axis=-1, keepdims=True)
    )


def gelu_pair(values):
    t = 1.0 / (1.0 + (ERFC_RATE * 0.7071067811865476) * jnp.abs(values))
    poly = 0.5 * ERFC[-1]
    for factor in ERFC[-2::-1]:
        poly = poly * t + 0.5 * factor
    bell = jnp.exp(values * values * -0.5)
    tail = poly * t * bell
    share = jnp.where(values < 0, tail, 1.0 - tail)
    return values * share, share + values * bell * 0.3989422804014327


def size_of(array):
    return math.prod(array.shape) * jnp.dtype(array.dtype).itemsize


def call(kernel, args, outs, scratch, name, spare=6, far=(), loose=(), near=(), out_near=(), sems=()):
    spaces = [pl.ANY if i in loose else pltpu.HBM if i in far else pltpu.VMEM for i in range(len(args))]
    spaces[0] = pltpu.SMEM
    held = [a for i, a in enumerate(args) if i and i not in far and i not in near]
    held += [a for i, a in enumerate(outs) if i not in out_near] + list(scratch)
    args = [
        pltpu.with_memory_space_constraint(a, pltpu.HBM if i in far else pltpu.VMEM)
        if (i in far and i not in loose) or i in near
        else a
        for i, a in enumerate(args)
    ]
    return pl.pallas_call(
        kernel,
        in_specs=[pl.BlockSpec(memory_space=space) for space in spaces],
        out_specs=[pl.BlockSpec(memory_space=pltpu.VMEM)] * len(outs),
        out_shape=[pltpu.VMEM(a.shape, a.dtype) if i in out_near else a for i, a in enumerate(outs)],
        scratch_shapes=list(scratch) + [pltpu.SemaphoreType.DMA(count) for count in sems],
        compiler_params=pltpu.CompilerParams(vmem_limit_bytes=sum(map(size_of, held)) + spare * 2**20),
        cost_estimate=pl.CostEstimate(flops=1024, bytes_accessed=1024, transcendentals=0),
        name=name,
    )(*args)


def shape(dims, kind=F32):
    return jax.ShapeDtypeStruct(tuple(dims), kind)


def column_sum(values):
    return jnp.sum(values, axis=0, keepdims=True)


def project_kernel(count, places, x_ref, params_ref, *refs):
    pieces, (out_ref, sums_ref, weight, x, sems, sems_x) = refs[:count], refs[count:]
    copies = start_all([pltpu.make_async_copy(x_ref, x, sems_x.at[0])])
    wait_all(start_all(piece_copies(pieces, places, weight, sems)) + copies)
    sums_ref[...] = params_ref[...]

    @pl.loop(0, out_ref.shape[1] // TILE)
    def _(n):
        cols = part(n, TILE)
        values = dot(x[...], weight[:, cols])
        out_ref[:, cols] = values
        sums_ref[0:1, cols] = column_sum(values)
        sums_ref[1:2, cols] = column_sum(values * values)


def attend_kernel(count, tokens, places, projected_ref, sums_ref, doc_row, doc_col, *refs):
    pieces = refs[:count]
    packed_out, mixed_out, lse_out, weight, embedded, sems = refs[count:]
    length, width = projected_ref.shape

    def fetch(c):
        return piece_copies(pieces, places, weight, sems.at[c], part(c, width), part(c, width))

    for c in range(3):
        start_all(fetch(c))

    @functools.partial(by_rows, length)
    def _(rows):
        embedded[rows, :] = embed(projected_ref, sums_ref, tokens, rows).astype(LOW)

    @pl.loop(0, 3)
    def _(c):
        wait_all(fetch(c))
        for n in range(width // TILE):
            cols = part(c * (width // TILE) + n, TILE)
            packed_out[cols, :] = dot(embedded[...], weight[:, cols]).T.astype(LOW)

    same = doc_col[...] == doc_row[...]
    heads = width // HEAD_DIM

    @pl.loop(0, heads, unroll=3)
    def _(head):
        queries = packed_out[part(head, HEAD_DIM), :] * jnp.asarray(SCORE_SCALE, LOW)
        keys = packed_out[part(head + heads, HEAD_DIM), :]
        values = packed_out[part(head + 2 * heads, HEAD_DIM), :]
        scores = jnp.where(same, dot(keys, queries, 0, 0), MASKED)
        top = jnp.max(scores, axis=0, keepdims=True)
        expo = jnp.exp(scores - top)
        total = jnp.sum(expo, axis=0, keepdims=True)
        mixed = dot(values, expo.astype(LOW)) * (1.0 / total)
        mixed_out[part(head, HEAD_DIM), :] = mixed.astype(LOW)
        lse_out[pl.ds(head, 1), :] = top + jnp.log(total)


def expand_kernel(count, tokens, places, projected_ref, sums_ref, mixed_ref, *refs):
    ups, refs = refs[:count], refs[count:]
    hat_out, inv_out, active_out, slope_out, weight_out, weight_up, low_one, sems_out, sems_up = refs
    length, width = projected_ref.shape
    copies_out = start_all(piece_copies(ups, places, weight_out, sems_out, pl.ds(4 * width, width)))

    def fetch(c):
        return piece_copies(ups, places, weight_up, sems_up.at[c], part(c, width), part(c, width))

    for c in range(4):
        start_all(fetch(c))
    wait_all(copies_out)
    hat_out[...] = dot(mixed_ref[...], weight_out[...], 0, 0)

    @functools.partial(by_rows, length)
    def _(rows):
        hat, inv = normalize(embed(projected_ref, sums_ref, tokens, rows) + hat_out[rows, :])
        hat_out[rows, :] = hat
        inv_out[rows, :] = inv
        low_one[rows, :] = (hat * sums_ref[4:5, :] + sums_ref[5:6, :]).astype(LOW)

    @pl.loop(0, 4)
    def _(c):
        wait_all(fetch(c))
        for n in range(width // TILE):
            cols = part(c * (width // TILE) + n, TILE)
            active, slope = gelu_pair(dot(low_one[...], weight_up[:, cols]))
            active_out[:, cols] = active.astype(LOW)
            slope_out[:, cols] = slope.astype(LOW)


def contract_kernel(count, places, hat_ref, sums_ref, active_ref, grad_ref, *refs):
    pieces, refs = refs[:count], refs[count:]
    halves, refs = refs[:-9], refs[-9:]
    layer_out, back_out, grads_out, weight, branch, low_back, grad, sems, sems_grad = refs
    length, width = hat_ref.shape
    copies = start_all(piece_copies(pieces, places, weight, sems))
    grad_copy = start_all([pltpu.make_async_copy(grad_ref, grad, sems_grad.at[0])])
    if count == 1:
        wait_all(copies)

    @functools.partial(by_rows, length)
    def _(rows):
        branch[rows, :] = hat_ref[rows, :] * sums_ref[4:5, :] + sums_ref[5:6, :]

    @pl.loop(0, 4)
    def _(i):
        c = wait_chunk(count, copies, places, weight, sems, i)
        branch[...] += dot(active_ref[:, part(c, width)], weight[part(c, width), :])

    wait_all(grad_copy)
    grads_out[...] = jnp.zeros_like(grads_out)

    @functools.partial(by_rows, length)
    def _(rows):
        hat, inv = normalize(branch[rows, :])
        layer_out[rows, :] = (hat * sums_ref[6:7, :] + sums_ref[7:8, :]).astype(LOW)
        gradient = grad[rows, :].astype(F32)
        grads_out[0:1, :] += column_sum(gradient * hat)
        grads_out[1:2, :] += column_sum(gradient)
        back = normalize_back(gradient * sums_ref[6:7, :], hat, inv)
        back_out[rows, :] = back
        low_back[rows, :] = back.astype(LOW)

    row_blocks(halves, places, lambda at, n: dot(active_ref[:, lanes(at, n)], low_back[...], 0, 0))


def hidden_back_kernel(count, places, back_ref, hat_ref, sums_ref, slope_ref, *refs):
    pieces, refs = refs[:count], refs[count:]
    halves, (hidden_out, weight, low_back, low_one, work, sems) = refs[:-6], refs[-6:]
    length, width = hat_ref.shape
    copies = start_all(piece_copies(pieces, places, weight, sems))

    @functools.partial(by_rows, length)
    def _(rows):
        low_back[rows, :] = back_ref[rows, :].astype(LOW)
        low_one[:, rows] = (hat_ref[rows, :] * sums_ref[4:5, :] + sums_ref[5:6, :]).T.astype(LOW)

    if count == 1:
        wait_all(copies)

    @pl.loop(0, 4)
    def _(i):
        c = wait_chunk(count, copies, places, weight, sems, i)
        for n in range(width // TILE):
            cols = part(c * (width // TILE) + n, TILE)
            values = (dot(low_back[...], weight[cols, :], 1, 1) * slope_ref[:, cols].astype(F32)).astype(LOW)
            hidden_out[:, cols] = values
            put_blocks(halves, places, dot(low_one[...], values), slice(n * TILE, (n + 1) * TILE), work.at[n % 2], c)


def attend_back_head(head, first_head, packed_ref, mixed_back, lse_ref, same, out_ref, step, start):
    width = packed_ref.shape[0] // 3
    at = part(head + first_head, HEAD_DIM)
    queries = packed_ref[at, :] * jnp.asarray(SCORE_SCALE, LOW)
    at = part(head + first_head + width // HEAD_DIM, HEAD_DIM)
    keys = packed_ref[at, :]
    at = part(head + first_head + 2 * width // HEAD_DIM, HEAD_DIM)
    values = packed_ref[at, :]
    scores = jnp.where(same, dot(keys, queries, 0, 0), MASKED)
    probs = jnp.exp(scores - lse_ref[pl.ds(head + first_head, 1), :])
    grad_probs = dot(values, mixed_back, 0, 0)
    grad_values = dot(mixed_back, probs.astype(LOW), 1, 1)
    inner = jnp.sum(probs * grad_probs, axis=0, keepdims=True)
    grad_scores = (probs * (grad_probs - inner)).astype(LOW)
    grad_queries = dot(keys, grad_scores) * SCORE_SCALE
    grad_keys = dot(queries, grad_scores, 1, 1)
    for i, grad in enumerate((grad_queries, grad_keys, grad_values)):
        out_ref[part((i * step + start) // HEAD_DIM + head, HEAD_DIM), :] = grad.astype(LOW)


def expand_back_kernel(
    count, places, back_ref, hat_ref, inv_ref, sums_ref, hidden_ref, packed_ref, lse_ref, doc_row, doc_col, *refs
):
    ups, refs = refs[:count], refs[count:]
    (
        first_out, low_out, mixed_back_out, grads_out, grad_packed_out, weight_out, weight_up, total, sems_out, sems_up
    ) = refs
    length, width = hat_ref.shape

    def fetch(c):
        return piece_copies(ups, places, weight_up, sems_up.at[c], part(c, width), part(c, width))

    for c in range(4):
        start_all(fetch(c))
    copies_out = start_all(piece_copies(ups, places, weight_out, sems_out, pl.ds(4 * width, width)))
    total[...] = back_ref[...]

    @pl.loop(0, 4)
    def _(c):
        wait_all(fetch(c))
        total[...] += dot(hidden_ref[:, part(c, width)], weight_up[:, part(c, width)], 1, 1)

    grads_out[...] = jnp.zeros_like(grads_out)

    @functools.partial(by_rows, length)
    def _(rows):
        gradient, hat = total[rows, :], hat_ref[rows, :]
        grads_out[0:1, :] += column_sum(gradient * hat)
        grads_out[1:2, :] += column_sum(gradient)
        first = normalize_back(gradient * sums_ref[4:5, :], hat, inv_ref[rows, :])
        first_out[rows, :] = first
        low_out[rows, :] = first.astype(LOW)

    wait_all(copies_out)
    mixed_back_out[...] = dot(weight_out[...], low_out[...], 1, 1).astype(LOW)
    same = doc_col[...] == doc_row[...]
    heads = grad_packed_out.shape[0] // (3 * HEAD_DIM)

    @pl.loop(0, heads, unroll=3)
    def _(head):
        mixed_back = mixed_back_out[part(head, HEAD_DIM), :]
        attend_back_head(head, 0, packed_ref, mixed_back, lse_ref, same, grad_packed_out, heads * HEAD_DIM, 0)


def attend_back_kernel(
    count, tokens, places, packed_ref, mixed_back_ref, lse_ref, doc_row, doc_col, projected_ref, sums_ref, first_ref,
    done_ref, *refs
):
    pieces = refs[:count]
    grad_packed_out, embedded_out, grads_out, weight, sems = refs[count:]
    length, width = projected_ref.shape
    copies = start_all(piece_copies(pieces, places, weight, sems, pl.ds(0, 3 * width)))
    same = doc_col[...] == doc_row[...]
    done = done_ref.shape[0] // 3

    @pl.loop(0, (width - done) // HEAD_DIM, unroll=3)
    def _(head):
        mixed_back = mixed_back_ref[part(head + done // HEAD_DIM, HEAD_DIM), :]
        attend_back_head(head, done // HEAD_DIM, packed_ref, mixed_back, lse_ref, same, grad_packed_out, width, done)

    for i in range(3):
        grad_packed_out[i * width : i * width + done, :] = done_ref[i * done : (i + 1) * done, :]
    wait_all(copies)
    mean, _, inv = batch_scale(sums_ref, tokens)
    for n in range(width // TILE):
        cols = slice(n * TILE, (n + 1) * TILE)
        values = first_ref[:, cols] + dot(weight[cols, :], grad_packed_out[...]).T
        embedded_out[:, cols] = values
        normed = (projected_ref[:, cols] - mean[:, cols]) * inv[:, cols]
        grads_out[0:1, cols] = column_sum(values)
        grads_out[1:2, cols] = column_sum(values * normed)


def packed_gradient_kernel(tokens, places, projected_ref, sums_ref, grad_packed_ref, *refs):
    halves, (low, work, grad_packed, sems) = refs[:-4], refs[-4:]
    length, width = projected_ref.shape

    def fetch(c):
        return pltpu.make_async_copy(grad_packed_ref.at[part(c, width)], grad_packed.at[part(c, width)], sems.at[c])

    for c in range(3):
        fetch(c).start()

    @functools.partial(by_rows, length)
    def _(rows):
        low[:, rows] = embed(projected_ref, sums_ref, tokens, rows).T.astype(LOW)

    @pl.loop(0, 3)
    def _(c):
        fetch(c).wait()
        for n in range(width // TILE):
            cols = part(c * (width // TILE) + n, TILE)
            put_blocks(halves, places, dot(low[...], grad_packed[cols, :], 1, 1), cols, work.at[n % 2])


def project_back_kernel(tokens, places, embedded_ref, projected_ref, sums_ref, grads_ref, mixed_ref, low_ref, x_ref, *refs):
    halves, (low_out, work, x, sems) = refs[:-4], refs[-4:]
    copies = start_all([pltpu.make_async_copy(x_ref, x, sems.at[0])])
    mean, _, inv = batch_scale(sums_ref, tokens)
    roi_rows = x_ref.shape[1] * halves[0].shape[1] // (x_ref.shape[1] + low_ref.shape[1])

    @functools.partial(by_rows, projected_ref.shape[0])
    def _(rows):
        normed = (projected_ref[rows, :] - mean) * inv
        shift = grads_ref[0:1, :] * (1.0 / tokens) + normed * (grads_ref[1:2, :] * (1.0 / tokens))
        low_out[rows, :] = (sums_ref[2:3, :] * inv * (embedded_ref[rows, :] - shift)).astype(LOW)

    wait_all(copies)
    row_blocks(halves, places, lambda at, n: dot(x[:, lanes(at, n)], low_out[...], 0, 0), roi_rows)
    work[...] = dot(mixed_ref[...], low_ref[...]).astype(LOW)
    if len(halves) == 1:
        halves[0][0, roi_rows:, :] = work[...]
    else:
        rows = halves[0].shape[1] - roi_rows
        for rel in range(8):
            halves[rel & 1][rel >> 1, roi_rows:, :] = work[part(places[rel], rows), :]


def input_gradient_kernel(count, places, low_ref, *refs):
    pieces, (out_ref, weight, sems) = refs[:count], refs[count:]
    wait_all(start_all(piece_copies(pieces, places, weight, sems)))

    @pl.loop(0, weight.shape[0] // 512)
    def _(i):
        out_ref[:, part(i, 512)] = dot(low_ref[...], weight[part(i, 512), :], 1, 1)


def sides(own):
    return [swap(own, ACROSS), swap(own, ALONG)]


def corner_halves(across, along):
    half = across.shape[0] // 2
    return [swap(along[:half], ACROSS), swap(across[half:], ALONG)]


def with_cores(chips):
    pieces = []
    for shard in chips:
        pieces += [shard, swap(shard, CORE)]
    return pieces


def per_device(
    roi_features, doc_ids, w_roi, bn_gain, bn_beta, w_qkv, w_out, ln1_gain, ln1_beta,
    w_up, w_down, ln2_gain, ln2_beta, cotangent,
):
    _, length, roi_width = roi_features.shape
    width, hidden = w_roi.shape[1], w_up.shape[1]
    devices = lax.axis_size("dp") * lax.axis_size("shard")
    tokens = length * devices
    me = lax.axis_index("shard")
    direct = direct_mesh()
    shards, rows = 8 if direct else 1, w_up.shape[0]
    cores, chips = (2, 4) if direct else (1, 1)
    places = (me ^ jnp.arange(8)).astype(jnp.int32) if direct else jnp.zeros((8,), jnp.int32)

    x = roi_features.reshape(length, roi_width)
    doc_row, doc_col = doc_ids.reshape(1, length), doc_ids.reshape(length, 1)
    own_params = jnp.stack([bn_gain, bn_beta, ln1_gain, ln1_beta, ln2_gain, ln2_beta]).astype(F32)
    own_params = jnp.where(lax.axis_index("dp") == 0, own_params, 0.0)
    own_start = me * bn_gain.shape[0]
    params = lax.dynamic_update_slice(jnp.zeros((8, width), F32), own_params, (2, own_start))

    gather = functools.partial(lax.all_gather, axis_name="shard", axis=0, tiled=True)
    wide_up = jnp.concatenate([w_up, w_out], axis=1)
    if direct:
        roi_chips = [w_roi, *sides(w_roi), swap(w_roi, ACROSS | ALONG)]
        w_qkv = tie(w_qkv, params, wide_up)
        qkv_chips = [w_qkv, *sides(w_qkv), swap(w_qkv, ACROSS | ALONG)]
        roi_pieces = with_cores(tie(roi_chips, w_qkv))
    else:
        roi_pieces = [gather(w_roi)]
    count = len(roi_pieces)

    def blocks(r, c):
        return [shape((chips, r, c), LOW)] * cores

    def low(r, c):
        return pltpu.VMEM((r, c), LOW)

    projected, sums = call(
        functools.partial(project_kernel, count),
        [places, x, params, *roi_pieces],
        [shape((length, width)), shape((8, width))],
        [low(roi_width, width), low(length, roi_width)],
        "project",
        out_near=(0,),
        far=(1, *range(3, 100)),
        sems=((8,), (1,)),
        loose=(2 + count,),
    )
    if direct:
        sums = sums + swap(sums, CORE)
        sums = sums + swap(sums, 1, "dp")
        sums = sums + swap(sums, 2, "dp")
        around = [swap(sums, ACROSS), swap(sums, ALONG), swap(sums, ACROSS | ALONG)]
        qkv_chips = tie(qkv_chips, sums)
        around = tie(around, qkv_chips)
        sums = (sums + around[0]) + (around[1] + around[2])
        qkv_pieces = with_cores(qkv_chips)
        up_sides = sides(tie(wide_up, sums))
    else:
        sums = lax.psum(sums, ("dp", "shard"))
        qkv_pieces = [gather(w_qkv)]

    heads = width // HEAD_DIM
    part_width = heads // 2 * HEAD_DIM
    packed_qkv, mixed, lse = call(
        functools.partial(attend_kernel, count, tokens),
        [places, projected, sums, doc_row, doc_col, *qkv_pieces],
        [shape((3 * width, length), LOW), shape((width, length), LOW), shape((heads, length))],
        [low(width, 3 * width), low(length, width)],
        "attend",
        near=(1,), out_near=(0, 1, 2),
        far=range(5, 100),
        sems=((3, 8),),
        loose=(4 + count,),
    )
    if direct:
        up_sides = tie(up_sides, mixed)
        up_corner = jnp.concatenate(corner_halves(*up_sides))
        down_sides = sides(tie(w_down, up_sides))
        up_pieces = with_cores([wide_up, *up_sides, up_corner])
    else:
        up_pieces, down_parts = [gather(wide_up)], [gather(w_down)]
    hat, inv, active, slope = call(
        functools.partial(expand_kernel, count, tokens),
        [places, projected, sums, mixed, *up_pieces],
        [shape((length, width)), shape((length, 1)), shape((length, hidden), LOW), shape((length, hidden), LOW)],
        [low(width, width), low(width, hidden), low(length, width)],
        "expand",
        near=(1, 3), out_near=(0, 1, 2, 3),
        far=range(4, 100),
        sems=((8,), (4, 8)),
        loose=(3 + count,),
    )
    if direct:
        down_sides = tie(down_sides, active)
        down_parts = with_cores([w_down, *down_sides, jnp.concatenate(corner_halves(*down_sides))])
    *down_halves, layer_out, back, grads_two = call(
        functools.partial(contract_kernel, count),
        [places, hat, sums, active, cotangent.reshape(length, width), *down_parts],
        blocks(hidden // shards, width) + [shape((length, width), LOW), shape((length, width)), shape((2, width))],
        [low(hidden, width), pltpu.VMEM((length, width), F32), low(length, width), low(length, width)],
        "contract",
        near=(1, 3), out_near=(cores + 1,),
        far=range(4, 100),
        sems=((8,), (1,)),
        loose=(4 + count,),
    )
    down = OwnedSum(down_halves)
    *up_halves, grad_hidden = call(
        functools.partial(hidden_back_kernel, count),
        [places, back, hat, sums, slope, *down_parts],
        blocks(hidden // shards, width) + [shape((length, hidden), LOW)],
        [low(hidden, width), low(length, width), low(width, length), pltpu.VMEM((2, width, TILE), LOW)],
        "hidden_back",
        near=(1, 2, 4), out_near=(cores,),
        far=range(5, 100),
        sems=((8,),),
    )
    up = OwnedSum(up_halves)
    sent = down.plane_one(grad_hidden)
    first, low_first, mixed_back, grads_one, grad_part = call(
        functools.partial(expand_back_kernel, count),
        [
            tie(places, sent), back, hat, inv, sums, grad_hidden, packed_qkv, lse, doc_row, doc_col, *up_pieces,
        ],
        [
            shape((length, width)), shape((length, width), LOW), shape((width, length), LOW), shape((2, width)),
            shape((3 * part_width, length), LOW),
        ],
        [low(width, width), low(width, hidden), pltpu.VMEM((length, width), F32)],
        "expand_back",
        near=(1, 2, 3, 5, 6, 7), out_near=(0, 1, 2, 4),
        far=range(10, 100),
        sems=((8,), (4, 8)),
    )
    sent = down.plane_two(first)
    sent = up.plane_one(sent)
    grad_packed, grad_embedded, grads_bn = call(
        functools.partial(attend_back_kernel, count, tokens),
        [
            tie(places, sent), packed_qkv, mixed_back, lse, doc_row, doc_col, projected, sums, first, grad_part,
            *qkv_pieces,
        ],
        [shape((3 * width, length), LOW), shape((length, width)), shape((2, width))],
        [low(width, 3 * width)],
        "attend_back",
        near=(1, 2, 3, 6, 8, 9), out_near=(0, 1),
        far=range(10, 100),
        sems=((8,),),
    )
    second = jnp.concatenate([grads_bn, grads_one, grads_two, jnp.zeros((2, width), F32)])
    if direct:
        second = second + swap(tie(second, down.back), CORE)
        second = second + swap(second, 1, "dp")
        second = second + swap(second, 2, "dp")
        second = tie(second, up.came)
        around = [swap(second, ACROSS), swap(second, ALONG), swap(second, ACROSS | ALONG)]
        sent = up.plane_two(second)
        down_sum = LineSum(down.plane_done(sent))
        around = tie(around, sent, down_sum.step())
        second = (second + around[0]) + (around[1] + around[2])
    else:
        second = lax.psum(second, ("dp", "shard"))
    roi_rows, out_rows = roi_width // shards, width // shards
    *roi_halves, low_projected = call(
        functools.partial(project_back_kernel, tokens),
        [places, grad_embedded, projected, sums, second, mixed, low_first, x],
        blocks(roi_rows + out_rows, width) + [shape((length, width), LOW)],
        [low(width, width), low(length, roi_width)],
        "project_back",
        near=(1, 2, 5, 6), out_near=(cores,),
        far=(8,),
        sems=((1,),),
    )
    roi = OwnedSum(roi_halves)
    start_packed = tie(places, low_projected)
    qkv_halves = call(
        functools.partial(packed_gradient_kernel, tokens),
        [start_packed, projected, sums, grad_packed],
        blocks(width // shards, 3 * width),
        [low(width, length), pltpu.VMEM((2, width, TILE), LOW), low(3 * width, length)],
        "packed_gradient",
        near=(1,),
        far=(3,),
        sems=((3,),),
    )
    qkv = OwnedSum(qkv_halves)
    sent = roi.plane_one(qkv_halves)
    if direct:
        up_sum = LineSum(up.plane_done(sent))
        sent = up_sum.step()
    (roi_grad,) = call(
        functools.partial(input_gradient_kernel, count),
        [tie(places, sent), low_projected, *roi_pieces],
        [shape((length, roi_width))],
        [low(roi_width, width)],
        "input_gradient",
        near=(1,),
        far=range(2, 100),
        sems=((8,),),
    )
    if direct:
        sent = roi.plane_two(down_sum.step(roi_grad))
        sent = qkv.plane_one(sent)
        sent = down_sum.step(up_sum.step(sent))
        roi_sum = LineSum(roi.plane_done(sent))
        sent = roi_sum.step()
        sent = qkv.plane_two(sent)
        sent = up_sum.step(sent)
        sent = roi_sum.step(sent)
        qkv_sum = LineSum(qkv.plane_done(sent))
        sent = qkv_sum.step()
        sent = roi_sum.step(sent)
        sent = qkv_sum.step(sent)
        sent = qkv_sum.step(sent)
        sum_roi, sum_down, sum_up, sum_qkv = [g.total() for g in (roi_sum, down_sum, up_sum, qkv_sum)]
        sum_roi, sum_out = sum_roi[:roi_rows], sum_roi[roi_rows:]
        sum_up = jnp.concatenate([sum_up[i * rows : (i + 1) * rows] for i in range(4)], axis=1)
    else:
        grads = [roi_halves[0][0, :roi_rows], roi_halves[0][0, roi_rows:], down_halves[0][0], qkv_halves[0][0]]
        grads.append(up_halves[0][0].reshape(4, width, width).swapaxes(0, 1).reshape(width, hidden))
        sum_roi, sum_out, sum_down, sum_qkv, sum_up = [
            lax.psum(lax.psum_scatter(grad, "shard", scatter_dimension=0, tiled=True), "dp").astype(F32) for grad in grads
        ]
    own = lax.dynamic_slice_in_dim(second, own_start, bn_gain.shape[0], 1)
    mean = sums[0] / tokens
    return (
        layer_out[None], roi_grad[None], sum_roi, own[1], own[0], sum_qkv, sum_out, own[2], own[3],
        sum_up, sum_down, own[4], own[5], mean, sums[1] / tokens - mean * mean,
    )


def solution(mesh):
    rows3, rows2, split2, split1 = P(("dp", "shard"), None, None), P(("dp", "shard"), None), P("shard", None), P("shard")
    return jax.shard_map(
        per_device,
        mesh=mesh,
        in_specs=(
            rows3, rows2, split2, split1, split1, split2, split2, split1, split1, split2, split2, split1, split1, rows3,
        ),
        out_specs=(
            rows3, rows3, split2, split1, split1, split2, split2, split1, split1, split2, split2, split1, split1, P(), P(),
        ),
        check_vma=False,
    )
```

```python
import functools
import math

import jax
import jax.numpy as jnp
from jax import lax
from jax.experimental import pallas as pl
from jax.experimental.pallas import tpu as pltpu
from jax.sharding import PartitionSpec as P

HEAD_DIM = 64
EPSILON = 1e-05
SCORE_SCALE = 0.125
MASKED = -1000000000.0
CORE, ACROSS, ALONG = 1, 2, 4
TILE = 256
F32, LOW = jnp.float32, jnp.bfloat16

ERFC_RATE = 0.33
ERFC = (
    0.18636612594127655,
    0.18283699452877045,
    0.20192526280879974,
    0.04500619322061539,
    0.4125494658946991,
    -0.3554469347000122,
    0.46269258856773376,
    -0.13592977821826935,
)


def direct_mesh():
    return lax.axis_size("shard") == 8 and lax.axis_size("dp") == 4


def swap(values, step, axis="shard"):
    size = lax.axis_size(axis)
    return lax.ppermute(values, axis, [(i, i ^ step) for i in range(size)])


def add_low(*terms):
    total = terms[0].astype(F32)
    for term in terms[1:]:
        total = total + term.astype(F32)
    return total.astype(LOW)


def sum_everywhere(part):
    if not direct_mesh():
        return lax.psum(part, ("dp", "shard"))
    part = part + swap(part, CORE)
    part = (part + swap(part, 1, "dp")) + (swap(part, 2, "dp") + swap(part, 3, "dp"))
    return (part + swap(part, ACROSS)) + (swap(part, ALONG) + swap(part, ACROSS | ALONG))


def tie(values, *after):
    return lax.optimization_barrier((values, after))[0]


class OwnedSum:
    def __init__(self, halves):
        self.direct = direct_mesh()
        if self.direct:
            self.mine, self.got = halves[0], swap(halves[1], CORE)
            rows = self.mine.shape[1] // 2
            self.cuts = ((slice(0, rows), 1, 2), (slice(rows, None), 2, 1))
        else:
            whole = halves[0].reshape(-1, halves[0].shape[-1])
            self.part = lax.psum_scatter(whole, "shard", scatter_dimension=0, tiled=True)

    def plane_one(self, *after):
        if not self.direct:
            return self.part
        self.mine, self.got = tie((self.mine, self.got), *after)
        mine, got = self.mine, self.got
        sent = [
            add_low(jnp.stack([mine[near, cut], mine[3, cut]]), jnp.stack([got[near, cut], got[3, cut]]))
            for cut, near, _ in self.cuts
        ]
        self.came = [swap(part, 2 * near) for part, (_, near, _) in zip(sent, self.cuts)]
        return sent

    def plane_two(self, *after):
        if not self.direct:
            return self.part
        self.mine, self.got, self.came = tie((self.mine, self.got, self.came), *after)
        passed = [
            add_low(self.mine[far, cut], self.got[far, cut], came[1]) for came, (cut, _, far) in zip(self.came, self.cuts)
        ]
        self.back = [swap(part, 2 * far) for part, (_, _, far) in zip(passed, self.cuts)]
        return passed

    def plane_done(self, *after):
        if not self.direct:
            return self.part
        mine, got, came, back = tie((self.mine, self.got, self.came, self.back), *after)
        return jnp.concatenate(
            [add_low(mine[0, cut], got[0, cut], c[0], b) for c, b, (cut, _, _) in zip(came, back, self.cuts)]
        )


class LineSum:
    def __init__(self, part):
        self.part = part
        self.pairs = ([(0, 1), (3, 2)], [(1, 2), (2, 1)], [(1, 0), (2, 3)])
        self.number = 0

    def step(self, *after):
        if not direct_mesh():
            return self.part
        if self.number == 0:
            self.part = tie(self.part, *after)
        else:
            self.part = add_low(*tie((self.part, self.came), *after))
        self.came = lax.ppermute(self.part, "dp", self.pairs[self.number])
        self.number += 1
        return self.part

    def total(self):
        if not direct_mesh():
            return lax.psum(self.part, "dp").astype(F32)
        place = lax.axis_index("dp")
        return jnp.where((place == 1) | (place == 2), self.part, self.came).astype(F32)


def dot(left, right, left_dim=1, right_dim=0):
    return lax.dot_general(
        left, right, (((left_dim,), (right_dim,)), ((), ())), preferred_element_type=F32
    )


def wait_all(copies):
    for copy in copies:
        copy.wait()


def start_all(copies):
    for copy in copies:
        copy.start()
    return copies


def part(index, size):
    return pl.ds(pl.multiple_of(index * size, size), size)


def by_rows(count, body):
    @pl.loop(0, count // 128)
    def _(i):
        body(part(i, 128))


def piece_copies(pieces, places, target, sems, source_columns=None, columns=slice(None)):
    copies = []
    for i, piece in enumerate(pieces):
        rows = piece.shape[0]
        source = piece if source_columns is None else piece.at[:, source_columns]
        at = part(places[i], rows) if len(pieces) > 1 else pl.ds(0, rows)
        copies.append(pltpu.make_async_copy(source, target.at[at, columns], sems.at[i]))
    return copies


def wait_chunk(count, copies, places, target, sems, c):
    if count == 1:
        return c
    rows = target.shape[0] // 8
    for k in range(2):
        at = target.at[part(places[2 * c + k], rows)]
        pltpu.make_async_copy(at, at, sems.at[2 * c + k]).wait()
    return places[2 * c] >> 1


def put_blocks(halves, places, values, columns, work, section=0):
    if len(halves) == 1:
        halves[0][0, part(section, values.shape[0]), columns] = values.astype(LOW)
        return
    rows = values.shape[0] // 8
    work[...] = values.astype(LOW)
    for rel in range(8):
        halves[rel & 1][rel >> 1, part(section, rows), columns] = work[part(places[rel], rows), :]


def row_blocks(halves, places, make, rows=None):
    chips = halves[0].shape[0]
    rows = rows or halves[0].shape[1]
    if len(halves) == 1:
        step = min(rows, 512)

        @pl.loop(0, rows // step)
        def _(i):
            at = pl.multiple_of(i * step, step)
            halves[0][0, pl.ds(at, step)] = make(at, step).astype(LOW)

        return

    @pl.loop(0, chips)
    def _(j):
        for k in range(2):
            halves[k][j, :rows] = make(places[2 * j + k] * rows, rows).astype(LOW)


def lanes(first, size):
    return pl.ds(pl.multiple_of(first, 128), size)


def batch_scale(sums_ref, tokens):
    mean = sums_ref[0:1, :] * (1.0 / tokens)
    var = sums_ref[1:2, :] * (1.0 / tokens) - mean * mean
    return mean, var, lax.rsqrt(var + EPSILON)


def embed(projected_ref, sums_ref, tokens, rows=slice(None)):
    mean, _, inv = batch_scale(sums_ref, tokens)
    return (projected_ref[rows, :] - mean) * inv * sums_ref[2:3, :] + sums_ref[3:4, :]


def normalize(values):
    center = values - jnp.mean(values, axis=-1, keepdims=True)
    inv = lax.rsqrt(jnp.mean(center * center, axis=-1, keepdims=True) + EPSILON)
    return center * inv, inv


def normalize_back(scaled, normed, inv):
    return inv * (
        scaled
        - jnp.mean(scaled, axis=-1, keepdims=True)
        - normed * jnp.mean(scaled * normed, axis=-1, keepdims=True)
    )


def gelu_pair(values):
    t = 1.0 / (1.0 + (ERFC_RATE * 0.7071067811865476) * jnp.abs(values))
    poly = 0.5 * ERFC[-1]
    for factor in ERFC[-2::-1]:
        poly = poly * t + 0.5 * factor
    bell = jnp.exp(values * values * -0.5)
    tail = poly * t * bell
    share = jnp.where(values < 0, tail, 1.0 - tail)
    return values * share, share + values * bell * 0.3989422804014327


def size_of(array):
    return math.prod(array.shape) * jnp.dtype(array.dtype).itemsize


def call(kernel, args, outs, scratch, name, spare=6, far=(), loose=(), near=(), out_near=(), sems=()):
    spaces = [pl.ANY if i in loose else pltpu.HBM if i in far else pltpu.VMEM for i in range(len(args))]
    spaces[0] = pltpu.SMEM
    held = [a for i, a in enumerate(args) if i and i not in far and i not in near]
    held += [a for i, a in enumerate(outs) if i not in out_near] + list(scratch)
    args = [
        pltpu.with_memory_space_constraint(a, pltpu.HBM if i in far else pltpu.VMEM)
        if (i in far and i not in loose) or i in near
        else a
        for i, a in enumerate(args)
    ]
    return pl.pallas_call(
        kernel,
        in_specs=[pl.BlockSpec(memory_space=space) for space in spaces],
        out_specs=[pl.BlockSpec(memory_space=pltpu.VMEM)] * len(outs),
        out_shape=[pltpu.VMEM(a.shape, a.dtype) if i in out_near else a for i, a in enumerate(outs)],
        scratch_shapes=list(scratch) + [pltpu.SemaphoreType.DMA(count) for count in sems],
        compiler_params=pltpu.CompilerParams(vmem_limit_bytes=sum(map(size_of, held)) + spare * 2**20),
        cost_estimate=pl.CostEstimate(flops=1024, bytes_accessed=1024, transcendentals=0),
        name=name,
    )(*args)


def shape(dims, kind=F32):
    return jax.ShapeDtypeStruct(tuple(dims), kind)


def column_sum(values):
    return jnp.sum(values, axis=0, keepdims=True)


def project_kernel(count, places, x_ref, params_ref, *refs):
    pieces, (out_ref, sums_ref, weight, x, sems, sems_x) = refs[:count], refs[count:]
    copies = start_all([pltpu.make_async_copy(x_ref, x, sems_x.at[0])])
    wait_all(start_all(piece_copies(pieces, places, weight, sems)) + copies)
    sums_ref[...] = params_ref[...]

    @pl.loop(0, out_ref.shape[1] // TILE)
    def _(n):
        cols = part(n, TILE)
        values = dot(x[...], weight[:, cols])
        out_ref[:, cols] = values
        sums_ref[0:1, cols] = column_sum(values)
        sums_ref[1:2, cols] = column_sum(values * values)


def attend_kernel(count, tokens, places, projected_ref, sums_ref, doc_row, doc_col, *refs):
    pieces = refs[:count]
    packed_out, mixed_out, lse_out, weight, embedded, sems = refs[count:]
    length, width = projected_ref.shape

    def fetch(c):
        return piece_copies(pieces, places, weight, sems.at[c], part(c, width), part(c, width))

    for c in range(3):
        start_all(fetch(c))

    @functools.partial(by_rows, length)
    def _(rows):
        embedded[rows, :] = embed(projected_ref, sums_ref, tokens, rows).astype(LOW)

    @pl.loop(0, 3)
    def _(c):
        wait_all(fetch(c))
        for n in range(width // TILE):
            cols = part(c * (width // TILE) + n, TILE)
            packed_out[cols, :] = dot(embedded[...], weight[:, cols]).T.astype(LOW)

    same = doc_col[...] == doc_row[...]
    heads = width // HEAD_DIM

    @pl.loop(0, heads, unroll=3)
    def _(head):
        queries = packed_out[part(head, HEAD_DIM), :] * jnp.asarray(SCORE_SCALE, LOW)
        keys = packed_out[part(head + heads, HEAD_DIM), :]
        values = packed_out[part(head + 2 * heads, HEAD_DIM), :]
        scores = jnp.where(same, dot(keys, queries, 0, 0), MASKED)
        top = jnp.max(scores, axis=0, keepdims=True)
        expo = jnp.exp(scores - top)
        total = jnp.sum(expo, axis=0, keepdims=True)
        mixed = dot(values, expo.astype(LOW)) * (1.0 / total)
        mixed_out[part(head, HEAD_DIM), :] = mixed.astype(LOW)
        lse_out[pl.ds(head, 1), :] = top + jnp.log(total)


def expand_kernel(count, tokens, places, projected_ref, sums_ref, mixed_ref, *refs):
    ups, refs = refs[:count], refs[count:]
    hat_out, inv_out, active_out, slope_out, weight_out, weight_up, low_one, sems_out, sems_up = refs
    length, width = projected_ref.shape
    copies_out = start_all(piece_copies(ups, places, weight_out, sems_out, pl.ds(4 * width, width)))

    def fetch(c):
        return piece_copies(ups, places, weight_up, sems_up.at[c], part(c, width), part(c, width))

    for c in range(4):
        start_all(fetch(c))
    wait_all(copies_out)
    hat_out[...] = dot(mixed_ref[...], weight_out[...], 0, 0)

    @functools.partial(by_rows, length)
    def _(rows):
        hat, inv = normalize(embed(projected_ref, sums_ref, tokens, rows) + hat_out[rows, :])
        hat_out[rows, :] = hat
        inv_out[rows, :] = inv
        low_one[rows, :] = (hat * sums_ref[4:5, :] + sums_ref[5:6, :]).astype(LOW)

    @pl.loop(0, 4)
    def _(c):
        wait_all(fetch(c))
        for n in range(width // TILE):
            cols = part(c * (width // TILE) + n, TILE)
            active, slope = gelu_pair(dot(low_one[...], weight_up[:, cols]))
            active_out[:, cols] = active.astype(LOW)
            slope_out[:, cols] = slope.astype(LOW)


def contract_kernel(count, places, hat_ref, sums_ref, active_ref, grad_ref, *refs):
    pieces, refs = refs[:count], refs[count:]
    halves, refs = refs[:-9], refs[-9:]
    layer_out, back_out, grads_out, weight, branch, low_back, grad, sems, sems_grad = refs
    length, width = hat_ref.shape
    copies = start_all(piece_copies(pieces, places, weight, sems))
    grad_copy = start_all([pltpu.make_async_copy(grad_ref, grad, sems_grad.at[0])])
    if count == 1:
        wait_all(copies)

    @functools.partial(by_rows, length)
    def _(rows):
        branch[rows, :] = hat_ref[rows, :] * sums_ref[4:5, :] + sums_ref[5:6, :]

    @pl.loop(0, 4)
    def _(i):
        c = wait_chunk(count, copies, places, weight, sems, i)
        branch[...] += dot(active_ref[:, part(c, width)], weight[part(c, width), :])

    wait_all(grad_copy)
    grads_out[...] = jnp.zeros_like(grads_out)

    @functools.partial(by_rows, length)
    def _(rows):
        hat, inv = normalize(branch[rows, :])
        layer_out[rows, :] = (hat * sums_ref[6:7, :] + sums_ref[7:8, :]).astype(LOW)
        gradient = grad[rows, :].astype(F32)
        grads_out[0:1, :] += column_sum(gradient * hat)
        grads_out[1:2, :] += column_sum(gradient)
        back = normalize_back(gradient * sums_ref[6:7, :], hat, inv)
        back_out[rows, :] = back
        low_back[rows, :] = back.astype(LOW)

    row_blocks(halves, places, lambda at, n: dot(active_ref[:, lanes(at, n)], low_back[...], 0, 0))


def hidden_back_kernel(count, places, back_ref, hat_ref, sums_ref, slope_ref, *refs):
    pieces, refs = refs[:count], refs[count:]
    halves, (hidden_out, weight, low_back, low_one, work, sems) = refs[:-6], refs[-6:]
    length, width = hat_ref.shape
    copies = start_all(piece_copies(pieces, places, weight, sems))

    @functools.partial(by_rows, length)
    def _(rows):
        low_back[rows, :] = back_ref[rows, :].astype(LOW)
        low_one[:, rows] = (hat_ref[rows, :] * sums_ref[4:5, :] + sums_ref[5:6, :]).T.astype(LOW)

    if count == 1:
        wait_all(copies)

    @pl.loop(0, 4)
    def _(i):
        c = wait_chunk(count, copies, places, weight, sems, i)
        for n in range(width // TILE):
            cols = part(c * (width // TILE) + n, TILE)
            values = (dot(low_back[...], weight[cols, :], 1, 1) * slope_ref[:, cols].astype(F32)).astype(LOW)
            hidden_out[:, cols] = values
            put_blocks(halves, places, dot(low_one[...], values), slice(n * TILE, (n + 1) * TILE), work.at[n % 2], c)


def attend_back_head(head, first_head, packed_ref, mixed_back, lse_ref, same, out_ref, step, start):
    width = packed_ref.shape[0] // 3
    at = part(head + first_head, HEAD_DIM)
    queries = packed_ref[at, :] * jnp.asarray(SCORE_SCALE, LOW)
    at = part(head + first_head + width // HEAD_DIM, HEAD_DIM)
    keys = packed_ref[at, :]
    at = part(head + first_head + 2 * width // HEAD_DIM, HEAD_DIM)
    values = packed_ref[at, :]
    scores = jnp.where(same, dot(keys, queries, 0, 0), MASKED)
    probs = jnp.exp(scores - lse_ref[pl.ds(head + first_head, 1), :])
    grad_probs = dot(values, mixed_back, 0, 0)
    grad_values = dot(mixed_back, probs.astype(LOW), 1, 1)
    inner = jnp.sum(probs * grad_probs, axis=0, keepdims=True)
    grad_scores = (probs * (grad_probs - inner)).astype(LOW)
    grad_queries = dot(keys, grad_scores) * SCORE_SCALE
    grad_keys = dot(queries, grad_scores, 1, 1)
    for i, grad in enumerate((grad_queries, grad_keys, grad_values)):
        out_ref[part((i * step + start) // HEAD_DIM + head, HEAD_DIM), :] = grad.astype(LOW)


def expand_back_kernel(
    count, places, back_ref, hat_ref, inv_ref, sums_ref, hidden_ref, packed_ref, lse_ref, doc_row, doc_col, *refs
):
    ups, refs = refs[:count], refs[count:]
    (
        first_out, low_out, mixed_back_out, grads_out, grad_packed_out, weight_out, weight_up, total, sems_out, sems_up
    ) = refs
    length, width = hat_ref.shape

    def fetch(c):
        return piece_copies(ups, places, weight_up, sems_up.at[c], part(c, width), part(c, width))

    for c in range(4):
        start_all(fetch(c))
    copies_out = start_all(piece_copies(ups, places, weight_out, sems_out, pl.ds(4 * width, width)))
    total[...] = back_ref[...]

    @pl.loop(0, 4)
    def _(c):
        wait_all(fetch(c))
        total[...] += dot(hidden_ref[:, part(c, width)], weight_up[:, part(c, width)], 1, 1)

    grads_out[...] = jnp.zeros_like(grads_out)

    @functools.partial(by_rows, length)
    def _(rows):
        gradient, hat = total[rows, :], hat_ref[rows, :]
        grads_out[0:1, :] += column_sum(gradient * hat)
        grads_out[1:2, :] += column_sum(gradient)
        first = normalize_back(gradient * sums_ref[4:5, :], hat, inv_ref[rows, :])
        first_out[rows, :] = first
        low_out[rows, :] = first.astype(LOW)

    wait_all(copies_out)
    mixed_back_out[...] = dot(weight_out[...], low_out[...], 1, 1).astype(LOW)
    same = doc_col[...] == doc_row[...]
    heads = grad_packed_out.shape[0] // (3 * HEAD_DIM)

    @pl.loop(0, heads, unroll=3)
    def _(head):
        mixed_back = mixed_back_out[part(head, HEAD_DIM), :]
        attend_back_head(head, 0, packed_ref, mixed_back, lse_ref, same, grad_packed_out, heads * HEAD_DIM, 0)


def attend_back_kernel(
    count, tokens, places, packed_ref, mixed_back_ref, lse_ref, doc_row, doc_col, projected_ref, sums_ref, first_ref,
    done_ref, *refs
):
    pieces = refs[:count]
    grad_packed_out, embedded_out, grads_out, weight, sems = refs[count:]
    length, width = projected_ref.shape
    copies = start_all(piece_copies(pieces, places, weight, sems, pl.ds(0, 3 * width)))
    same = doc_col[...] == doc_row[...]
    done = done_ref.shape[0] // 3

    @pl.loop(0, (width - done) // HEAD_DIM, unroll=3)
    def _(head):
        mixed_back = mixed_back_ref[part(head + done // HEAD_DIM, HEAD_DIM), :]
        attend_back_head(head, done // HEAD_DIM, packed_ref, mixed_back, lse_ref, same, grad_packed_out, width, done)

    for i in range(3):
        grad_packed_out[i * width : i * width + done, :] = done_ref[i * done : (i + 1) * done, :]
    wait_all(copies)
    mean, _, inv = batch_scale(sums_ref, tokens)
    for n in range(width // TILE):
        cols = slice(n * TILE, (n + 1) * TILE)
        values = first_ref[:, cols] + dot(weight[cols, :], grad_packed_out[...]).T
        embedded_out[:, cols] = values
        normed = (projected_ref[:, cols] - mean[:, cols]) * inv[:, cols]
        grads_out[0:1, cols] = column_sum(values)
        grads_out[1:2, cols] = column_sum(values * normed)


def packed_gradient_kernel(tokens, places, projected_ref, sums_ref, grad_packed_ref, *refs):
    halves, (low, work, grad_packed, sems) = refs[:-4], refs[-4:]
    length, width = projected_ref.shape

    def fetch(c):
        return pltpu.make_async_copy(grad_packed_ref.at[part(c, width)], grad_packed.at[part(c, width)], sems.at[c])

    for c in range(3):
        fetch(c).start()

    @functools.partial(by_rows, length)
    def _(rows):
        low[:, rows] = embed(projected_ref, sums_ref, tokens, rows).T.astype(LOW)

    @pl.loop(0, 3)
    def _(c):
        fetch(c).wait()
        for n in range(width // TILE):
            cols = part(c * (width // TILE) + n, TILE)
            put_blocks(halves, places, dot(low[...], grad_packed[cols, :], 1, 1), cols, work.at[n % 2])


def project_back_kernel(tokens, places, embedded_ref, projected_ref, sums_ref, grads_ref, mixed_ref, low_ref, x_ref, *refs):
    halves, (low_out, work, x, sems) = refs[:-4], refs[-4:]
    copies = start_all([pltpu.make_async_copy(x_ref, x, sems.at[0])])
    mean, _, inv = batch_scale(sums_ref, tokens)
    roi_rows = x_ref.shape[1] * halves[0].shape[1] // (x_ref.shape[1] + low_ref.shape[1])

    @functools.partial(by_rows, projected_ref.shape[0])
    def _(rows):
        normed = (projected_ref[rows, :] - mean) * inv
        shift = grads_ref[0:1, :] * (1.0 / tokens) + normed * (grads_ref[1:2, :] * (1.0 / tokens))
        low_out[rows, :] = (sums_ref[2:3, :] * inv * (embedded_ref[rows, :] - shift)).astype(LOW)

    wait_all(copies)
    row_blocks(halves, places, lambda at, n: dot(x[:, lanes(at, n)], low_out[...], 0, 0), roi_rows)
    work[...] = dot(mixed_ref[...], low_ref[...]).astype(LOW)
    if len(halves) == 1:
        halves[0][0, roi_rows:, :] = work[...]
    else:
        rows = halves[0].shape[1] - roi_rows
        for rel in range(8):
            halves[rel & 1][rel >> 1, roi_rows:, :] = work[part(places[rel], rows), :]


def input_gradient_kernel(count, places, low_ref, *refs):
    pieces, (out_ref, weight, sems) = refs[:count], refs[count:]
    wait_all(start_all(piece_copies(pieces, places, weight, sems)))

    @pl.loop(0, weight.shape[0] // 512)
    def _(i):
        out_ref[:, part(i, 512)] = dot(low_ref[...], weight[part(i, 512), :], 1, 1)


def sides(own):
    return [swap(own, ACROSS), swap(own, ALONG)]


def corner_halves(across, along):
    half = across.shape[0] // 2
    return [swap(along[:half], ACROSS), swap(across[half:], ALONG)]


def with_cores(chips):
    pieces = []
    for shard in chips:
        pieces += [shard, swap(shard, CORE)]
    return pieces


def per_device(
    roi_features, doc_ids, w_roi, bn_gain, bn_beta, w_qkv, w_out, ln1_gain, ln1_beta,
    w_up, w_down, ln2_gain, ln2_beta, cotangent,
):
    _, length, roi_width = roi_features.shape
    width, hidden = w_roi.shape[1], w_up.shape[1]
    devices = lax.axis_size("dp") * lax.axis_size("shard")
    tokens = length * devices
    me = lax.axis_index("shard")
    direct = direct_mesh()
    shards, rows = 8 if direct else 1, w_up.shape[0]
    cores, chips = (2, 4) if direct else (1, 1)
    places = (me ^ jnp.arange(8)).astype(jnp.int32) if direct else jnp.zeros((8,), jnp.int32)

    x = roi_features.reshape(length, roi_width)
    doc_row, doc_col = doc_ids.reshape(1, length), doc_ids.reshape(length, 1)
    own_params = jnp.stack([bn_gain, bn_beta, ln1_gain, ln1_beta, ln2_gain, ln2_beta]).astype(F32)
    own_params = jnp.where(lax.axis_index("dp") == 0, own_params, 0.0)
    own_start = me * bn_gain.shape[0]
    params = lax.dynamic_update_slice(jnp.zeros((8, width), F32), own_params, (2, own_start))

    gather = functools.partial(lax.all_gather, axis_name="shard", axis=0, tiled=True)
    wide_up = jnp.concatenate([w_up, w_out], axis=1)
    if direct:
        roi_chips = [w_roi, *sides(w_roi), swap(w_roi, ACROSS | ALONG)]
        w_qkv = tie(w_qkv, params, wide_up)
        qkv_chips = [w_qkv, *sides(w_qkv), swap(w_qkv, ACROSS | ALONG)]
        roi_pieces = with_cores(tie(roi_chips, w_qkv))
    else:
        roi_pieces = [gather(w_roi)]
    count = len(roi_pieces)

    def blocks(r, c):
        return [shape((chips, r, c), LOW)] * cores

    def low(r, c):
        return pltpu.VMEM((r, c), LOW)

    projected, sums = call(
        functools.partial(project_kernel, count),
        [places, x, params, *roi_pieces],
        [shape((length, width)), shape((8, width))],
        [low(roi_width, width), low(length, roi_width)],
        "project",
        out_near=(0,),
        far=(1, *range(3, 100)),
        sems=((8,), (1,)),
        loose=(2 + count,),
    )
    if direct:
        sums = sums + swap(sums, CORE)
        sums = sums + swap(sums, 1, "dp")
        sums = sums + swap(sums, 2, "dp")
        around = [swap(sums, ACROSS), swap(sums, ALONG), swap(sums, ACROSS | ALONG)]
        qkv_chips = tie(qkv_chips, sums)
        around = tie(around, qkv_chips)
        sums = (sums + around[0]) + (around[1] + around[2])
        qkv_pieces = with_cores(qkv_chips)
        up_sides = sides(tie(wide_up, sums))
    else:
        sums = lax.psum(sums, ("dp", "shard"))
        qkv_pieces = [gather(w_qkv)]

    heads = width // HEAD_DIM
    part_width = heads // 2 * HEAD_DIM
    packed_qkv, mixed, lse = call(
        functools.partial(attend_kernel, count, tokens),
        [places, projected, sums, doc_row, doc_col, *qkv_pieces],
        [shape((3 * width, length), LOW), shape((width, length), LOW), shape((heads, length))],
        [low(width, 3 * width), low(length, width)],
        "attend",
        near=(1,), out_near=(0, 1, 2),
        far=range(5, 100),
        sems=((3, 8),),
        loose=(4 + count,),
    )
    if direct:
        up_sides = tie(up_sides, mixed)
        up_corner = jnp.concatenate(corner_halves(*up_sides))
        down_sides = sides(tie(w_down, up_sides))
        up_pieces = with_cores([wide_up, *up_sides, up_corner])
    else:
        up_pieces, down_parts = [gather(wide_up)], [gather(w_down)]
    hat, inv, active, slope = call(
        functools.partial(expand_kernel, count, tokens),
        [places, projected, sums, mixed, *up_pieces],
        [shape((length, width)), shape((length, 1)), shape((length, hidden), LOW), shape((length, hidden), LOW)],
        [low(width, width), low(width, hidden), low(length, width)],
        "expand",
        near=(1, 3), out_near=(0, 1, 2, 3),
        far=range(4, 100),
        sems=((8,), (4, 8)),
        loose=(3 + count,),
    )
    if direct:
        down_sides = tie(down_sides, active)
        down_parts = with_cores([w_down, *down_sides, jnp.concatenate(corner_halves(*down_sides))])
    *down_halves, layer_out, back, grads_two = call(
        functools.partial(contract_kernel, count),
        [places, hat, sums, active, cotangent.reshape(length, width), *down_parts],
        blocks(hidden // shards, width) + [shape((length, width), LOW), shape((length, width)), shape((2, width))],
        [low(hidden, width), pltpu.VMEM((length, width), F32), low(length, width), low(length, width)],
        "contract",
        near=(1, 3), out_near=(cores + 1,),
        far=range(4, 100),
        sems=((8,), (1,)),
        loose=(4 + count,),
    )
    down = OwnedSum(down_halves)
    *up_halves, grad_hidden = call(
        functools.partial(hidden_back_kernel, count),
        [places, back, hat, sums, slope, *down_parts],
        blocks(hidden // shards, width) + [shape((length, hidden), LOW)],
        [low(hidden, width), low(length, width), low(width, length), pltpu.VMEM((2, width, TILE), LOW)],
        "hidden_back",
        near=(1, 2, 4), out_near=(cores,),
        far=range(5, 100),
        sems=((8,),),
    )
    up = OwnedSum(up_halves)
    sent = down.plane_one(grad_hidden)
    first, low_first, mixed_back, grads_one, grad_part = call(
        functools.partial(expand_back_kernel, count),
        [
            tie(places, sent), back, hat, inv, sums, grad_hidden, packed_qkv, lse, doc_row, doc_col, *up_pieces,
        ],
        [
            shape((length, width)), shape((length, width), LOW), shape((width, length), LOW), shape((2, width)),
            shape((3 * part_width, length), LOW),
        ],
        [low(width, width), low(width, hidden), pltpu.VMEM((length, width), F32)],
        "expand_back",
        near=(1, 2, 3, 5, 6, 7), out_near=(0, 1, 2, 4),
        far=range(10, 100),
        sems=((8,), (4, 8)),
    )
    sent = down.plane_two(first)
    sent = up.plane_one(sent)
    grad_packed, grad_embedded, grads_bn = call(
        functools.partial(attend_back_kernel, count, tokens),
        [
            tie(places, sent), packed_qkv, mixed_back, lse, doc_row, doc_col, projected, sums, first, grad_part,
            *qkv_pieces,
        ],
        [shape((3 * width, length), LOW), shape((length, width)), shape((2, width))],
        [low(width, 3 * width)],
        "attend_back",
        near=(1, 2, 3, 6, 8, 9), out_near=(0, 1),
        far=range(10, 100),
        sems=((8,),),
    )
    second = jnp.concatenate([grads_bn, grads_one, grads_two, jnp.zeros((2, width), F32)])
    if direct:
        second = second + swap(tie(second, down.back), CORE)
        second = second + swap(second, 1, "dp")
        second = second + swap(second, 2, "dp")
        second = tie(second, up.came)
        around = [swap(second, ACROSS), swap(second, ALONG), swap(second, ACROSS | ALONG)]
        sent = up.plane_two(second)
        down_sum = LineSum(down.plane_done(sent))
        around = tie(around, sent, down_sum.step())
        second = (second + around[0]) + (around[1] + around[2])
    else:
        second = lax.psum(second, ("dp", "shard"))
    roi_rows, out_rows = roi_width // shards, width // shards
    *roi_halves, low_projected = call(
        functools.partial(project_back_kernel, tokens),
        [places, grad_embedded, projected, sums, second, mixed, low_first, x],
        blocks(roi_rows + out_rows, width) + [shape((length, width), LOW)],
        [low(width, width), low(length, roi_width)],
        "project_back",
        near=(1, 2, 5, 6), out_near=(cores,),
        far=(8,),
        sems=((1,),),
    )
    roi = OwnedSum(roi_halves)
    start_packed = tie(places, low_projected)
    qkv_halves = call(
        functools.partial(packed_gradient_kernel, tokens),
        [start_packed, projected, sums, grad_packed],
        blocks(width // shards, 3 * width),
        [low(width, length), pltpu.VMEM((2, width, TILE), LOW), low(3 * width, length)],
        "packed_gradient",
        near=(1,),
        far=(3,),
        sems=((3,),),
    )
    qkv = OwnedSum(qkv_halves)
    sent = roi.plane_one(qkv_halves)
    if direct:
        up_sum = LineSum(up.plane_done(sent))
        sent = up_sum.step()
    def input_gradient(*sent):
        return call(
            functools.partial(input_gradient_kernel, count),
            [tie(places, *sent), low_projected, *roi_pieces],
            [shape((length, roi_width))],
            [low(roi_width, width)],
            "input_gradient",
            near=(1,),
            far=range(2, 100),
            sems=((8,),),
        )[0]

    if direct:
        sent = down_sum.step(sent)
        sent = roi_grad = input_gradient(sent)
        sent = roi.plane_two(sent)
        sent = qkv.plane_one(sent)
        sent = down_sum.step(up_sum.step(sent))
        roi_sum = LineSum(roi.plane_done(sent))
        sent = roi_sum.step()
        sent = qkv.plane_two(sent)
        sent = up_sum.step(sent)
        sent = roi_sum.step(sent)
        qkv_sum = LineSum(qkv.plane_done(sent))
        sent = qkv_sum.step()
        sent = roi_sum.step(sent)
        sent = qkv_sum.step(sent)
        sent = qkv_sum.step(sent)
        sum_roi, sum_down, sum_up, sum_qkv = [g.total() for g in (roi_sum, down_sum, up_sum, qkv_sum)]
        sum_roi, sum_out = sum_roi[:roi_rows], sum_roi[roi_rows:]
        sum_up = jnp.concatenate([sum_up[i * rows : (i + 1) * rows] for i in range(4)], axis=1)
    else:
        roi_grad = input_gradient()
        grads = [roi_halves[0][0, :roi_rows], roi_halves[0][0, roi_rows:], down_halves[0][0], qkv_halves[0][0]]
        grads.append(up_halves[0][0].reshape(4, width, width).swapaxes(0, 1).reshape(width, hidden))
        sum_roi, sum_out, sum_down, sum_qkv, sum_up = [
            lax.psum(lax.psum_scatter(grad, "shard", scatter_dimension=0, tiled=True), "dp").astype(F32) for grad in grads
        ]
    own = lax.dynamic_slice_in_dim(second, own_start, bn_gain.shape[0], 1)
    mean = sums[0] / tokens
    return (
        layer_out[None], roi_grad[None], sum_roi, own[1], own[0], sum_qkv, sum_out, own[2], own[3],
        sum_up, sum_down, own[4], own[5], mean, sums[1] / tokens - mean * mean,
    )


def solution(mesh):
    rows3, rows2, split2, split1 = P(("dp", "shard"), None, None), P(("dp", "shard"), None), P("shard", None), P("shard")
    return jax.shard_map(
        per_device,
        mesh=mesh,
        in_specs=(
            rows3, rows2, split2, split1, split1, split2, split2, split1, split1, split2, split2, split1, split1, rows3,
        ),
        out_specs=(
            rows3, rows3, split2, split1, split1, split2, split2, split1, split1, split2, split2, split1, split1, P(), P(),
        ),
        check_vma=False,
    )
```

```python
import functools
import math

import jax
import jax.numpy as jnp
from jax import lax
from jax.experimental import pallas as pl
from jax.experimental.pallas import tpu as pltpu
from jax.sharding import PartitionSpec as P

HEAD_DIM = 64
EPSILON = 1e-05
SCORE_SCALE = 0.125
MASKED = -1000000000.0
CORE, ACROSS, ALONG = 1, 2, 4
TILE = 256
F32, LOW = jnp.float32, jnp.bfloat16

ERFC_RATE = 0.33
ERFC = (
    0.18636612594127655,
    0.18283699452877045,
    0.20192526280879974,
    0.04500619322061539,
    0.4125494658946991,
    -0.3554469347000122,
    0.46269258856773376,
    -0.13592977821826935,
)


def direct_mesh():
    return lax.axis_size("shard") == 8 and lax.axis_size("dp") == 4


def swap(values, step, axis="shard"):
    size = lax.axis_size(axis)
    return lax.ppermute(values, axis, [(i, i ^ step) for i in range(size)])


def add_low(*terms):
    total = terms[0].astype(F32)
    for term in terms[1:]:
        total = total + term.astype(F32)
    return total.astype(LOW)


def sum_everywhere(part):
    if not direct_mesh():
        return lax.psum(part, ("dp", "shard"))
    part = part + swap(part, CORE)
    part = (part + swap(part, 1, "dp")) + (swap(part, 2, "dp") + swap(part, 3, "dp"))
    return (part + swap(part, ACROSS)) + (swap(part, ALONG) + swap(part, ACROSS | ALONG))


def tie(values, *after):
    return lax.optimization_barrier((values, after))[0]


class OwnedSum:
    def __init__(self, halves):
        self.direct = direct_mesh()
        if self.direct:
            self.mine, self.got = halves[0], swap(halves[1], CORE)
            rows = self.mine.shape[1] // 2
            self.cuts = ((slice(0, rows), 1, 2), (slice(rows, None), 2, 1))
        else:
            whole = halves[0].reshape(-1, halves[0].shape[-1])
            self.part = lax.psum_scatter(whole, "shard", scatter_dimension=0, tiled=True)

    def sent(self):
        mine, got = self.mine, self.got
        return [
            add_low(jnp.stack([mine[near, cut], mine[3, cut]]), jnp.stack([got[near, cut], got[3, cut]]))
            for cut, near, _ in self.cuts
        ]

    def passed(self):
        return [
            add_low(self.mine[far, cut], self.got[far, cut], came[1]) for came, (cut, _, far) in zip(self.came, self.cuts)
        ]

    def plane_one(self, *after):
        if not self.direct:
            return self.part
        self.mine, self.got = tie((self.mine, self.got), *after)
        sent = self.sent()
        self.came = [swap(part, 2 * near) for part, (_, near, _) in zip(sent, self.cuts)]
        return sent

    def plane_two(self, *after):
        if not self.direct:
            return self.part
        self.mine, self.got, self.came = tie((self.mine, self.got, self.came), *after)
        passed = self.passed()
        self.back = [swap(part, 2 * far) for part, (_, _, far) in zip(passed, self.cuts)]
        return passed

    def plane_done(self, *after):
        if not self.direct:
            return self.part
        mine, got, came, back = tie((self.mine, self.got, self.came, self.back), *after)
        return jnp.concatenate(
            [add_low(mine[0, cut], got[0, cut], c[0], b) for c, b, (cut, _, _) in zip(came, back, self.cuts)]
        )


def plane_together(older, newer, *after):
    older.mine, older.got, older.came, newer.mine, newer.got = tie(
        (older.mine, older.got, older.came, newer.mine, newer.got), *after
    )
    passed, sent = older.passed(), newer.sent()
    parts, size = [jnp.concatenate([new.reshape(-1, new.shape[-1]), old]) for new, old in zip(sent, passed[::-1])], sent[0]
    came = [swap(parts[0], ACROSS), swap(parts[1], ALONG)]
    rows = size.shape[0] * size.shape[1]
    newer.came = [part[:rows].reshape(size.shape) for part in came]
    older.back = [part[rows:] for part in came[::-1]]
    return parts


class LineSum:
    def __init__(self, part):
        self.part = part
        self.pairs = ([(0, 1), (3, 2)], [(1, 2), (2, 1)], [(1, 0), (2, 3)])
        self.number = 0

    def step(self, *after):
        if not direct_mesh():
            return self.part
        if self.number == 0:
            self.part = tie(self.part, *after)
        else:
            self.part = add_low(*tie((self.part, self.came), *after))
        self.came = lax.ppermute(self.part, "dp", self.pairs[self.number])
        self.number += 1
        return self.part

    def total(self):
        if not direct_mesh():
            return lax.psum(self.part, "dp").astype(F32)
        place = lax.axis_index("dp")
        return jnp.where((place == 1) | (place == 2), self.part, self.came).astype(F32)


def dot(left, right, left_dim=1, right_dim=0):
    return lax.dot_general(
        left, right, (((left_dim,), (right_dim,)), ((), ())), preferred_element_type=F32
    )


def wait_all(copies):
    for copy in copies:
        copy.wait()


def start_all(copies):
    for copy in copies:
        copy.start()
    return copies


def part(index, size):
    return pl.ds(pl.multiple_of(index * size, size), size)


def by_rows(count, body):
    @pl.loop(0, count // 128)
    def _(i):
        body(part(i, 128))


def piece_copies(pieces, places, target, sems, source_columns=None, columns=slice(None)):
    copies = []
    for i, piece in enumerate(pieces):
        rows = piece.shape[0]
        source = piece if source_columns is None else piece.at[:, source_columns]
        at = part(places[i], rows) if len(pieces) > 1 else pl.ds(0, rows)
        copies.append(pltpu.make_async_copy(source, target.at[at, columns], sems.at[i]))
    return copies


def wait_chunk(count, copies, places, target, sems, c):
    if count == 1:
        return c
    rows = target.shape[0] // 8
    for k in range(2):
        at = target.at[part(places[2 * c + k], rows)]
        pltpu.make_async_copy(at, at, sems.at[2 * c + k]).wait()
    return places[2 * c] >> 1


def put_blocks(halves, places, values, columns, work, section=0):
    if len(halves) == 1:
        halves[0][0, part(section, values.shape[0]), columns] = values.astype(LOW)
        return
    rows = values.shape[0] // 8
    work[...] = values.astype(LOW)
    for rel in range(8):
        halves[rel & 1][rel >> 1, part(section, rows), columns] = work[part(places[rel], rows), :]


def row_blocks(halves, places, make, rows=None):
    chips = halves[0].shape[0]
    rows = rows or halves[0].shape[1]
    if len(halves) == 1:
        step = min(rows, 512)

        @pl.loop(0, rows // step)
        def _(i):
            at = pl.multiple_of(i * step, step)
            halves[0][0, pl.ds(at, step)] = make(at, step).astype(LOW)

        return

    @pl.loop(0, chips)
    def _(j):
        for k in range(2):
            halves[k][j, :rows] = make(places[2 * j + k] * rows, rows).astype(LOW)


def lanes(first, size):
    return pl.ds(pl.multiple_of(first, 128), size)


def batch_scale(sums_ref, tokens):
    mean = sums_ref[0:1, :] * (1.0 / tokens)
    var = sums_ref[1:2, :] * (1.0 / tokens) - mean * mean
    return mean, var, lax.rsqrt(var + EPSILON)


def embed(projected_ref, sums_ref, tokens, rows=slice(None)):
    mean, _, inv = batch_scale(sums_ref, tokens)
    return (projected_ref[rows, :] - mean) * inv * sums_ref[2:3, :] + sums_ref[3:4, :]


def normalize(values):
    center = values - jnp.mean(values, axis=-1, keepdims=True)
    inv = lax.rsqrt(jnp.mean(center * center, axis=-1, keepdims=True) + EPSILON)
    return center * inv, inv


def normalize_back(scaled, normed, inv):
    return inv * (
        scaled
        - jnp.mean(scaled, axis=-1, keepdims=True)
        - normed * jnp.mean(scaled * normed, axis=-1, keepdims=True)
    )


def gelu_pair(values):
    t = 1.0 / (1.0 + (ERFC_RATE * 0.7071067811865476) * jnp.abs(values))
    poly = 0.5 * ERFC[-1]
    for factor in ERFC[-2::-1]:
        poly = poly * t + 0.5 * factor
    bell = jnp.exp(values * values * -0.5)
    tail = poly * t * bell
    share = jnp.where(values < 0, tail, 1.0 - tail)
    return values * share, share + values * bell * 0.3989422804014327


def size_of(array):
    return math.prod(array.shape) * jnp.dtype(array.dtype).itemsize


def call(kernel, args, outs, scratch, name, spare=6, far=(), loose=(), near=(), out_near=(), sems=()):
    spaces = [pl.ANY if i in loose else pltpu.HBM if i in far else pltpu.VMEM for i in range(len(args))]
    spaces[0] = pltpu.SMEM
    held = [a for i, a in enumerate(args) if i and i not in far and i not in near]
    held += [a for i, a in enumerate(outs) if i not in out_near] + list(scratch)
    args = [
        pltpu.with_memory_space_constraint(a, pltpu.HBM if i in far else pltpu.VMEM)
        if (i in far and i not in loose) or i in near
        else a
        for i, a in enumerate(args)
    ]
    return pl.pallas_call(
        kernel,
        in_specs=[pl.BlockSpec(memory_space=space) for space in spaces],
        out_specs=[pl.BlockSpec(memory_space=pltpu.VMEM)] * len(outs),
        out_shape=[pltpu.VMEM(a.shape, a.dtype) if i in out_near else a for i, a in enumerate(outs)],
        scratch_shapes=list(scratch) + [pltpu.SemaphoreType.DMA(count) for count in sems],
        compiler_params=pltpu.CompilerParams(vmem_limit_bytes=sum(map(size_of, held)) + spare * 2**20),
        cost_estimate=pl.CostEstimate(flops=1024, bytes_accessed=1024, transcendentals=0),
        name=name,
    )(*args)


def shape(dims, kind=F32):
    return jax.ShapeDtypeStruct(tuple(dims), kind)


def column_sum(values):
    return jnp.sum(values, axis=0, keepdims=True)


def project_kernel(count, places, x_ref, params_ref, *refs):
    pieces, (out_ref, sums_ref, weight, x, sems, sems_x) = refs[:count], refs[count:]
    copies = start_all([pltpu.make_async_copy(x_ref, x, sems_x.at[0])])
    wait_all(start_all(piece_copies(pieces, places, weight, sems)) + copies)
    sums_ref[...] = params_ref[...]

    @pl.loop(0, out_ref.shape[1] // TILE)
    def _(n):
        cols = part(n, TILE)
        values = dot(x[...], weight[:, cols])
        out_ref[:, cols] = values
        sums_ref[0:1, cols] = column_sum(values)
        sums_ref[1:2, cols] = column_sum(values * values)


def attend_kernel(count, tokens, places, projected_ref, sums_ref, doc_row, doc_col, *refs):
    pieces = refs[:count]
    packed_out, mixed_out, lse_out, weight, embedded, sems = refs[count:]
    length, width = projected_ref.shape

    def fetch(c):
        return piece_copies(pieces, places, weight, sems.at[c], part(c, width), part(c, width))

    for c in range(3):
        start_all(fetch(c))

    @functools.partial(by_rows, length)
    def _(rows):
        embedded[rows, :] = embed(projected_ref, sums_ref, tokens, rows).astype(LOW)

    @pl.loop(0, 3)
    def _(c):
        wait_all(fetch(c))
        for n in range(width // TILE):
            cols = part(c * (width // TILE) + n, TILE)
            packed_out[cols, :] = dot(embedded[...], weight[:, cols]).T.astype(LOW)

    same = doc_col[...] == doc_row[...]
    heads = width // HEAD_DIM

    @pl.loop(0, heads, unroll=3)
    def _(head):
        queries = packed_out[part(head, HEAD_DIM), :] * jnp.asarray(SCORE_SCALE, LOW)
        keys = packed_out[part(head + heads, HEAD_DIM), :]
        values = packed_out[part(head + 2 * heads, HEAD_DIM), :]
        scores = jnp.where(same, dot(keys, queries, 0, 0), MASKED)
        top = jnp.max(scores, axis=0, keepdims=True)
        expo = jnp.exp(scores - top)
        total = jnp.sum(expo, axis=0, keepdims=True)
        mixed = dot(values, expo.astype(LOW)) * (1.0 / total)
        mixed_out[part(head, HEAD_DIM), :] = mixed.astype(LOW)
        lse_out[pl.ds(head, 1), :] = top + jnp.log(total)


def expand_kernel(count, tokens, places, projected_ref, sums_ref, mixed_ref, *refs):
    ups, refs = refs[:count], refs[count:]
    hat_out, inv_out, active_out, slope_out, weight_out, weight_up, low_one, sems_out, sems_up = refs
    length, width = projected_ref.shape
    copies_out = start_all(piece_copies(ups, places, weight_out, sems_out, pl.ds(4 * width, width)))

    def fetch(c):
        return piece_copies(ups, places, weight_up, sems_up.at[c], part(c, width), part(c, width))

    for c in range(4):
        start_all(fetch(c))
    wait_all(copies_out)
    hat_out[...] = dot(mixed_ref[...], weight_out[...], 0, 0)

    @functools.partial(by_rows, length)
    def _(rows):
        hat, inv = normalize(embed(projected_ref, sums_ref, tokens, rows) + hat_out[rows, :])
        hat_out[rows, :] = hat
        inv_out[rows, :] = inv
        low_one[rows, :] = (hat * sums_ref[4:5, :] + sums_ref[5:6, :]).astype(LOW)

    @pl.loop(0, 4)
    def _(c):
        wait_all(fetch(c))
        for n in range(width // TILE):
            cols = part(c * (width // TILE) + n, TILE)
            active, slope = gelu_pair(dot(low_one[...], weight_up[:, cols]))
            active_out[:, cols] = active.astype(LOW)
            slope_out[:, cols] = slope.astype(LOW)


def contract_kernel(count, places, hat_ref, sums_ref, active_ref, grad_ref, *refs):
    pieces, refs = refs[:count], refs[count:]
    halves, refs = refs[:-9], refs[-9:]
    layer_out, back_out, grads_out, weight, branch, low_back, grad, sems, sems_grad = refs
    length, width = hat_ref.shape
    copies = start_all(piece_copies(pieces, places, weight, sems))
    grad_copy = start_all([pltpu.make_async_copy(grad_ref, grad, sems_grad.at[0])])
    if count == 1:
        wait_all(copies)

    @functools.partial(by_rows, length)
    def _(rows):
        branch[rows, :] = hat_ref[rows, :] * sums_ref[4:5, :] + sums_ref[5:6, :]

    @pl.loop(0, 4)
    def _(i):
        c = wait_chunk(count, copies, places, weight, sems, i)
        branch[...] += dot(active_ref[:, part(c, width)], weight[part(c, width), :])

    wait_all(grad_copy)
    grads_out[...] = jnp.zeros_like(grads_out)

    @functools.partial(by_rows, length)
    def _(rows):
        hat, inv = normalize(branch[rows, :])
        layer_out[rows, :] = (hat * sums_ref[6:7, :] + sums_ref[7:8, :]).astype(LOW)
        gradient = grad[rows, :].astype(F32)
        grads_out[0:1, :] += column_sum(gradient * hat)
        grads_out[1:2, :] += column_sum(gradient)
        back = normalize_back(gradient * sums_ref[6:7, :], hat, inv)
        back_out[rows, :] = back
        low_back[rows, :] = back.astype(LOW)

    row_blocks(halves, places, lambda at, n: dot(active_ref[:, lanes(at, n)], low_back[...], 0, 0))


def hidden_back_kernel(count, places, back_ref, hat_ref, sums_ref, slope_ref, *refs):
    pieces, refs = refs[:count], refs[count:]
    halves, (hidden_out, weight, low_back, low_one, work, sems) = refs[:-6], refs[-6:]
    length, width = hat_ref.shape
    copies = start_all(piece_copies(pieces, places, weight, sems))

    @functools.partial(by_rows, length)
    def _(rows):
        low_back[rows, :] = back_ref[rows, :].astype(LOW)
        low_one[:, rows] = (hat_ref[rows, :] * sums_ref[4:5, :] + sums_ref[5:6, :]).T.astype(LOW)

    if count == 1:
        wait_all(copies)

    @pl.loop(0, 4)
    def _(i):
        c = wait_chunk(count, copies, places, weight, sems, i)
        for n in range(width // TILE):
            cols = part(c * (width // TILE) + n, TILE)
            values = (dot(low_back[...], weight[cols, :], 1, 1) * slope_ref[:, cols].astype(F32)).astype(LOW)
            hidden_out[:, cols] = values
            put_blocks(halves, places, dot(low_one[...], values), slice(n * TILE, (n + 1) * TILE), work.at[n % 2], c)


def attend_back_head(head, first_head, packed_ref, mixed_back, lse_ref, same, out_ref, step, start):
    width = packed_ref.shape[0] // 3
    at = part(head + first_head, HEAD_DIM)
    queries = packed_ref[at, :] * jnp.asarray(SCORE_SCALE, LOW)
    at = part(head + first_head + width // HEAD_DIM, HEAD_DIM)
    keys = packed_ref[at, :]
    at = part(head + first_head + 2 * width // HEAD_DIM, HEAD_DIM)
    values = packed_ref[at, :]
    scores = jnp.where(same, dot(keys, queries, 0, 0), MASKED)
    probs = jnp.exp(scores - lse_ref[pl.ds(head + first_head, 1), :])
    grad_probs = dot(values, mixed_back, 0, 0)
    grad_values = dot(mixed_back, probs.astype(LOW), 1, 1)
    inner = jnp.sum(probs * grad_probs, axis=0, keepdims=True)
    grad_scores = (probs * (grad_probs - inner)).astype(LOW)
    grad_queries = dot(keys, grad_scores) * SCORE_SCALE
    grad_keys = dot(queries, grad_scores, 1, 1)
    for i, grad in enumerate((grad_queries, grad_keys, grad_values)):
        out_ref[part((i * step + start) // HEAD_DIM + head, HEAD_DIM), :] = grad.astype(LOW)


def expand_back_kernel(
    count, places, back_ref, hat_ref, inv_ref, sums_ref, hidden_ref, packed_ref, lse_ref, doc_row, doc_col, *refs
):
    ups, refs = refs[:count], refs[count:]
    (
        first_out, low_out, mixed_back_out, grads_out, grad_packed_out, weight_out, weight_up, total, sems_out, sems_up
    ) = refs
    length, width = hat_ref.shape

    def fetch(c):
        return piece_copies(ups, places, weight_up, sems_up.at[c], part(c, width), part(c, width))

    for c in range(4):
        start_all(fetch(c))
    copies_out = start_all(piece_copies(ups, places, weight_out, sems_out, pl.ds(4 * width, width)))
    total[...] = back_ref[...]

    @pl.loop(0, 4)
    def _(c):
        wait_all(fetch(c))
        total[...] += dot(hidden_ref[:, part(c, width)], weight_up[:, part(c, width)], 1, 1)

    grads_out[...] = jnp.zeros_like(grads_out)

    @functools.partial(by_rows, length)
    def _(rows):
        gradient, hat = total[rows, :], hat_ref[rows, :]
        grads_out[0:1, :] += column_sum(gradient * hat)
        grads_out[1:2, :] += column_sum(gradient)
        first = normalize_back(gradient * sums_ref[4:5, :], hat, inv_ref[rows, :])
        first_out[rows, :] = first
        low_out[rows, :] = first.astype(LOW)

    wait_all(copies_out)
    mixed_back_out[...] = dot(weight_out[...], low_out[...], 1, 1).astype(LOW)
    same = doc_col[...] == doc_row[...]
    heads = grad_packed_out.shape[0] // (3 * HEAD_DIM)

    @pl.loop(0, heads, unroll=3)
    def _(head):
        mixed_back = mixed_back_out[part(head, HEAD_DIM), :]
        attend_back_head(head, 0, packed_ref, mixed_back, lse_ref, same, grad_packed_out, heads * HEAD_DIM, 0)


def attend_back_kernel(
    count, tokens, places, packed_ref, mixed_back_ref, lse_ref, doc_row, doc_col, projected_ref, sums_ref, first_ref,
    done_ref, *refs
):
    pieces = refs[:count]
    grad_packed_out, embedded_out, grads_out, weight, sems = refs[count:]
    length, width = projected_ref.shape
    copies = start_all(piece_copies(pieces, places, weight, sems, pl.ds(0, 3 * width)))
    same = doc_col[...] == doc_row[...]
    done = done_ref.shape[0] // 3

    @pl.loop(0, (width - done) // HEAD_DIM, unroll=3)
    def _(head):
        mixed_back = mixed_back_ref[part(head + done // HEAD_DIM, HEAD_DIM), :]
        attend_back_head(head, done // HEAD_DIM, packed_ref, mixed_back, lse_ref, same, grad_packed_out, width, done)

    for i in range(3):
        grad_packed_out[i * width : i * width + done, :] = done_ref[i * done : (i + 1) * done, :]
    wait_all(copies)
    mean, _, inv = batch_scale(sums_ref, tokens)
    for n in range(width // TILE):
        cols = slice(n * TILE, (n + 1) * TILE)
        values = first_ref[:, cols] + dot(weight[cols, :], grad_packed_out[...]).T
        embedded_out[:, cols] = values
        normed = (projected_ref[:, cols] - mean[:, cols]) * inv[:, cols]
        grads_out[0:1, cols] = column_sum(values)
        grads_out[1:2, cols] = column_sum(values * normed)


def packed_gradient_kernel(tokens, places, projected_ref, sums_ref, grad_packed_ref, *refs):
    halves, (low, work, grad_packed, sems) = refs[:-4], refs[-4:]
    length, width = projected_ref.shape

    def fetch(c):
        return pltpu.make_async_copy(grad_packed_ref.at[part(c, width)], grad_packed.at[part(c, width)], sems.at[c])

    for c in range(3):
        fetch(c).start()

    @functools.partial(by_rows, length)
    def _(rows):
        low[:, rows] = embed(projected_ref, sums_ref, tokens, rows).T.astype(LOW)

    @pl.loop(0, 3)
    def _(c):
        fetch(c).wait()
        for n in range(width // TILE):
            cols = part(c * (width // TILE) + n, TILE)
            put_blocks(halves, places, dot(low[...], grad_packed[cols, :], 1, 1), cols, work.at[n % 2])


def project_back_kernel(tokens, places, embedded_ref, projected_ref, sums_ref, grads_ref, mixed_ref, low_ref, x_ref, *refs):
    halves, (low_out, work, x, sems) = refs[:-4], refs[-4:]
    copies = start_all([pltpu.make_async_copy(x_ref, x, sems.at[0])])
    mean, _, inv = batch_scale(sums_ref, tokens)
    roi_rows = x_ref.shape[1] * halves[0].shape[1] // (x_ref.shape[1] + low_ref.shape[1])

    @functools.partial(by_rows, projected_ref.shape[0])
    def _(rows):
        normed = (projected_ref[rows, :] - mean) * inv
        shift = grads_ref[0:1, :] * (1.0 / tokens) + normed * (grads_ref[1:2, :] * (1.0 / tokens))
        low_out[rows, :] = (sums_ref[2:3, :] * inv * (embedded_ref[rows, :] - shift)).astype(LOW)

    wait_all(copies)
    row_blocks(halves, places, lambda at, n: dot(x[:, lanes(at, n)], low_out[...], 0, 0), roi_rows)
    work[...] = dot(mixed_ref[...], low_ref[...]).astype(LOW)
    if len(halves) == 1:
        halves[0][0, roi_rows:, :] = work[...]
    else:
        rows = halves[0].shape[1] - roi_rows
        for rel in range(8):
            halves[rel & 1][rel >> 1, roi_rows:, :] = work[part(places[rel], rows), :]


def input_gradient_kernel(count, places, low_ref, *refs):
    pieces, (out_ref, weight, sems) = refs[:count], refs[count:]
    wait_all(start_all(piece_copies(pieces, places, weight, sems)))

    @pl.loop(0, weight.shape[0] // 512)
    def _(i):
        out_ref[:, part(i, 512)] = dot(low_ref[...], weight[part(i, 512), :], 1, 1)


def sides(own):
    return [swap(own, ACROSS), swap(own, ALONG)]


def corner_halves(across, along):
    half = across.shape[0] // 2
    return [swap(along[:half], ACROSS), swap(across[half:], ALONG)]


def with_cores(chips):
    pieces = []
    for shard in chips:
        pieces += [shard, swap(shard, CORE)]
    return pieces


def per_device(
    roi_features, doc_ids, w_roi, bn_gain, bn_beta, w_qkv, w_out, ln1_gain, ln1_beta,
    w_up, w_down, ln2_gain, ln2_beta, cotangent,
):
    _, length, roi_width = roi_features.shape
    width, hidden = w_roi.shape[1], w_up.shape[1]
    devices = lax.axis_size("dp") * lax.axis_size("shard")
    tokens = length * devices
    me = lax.axis_index("shard")
    direct = direct_mesh()
    shards, rows = 8 if direct else 1, w_up.shape[0]
    cores, chips = (2, 4) if direct else (1, 1)
    places = (me ^ jnp.arange(8)).astype(jnp.int32) if direct else jnp.zeros((8,), jnp.int32)

    x = roi_features.reshape(length, roi_width)
    doc_row, doc_col = doc_ids.reshape(1, length), doc_ids.reshape(length, 1)
    own_params = jnp.stack([bn_gain, bn_beta, ln1_gain, ln1_beta, ln2_gain, ln2_beta]).astype(F32)
    own_params = jnp.where(lax.axis_index("dp") == 0, own_params, 0.0)
    own_start = me * bn_gain.shape[0]
    params = lax.dynamic_update_slice(jnp.zeros((8, width), F32), own_params, (2, own_start))

    gather = functools.partial(lax.all_gather, axis_name="shard", axis=0, tiled=True)
    wide_up = jnp.concatenate([w_up, w_out], axis=1)
    if direct:
        roi_chips = [w_roi, *sides(w_roi), swap(w_roi, ACROSS | ALONG)]
        w_qkv = tie(w_qkv, params, wide_up)
        qkv_chips = [w_qkv, *sides(w_qkv), swap(w_qkv, ACROSS | ALONG)]
        roi_pieces = with_cores(tie(roi_chips, w_qkv))
    else:
        roi_pieces = [gather(w_roi)]
    count = len(roi_pieces)

    def blocks(r, c):
        return [shape((chips, r, c), LOW)] * cores

    def low(r, c):
        return pltpu.VMEM((r, c), LOW)

    projected, sums = call(
        functools.partial(project_kernel, count),
        [places, x, params, *roi_pieces],
        [shape((length, width)), shape((8, width))],
        [low(roi_width, width), low(length, roi_width)],
        "project",
        out_near=(0,),
        far=(1, *range(3, 100)),
        sems=((8,), (1,)),
        loose=(4, 6, 8, 10),
    )
    if direct:
        sums = sums + swap(sums, CORE)
        sums = sums + swap(sums, 1, "dp")
        sums = sums + swap(sums, 2, "dp")
        around = [swap(sums, ACROSS), swap(sums, ALONG), swap(sums, ACROSS | ALONG)]
        qkv_chips = tie(qkv_chips, sums)
        around = tie(around, qkv_chips)
        sums = (sums + around[0]) + (around[1] + around[2])
        qkv_pieces = with_cores(qkv_chips)
        up_sides = sides(tie(wide_up, sums))
    else:
        sums = lax.psum(sums, ("dp", "shard"))
        qkv_pieces = [gather(w_qkv)]

    heads = width // HEAD_DIM
    part_width = heads // 2 * HEAD_DIM
    packed_qkv, mixed, lse = call(
        functools.partial(attend_kernel, count, tokens),
        [places, projected, sums, doc_row, doc_col, *qkv_pieces],
        [shape((3 * width, length), LOW), shape((width, length), LOW), shape((heads, length))],
        [low(width, 3 * width), low(length, width)],
        "attend",
        near=(1,), out_near=(0, 1, 2),
        far=range(5, 100),
        sems=((3, 8),),
        loose=(6, 8, 10, 12),
    )
    if direct:
        up_sides = tie(up_sides, mixed)
        up_corner = jnp.concatenate(corner_halves(*up_sides))
        down_sides = sides(tie(w_down, up_sides))
        up_pieces = with_cores([wide_up, *up_sides, up_corner])
    else:
        up_pieces, down_parts = [gather(wide_up)], [gather(w_down)]
    hat, inv, active, slope = call(
        functools.partial(expand_kernel, count, tokens),
        [places, projected, sums, mixed, *up_pieces],
        [shape((length, width)), shape((length, 1)), shape((length, hidden), LOW), shape((length, hidden), LOW)],
        [low(width, width), low(width, hidden), low(length, width)],
        "expand",
        near=(1, 3), out_near=(0, 1, 2, 3),
        far=range(4, 100),
        sems=((8,), (4, 8)),
        loose=(5, 7, 9, 11),
    )
    if direct:
        down_sides = tie(down_sides, active)
        down_parts = with_cores([w_down, *down_sides, jnp.concatenate(corner_halves(*down_sides))])
    *down_halves, layer_out, back, grads_two = call(
        functools.partial(contract_kernel, count),
        [places, hat, sums, active, cotangent.reshape(length, width), *down_parts],
        blocks(hidden // shards, width) + [shape((length, width), LOW), shape((length, width)), shape((2, width))],
        [low(hidden, width), pltpu.VMEM((length, width), F32), low(length, width), low(length, width)],
        "contract",
        near=(1, 3), out_near=(cores + 1,),
        far=range(4, 100),
        sems=((8,), (1,)),
        loose=(6, 8, 10, 12),
    )
    down = OwnedSum(down_halves)
    *up_halves, grad_hidden = call(
        functools.partial(hidden_back_kernel, count),
        [places, back, hat, sums, slope, *down_parts],
        blocks(hidden // shards, width) + [shape((length, hidden), LOW)],
        [low(hidden, width), low(length, width), low(width, length), pltpu.VMEM((2, width, TILE), LOW)],
        "hidden_back",
        near=(1, 2, 4), out_near=(cores,),
        far=range(5, 100),
        sems=((8,),),
    )
    up = OwnedSum(up_halves)
    sent = down.plane_one(grad_hidden)
    first, low_first, mixed_back, grads_one, grad_part = call(
        functools.partial(expand_back_kernel, count),
        [
            tie(places, sent), back, hat, inv, sums, grad_hidden, packed_qkv, lse, doc_row, doc_col, *up_pieces,
        ],
        [
            shape((length, width)), shape((length, width), LOW), shape((width, length), LOW), shape((2, width)),
            shape((3 * part_width, length), LOW),
        ],
        [low(width, width), low(width, hidden), pltpu.VMEM((length, width), F32)],
        "expand_back",
        near=(1, 2, 3, 5, 6, 7), out_near=(0, 1, 2, 4),
        far=range(10, 100),
        sems=((8,), (4, 8)),
    )
    sent = plane_together(down, up, first) if direct else first
    grad_packed, grad_embedded, grads_bn = call(
        functools.partial(attend_back_kernel, count, tokens),
        [
            tie(places, sent), packed_qkv, mixed_back, lse, doc_row, doc_col, projected, sums, first, grad_part,
            *qkv_pieces,
        ],
        [shape((3 * width, length), LOW), shape((length, width)), shape((2, width))],
        [low(width, 3 * width)],
        "attend_back",
        near=(1, 2, 3, 6, 8, 9), out_near=(0, 1),
        far=range(10, 100),
        sems=((8,),),
    )
    second = jnp.concatenate([grads_bn, grads_one, grads_two, jnp.zeros((2, width), F32)])
    if direct:
        second = second + swap(second, CORE)
        second = second + swap(second, 1, "dp")
        second = second + swap(second, 2, "dp")
        second = tie(second, up.came)
        around = [swap(second, ACROSS), swap(second, ALONG), swap(second, ACROSS | ALONG)]
        sent = up.plane_two(second)
        down_sum = LineSum(down.plane_done(sent))
        around = tie(around, sent, down_sum.step())
        second = (second + around[0]) + (around[1] + around[2])
    else:
        second = lax.psum(second, ("dp", "shard"))
    roi_rows, out_rows = roi_width // shards, width // shards
    *roi_halves, low_projected = call(
        functools.partial(project_back_kernel, tokens),
        [places, grad_embedded, projected, sums, second, mixed, low_first, x],
        blocks(roi_rows + out_rows, width) + [shape((length, width), LOW)],
        [low(width, width), low(length, roi_width)],
        "project_back",
        near=(1, 2, 5, 6), out_near=(cores,),
        far=(8,),
        sems=((1,),),
    )
    roi = OwnedSum(roi_halves)
    start_packed = tie(places, low_projected)
    qkv_halves = call(
        functools.partial(packed_gradient_kernel, tokens),
        [start_packed, projected, sums, grad_packed],
        blocks(width // shards, 3 * width),
        [low(width, length), pltpu.VMEM((2, width, TILE), LOW), low(3 * width, length)],
        "packed_gradient",
        near=(1,),
        far=(3,),
        sems=((3,),),
    )
    qkv = OwnedSum(qkv_halves)
    sent = roi.plane_one(qkv_halves)
    if direct:
        up_sum = LineSum(up.plane_done(sent))
        sent = up_sum.step()
    def input_gradient(*sent):
        return call(
            functools.partial(input_gradient_kernel, count),
            [tie(places, *sent), low_projected, *roi_pieces],
            [shape((length, roi_width))],
            [low(roi_width, width)],
            "input_gradient",
            near=(1,),
            far=range(2, 100),
            sems=((8,),),
        )[0]

    if direct:
        sent = down_sum.step(sent)
        sent = roi.plane_two(sent)
        sent = qkv.plane_one(sent)
        sent = down_sum.step(up_sum.step(sent))
        roi_sum = LineSum(roi.plane_done(sent))
        sent = roi_sum.step()
        sent = qkv.plane_two(sent)
        sent = up_sum.step(sent)
        sent = roi_sum.step(sent)
        qkv_sum = LineSum(qkv.plane_done(sent))
        sent = qkv_sum.step()
        sent = roi_sum.step(sent)
        sent = qkv_sum.step(sent)
        sent = roi_grad = input_gradient(sent)
        sent = qkv_sum.step(sent)
        sum_roi, sum_down, sum_up, sum_qkv = [g.total() for g in (roi_sum, down_sum, up_sum, qkv_sum)]
        sum_roi, sum_out = sum_roi[:roi_rows], sum_roi[roi_rows:]
        sum_up = jnp.concatenate([sum_up[i * rows : (i + 1) * rows] for i in range(4)], axis=1)
    else:
        roi_grad = input_gradient()
        grads = [roi_halves[0][0, :roi_rows], roi_halves[0][0, roi_rows:], down_halves[0][0], qkv_halves[0][0]]
        grads.append(up_halves[0][0].reshape(4, width, width).swapaxes(0, 1).reshape(width, hidden))
        sum_roi, sum_out, sum_down, sum_qkv, sum_up = [
            lax.psum(lax.psum_scatter(grad, "shard", scatter_dimension=0, tiled=True), "dp").astype(F32) for grad in grads
        ]
    own = lax.dynamic_slice_in_dim(second, own_start, bn_gain.shape[0], 1)
    mean = sums[0] / tokens
    return (
        layer_out[None], roi_grad[None], sum_roi, own[1], own[0], sum_qkv, sum_out, own[2], own[3],
        sum_up, sum_down, own[4], own[5], mean, sums[1] / tokens - mean * mean,
    )


def solution(mesh):
    rows3, rows2, split2, split1 = P(("dp", "shard"), None, None), P(("dp", "shard"), None), P("shard", None), P("shard")
    return jax.shard_map(
        per_device,
        mesh=mesh,
        in_specs=(
            rows3, rows2, split2, split1, split1, split2, split2, split1, split1, split2, split2, split1, split1, rows3,
        ),
        out_specs=(
            rows3, rows3, split2, split1, split1, split2, split2, split1, split1, split2, split2, split1, split1, P(), P(),
        ),
        check_vma=False,
    )
```

```python
import functools
import math

import jax
import jax.numpy as jnp
from jax import lax
from jax.experimental import pallas as pl
from jax.experimental.pallas import tpu as pltpu
from jax.sharding import PartitionSpec as P

HEAD_DIM = 64
EPSILON = 1e-05
SCORE_SCALE = 0.125
MASKED = -1000000000.0
CORE, ACROSS, ALONG = 1, 2, 4
TILE = 256
F32, LOW = jnp.float32, jnp.bfloat16

ERFC_RATE = 0.33
ERFC = (
    0.18636612594127655,
    0.18283699452877045,
    0.20192526280879974,
    0.04500619322061539,
    0.4125494658946991,
    -0.3554469347000122,
    0.46269258856773376,
    -0.13592977821826935,
)


def direct_mesh():
    return lax.axis_size("shard") == 8 and lax.axis_size("dp") == 4


def swap(values, step, axis="shard"):
    size = lax.axis_size(axis)
    return lax.ppermute(values, axis, [(i, i ^ step) for i in range(size)])


def add_low(*terms):
    total = terms[0].astype(F32)
    for term in terms[1:]:
        total = total + term.astype(F32)
    return total.astype(LOW)


def sum_everywhere(part):
    if not direct_mesh():
        return lax.psum(part, ("dp", "shard"))
    part = part + swap(part, CORE)
    part = (part + swap(part, 1, "dp")) + (swap(part, 2, "dp") + swap(part, 3, "dp"))
    return (part + swap(part, ACROSS)) + (swap(part, ALONG) + swap(part, ACROSS | ALONG))


def tie(values, *after):
    return lax.optimization_barrier((values, after))[0]


class OwnedSum:
    def __init__(self, halves):
        self.direct = direct_mesh()
        if self.direct:
            self.mine, self.got = halves[0], swap(halves[1], CORE)
            rows = self.mine.shape[1] // 2
            self.cuts = ((slice(0, rows), 1, 2), (slice(rows, None), 2, 1))
        else:
            whole = halves[0].reshape(-1, halves[0].shape[-1])
            self.part = lax.psum_scatter(whole, "shard", scatter_dimension=0, tiled=True)

    def sent(self):
        mine, got = self.mine, self.got
        return [
            add_low(jnp.stack([mine[near, cut], mine[3, cut]]), jnp.stack([got[near, cut], got[3, cut]]))
            for cut, near, _ in self.cuts
        ]

    def passed(self):
        return [
            add_low(self.mine[far, cut], self.got[far, cut], came[1]) for came, (cut, _, far) in zip(self.came, self.cuts)
        ]

    def plane_one(self, *after):
        if not self.direct:
            return self.part
        self.mine, self.got = tie((self.mine, self.got), *after)
        sent = self.sent()
        self.came = [swap(part, 2 * near) for part, (_, near, _) in zip(sent, self.cuts)]
        return sent

    def plane_two(self, *after):
        if not self.direct:
            return self.part
        self.mine, self.got, self.came = tie((self.mine, self.got, self.came), *after)
        passed = self.passed()
        self.back = [swap(part, 2 * far) for part, (_, _, far) in zip(passed, self.cuts)]
        return passed

    def plane_done(self, *after):
        if not self.direct:
            return self.part
        mine, got, came, back = tie((self.mine, self.got, self.came, self.back), *after)
        return jnp.concatenate(
            [add_low(mine[0, cut], got[0, cut], c[0], b) for c, b, (cut, _, _) in zip(came, back, self.cuts)]
        )


def plane_together(older, newer, *after):
    older.mine, older.got, older.came, newer.mine, newer.got = tie(
        (older.mine, older.got, older.came, newer.mine, newer.got), *after
    )
    passed, sent = older.passed(), newer.sent()
    parts, size = [jnp.concatenate([new.reshape(-1, new.shape[-1]), old]) for new, old in zip(sent, passed[::-1])], sent[0]
    came = [swap(parts[0], ACROSS), swap(parts[1], ALONG)]
    rows = size.shape[0] * size.shape[1]
    newer.came = [part[:rows].reshape(size.shape) for part in came]
    older.back = [part[rows:] for part in came[::-1]]
    return parts


class LineSum:
    def __init__(self, part):
        self.part = part
        self.pairs = ([(0, 1), (3, 2)], [(1, 2), (2, 1)], [(1, 0), (2, 3)])
        self.number = 0

    def step(self, *after):
        if not direct_mesh():
            return self.part
        if self.number == 0:
            self.part = tie(self.part, *after)
        else:
            self.part = add_low(*tie((self.part, self.came), *after))
        self.came = lax.ppermute(self.part, "dp", self.pairs[self.number])
        self.number += 1
        return self.part

    def total(self):
        if not direct_mesh():
            return lax.psum(self.part, "dp").astype(F32)
        place = lax.axis_index("dp")
        return jnp.where((place == 1) | (place == 2), self.part, self.came).astype(F32)


def dot(left, right, left_dim=1, right_dim=0):
    return lax.dot_general(
        left, right, (((left_dim,), (right_dim,)), ((), ())), preferred_element_type=F32
    )


def wait_all(copies):
    for copy in copies:
        copy.wait()


def start_all(copies):
    for copy in copies:
        copy.start()
    return copies


def part(index, size):
    return pl.ds(pl.multiple_of(index * size, size), size)


def by_rows(count, body):
    @pl.loop(0, count // 128)
    def _(i):
        body(part(i, 128))


def piece_copies(pieces, places, target, sems, source_columns=None, columns=slice(None)):
    copies = []
    for i, piece in enumerate(pieces):
        rows = piece.shape[0]
        source = piece if source_columns is None else piece.at[:, source_columns]
        at = part(places[i], rows) if len(pieces) > 1 else pl.ds(0, rows)
        copies.append(pltpu.make_async_copy(source, target.at[at, columns], sems.at[i]))
    return copies


def wait_chunk(count, copies, places, target, sems, c):
    if count == 1:
        return c
    rows = target.shape[0] // 8
    for k in range(2):
        at = target.at[part(places[2 * c + k], rows)]
        pltpu.make_async_copy(at, at, sems.at[2 * c + k]).wait()
    return places[2 * c] >> 1


def put_blocks(halves, places, values, columns, work, section=0):
    if len(halves) == 1:
        halves[0][0, part(section, values.shape[0]), columns] = values.astype(LOW)
        return
    rows = values.shape[0] // 8
    work[...] = values.astype(LOW)
    for rel in range(8):
        halves[rel & 1][rel >> 1, part(section, rows), columns] = work[part(places[rel], rows), :]


def row_blocks(halves, places, make, rows=None):
    chips = halves[0].shape[0]
    rows = rows or halves[0].shape[1]
    if len(halves) == 1:
        step = min(rows, 512)

        @pl.loop(0, rows // step)
        def _(i):
            at = pl.multiple_of(i * step, step)
            halves[0][0, pl.ds(at, step)] = make(at, step).astype(LOW)

        return

    @pl.loop(0, chips, unroll=2)
    def _(j):
        for k in range(2):
            halves[k][j, :rows] = make(places[2 * j + k] * rows, rows).astype(LOW)


def lanes(first, size):
    return pl.ds(pl.multiple_of(first, 128), size)


def batch_scale(sums_ref, tokens):
    mean = sums_ref[0:1, :] * (1.0 / tokens)
    var = sums_ref[1:2, :] * (1.0 / tokens) - mean * mean
    return mean, var, lax.rsqrt(var + EPSILON)


def embed(projected_ref, sums_ref, tokens, rows=slice(None)):
    mean, _, inv = batch_scale(sums_ref, tokens)
    return (projected_ref[rows, :] - mean) * inv * sums_ref[2:3, :] + sums_ref[3:4, :]


def normalize(values):
    center = values - jnp.mean(values, axis=-1, keepdims=True)
    inv = lax.rsqrt(jnp.mean(center * center, axis=-1, keepdims=True) + EPSILON)
    return center * inv, inv


def normalize_back(scaled, normed, inv):
    return inv * (
        scaled
        - jnp.mean(scaled, axis=-1, keepdims=True)
        - normed * jnp.mean(scaled * normed, axis=-1, keepdims=True)
    )


def gelu_pair(values):
    t = 1.0 / (1.0 + (ERFC_RATE * 0.7071067811865476) * jnp.abs(values))
    poly = 0.5 * ERFC[-1]
    for factor in ERFC[-2::-1]:
        poly = poly * t + 0.5 * factor
    bell = jnp.exp(values * values * -0.5)
    tail = poly * t * bell
    share = jnp.where(values < 0, tail, 1.0 - tail)
    return values * share, share + values * bell * 0.3989422804014327


def size_of(array):
    return math.prod(array.shape) * jnp.dtype(array.dtype).itemsize


def call(kernel, args, outs, scratch, name, spare=6, far=(), loose=(), near=(), out_near=(), sems=()):
    spaces = [pl.ANY if i in loose else pltpu.HBM if i in far else pltpu.VMEM for i in range(len(args))]
    spaces[0] = pltpu.SMEM
    held = [a for i, a in enumerate(args) if i and i not in far and i not in near]
    held += [a for i, a in enumerate(outs) if i not in out_near] + list(scratch)
    args = [
        pltpu.with_memory_space_constraint(a, pltpu.HBM if i in far else pltpu.VMEM)
        if (i in far and i not in loose) or i in near
        else a
        for i, a in enumerate(args)
    ]
    return pl.pallas_call(
        kernel,
        in_specs=[pl.BlockSpec(memory_space=space) for space in spaces],
        out_specs=[pl.BlockSpec(memory_space=pltpu.VMEM)] * len(outs),
        out_shape=[pltpu.VMEM(a.shape, a.dtype) if i in out_near else a for i, a in enumerate(outs)],
        scratch_shapes=list(scratch) + [pltpu.SemaphoreType.DMA(count) for count in sems],
        compiler_params=pltpu.CompilerParams(vmem_limit_bytes=sum(map(size_of, held)) + spare * 2**20),
        cost_estimate=pl.CostEstimate(flops=1024, bytes_accessed=1024, transcendentals=0),
        name=name,
    )(*args)


def shape(dims, kind=F32):
    return jax.ShapeDtypeStruct(tuple(dims), kind)


def column_sum(values):
    return jnp.sum(values, axis=0, keepdims=True)


def project_kernel(count, places, x_ref, params_ref, *refs):
    pieces, (out_ref, sums_ref, weight, x, sems, sems_x) = refs[:count], refs[count:]
    copies = start_all([pltpu.make_async_copy(x_ref, x, sems_x.at[0])])
    wait_all(start_all(piece_copies(pieces, places, weight, sems)) + copies)
    sums_ref[...] = params_ref[...]

    @pl.loop(0, out_ref.shape[1] // TILE)
    def _(n):
        cols = part(n, TILE)
        values = dot(x[...], weight[:, cols])
        out_ref[:, cols] = values
        sums_ref[0:1, cols] = column_sum(values)
        sums_ref[1:2, cols] = column_sum(values * values)


def attend_kernel(count, tokens, places, projected_ref, sums_ref, doc_row, doc_col, *refs):
    pieces = refs[:count]
    packed_out, mixed_out, lse_out, weight, embedded, sems = refs[count:]
    length, width = projected_ref.shape

    def fetch(c):
        return piece_copies(pieces, places, weight, sems.at[c], part(c, width), part(c, width))

    for c in range(3):
        start_all(fetch(c))

    @functools.partial(by_rows, length)
    def _(rows):
        embedded[rows, :] = embed(projected_ref, sums_ref, tokens, rows).astype(LOW)

    @pl.loop(0, 3)
    def _(c):
        wait_all(fetch(c))
        for n in range(width // TILE):
            cols = part(c * (width // TILE) + n, TILE)
            packed_out[cols, :] = dot(embedded[...], weight[:, cols]).T.astype(LOW)

    same = doc_col[...] == doc_row[...]
    heads = width // HEAD_DIM

    @pl.loop(0, heads, unroll=3)
    def _(head):
        queries = packed_out[part(head, HEAD_DIM), :] * jnp.asarray(SCORE_SCALE, LOW)
        keys = packed_out[part(head + heads, HEAD_DIM), :]
        values = packed_out[part(head + 2 * heads, HEAD_DIM), :]
        scores = jnp.where(same, dot(keys, queries, 0, 0), MASKED)
        top = jnp.max(scores, axis=0, keepdims=True)
        expo = jnp.exp(scores - top)
        total = jnp.sum(expo, axis=0, keepdims=True)
        mixed = dot(values, expo.astype(LOW)) * (1.0 / total)
        mixed_out[part(head, HEAD_DIM), :] = mixed.astype(LOW)
        lse_out[pl.ds(head, 1), :] = top + jnp.log(total)


def expand_kernel(count, tokens, places, projected_ref, sums_ref, mixed_ref, *refs):
    ups, refs = refs[:count], refs[count:]
    hat_out, inv_out, active_out, slope_out, weight_out, weight_up, low_one, sems_out, sems_up = refs
    length, width = projected_ref.shape
    copies_out = start_all(piece_copies(ups, places, weight_out, sems_out, pl.ds(4 * width, width)))

    def fetch(c):
        return piece_copies(ups, places, weight_up, sems_up.at[c], part(c, width), part(c, width))

    for c in range(4):
        start_all(fetch(c))
    wait_all(copies_out)
    hat_out[...] = dot(mixed_ref[...], weight_out[...], 0, 0)

    @functools.partial(by_rows, length)
    def _(rows):
        hat, inv = normalize(embed(projected_ref, sums_ref, tokens, rows) + hat_out[rows, :])
        hat_out[rows, :] = hat
        inv_out[rows, :] = inv
        low_one[rows, :] = (hat * sums_ref[4:5, :] + sums_ref[5:6, :]).astype(LOW)

    @pl.loop(0, 4)
    def _(c):
        wait_all(fetch(c))
        for n in range(width // TILE):
            cols = part(c * (width // TILE) + n, TILE)
            active, slope = gelu_pair(dot(low_one[...], weight_up[:, cols]))
            active_out[:, cols] = active.astype(LOW)
            slope_out[:, cols] = slope.astype(LOW)


def contract_kernel(count, places, hat_ref, sums_ref, active_ref, grad_ref, *refs):
    pieces, refs = refs[:count], refs[count:]
    halves, refs = refs[:-9], refs[-9:]
    layer_out, back_out, grads_out, weight, branch, low_back, grad, sems, sems_grad = refs
    length, width = hat_ref.shape
    copies = start_all(piece_copies(pieces, places, weight, sems))
    grad_copy = start_all([pltpu.make_async_copy(grad_ref, grad, sems_grad.at[0])])
    if count == 1:
        wait_all(copies)

    @functools.partial(by_rows, length)
    def _(rows):
        branch[rows, :] = hat_ref[rows, :] * sums_ref[4:5, :] + sums_ref[5:6, :]

    @pl.loop(0, 4)
    def _(i):
        c = wait_chunk(count, copies, places, weight, sems, i)
        branch[...] += dot(active_ref[:, part(c, width)], weight[part(c, width), :])

    wait_all(grad_copy)
    grads_out[...] = jnp.zeros_like(grads_out)

    @functools.partial(by_rows, length)
    def _(rows):
        hat, inv = normalize(branch[rows, :])
        layer_out[rows, :] = (hat * sums_ref[6:7, :] + sums_ref[7:8, :]).astype(LOW)
        gradient = grad[rows, :].astype(F32)
        grads_out[0:1, :] += column_sum(gradient * hat)
        grads_out[1:2, :] += column_sum(gradient)
        back = normalize_back(gradient * sums_ref[6:7, :], hat, inv)
        back_out[rows, :] = back
        low_back[rows, :] = back.astype(LOW)

    row_blocks(halves, places, lambda at, n: dot(active_ref[:, lanes(at, n)], low_back[...], 0, 0))


def hidden_back_kernel(count, places, back_ref, hat_ref, sums_ref, slope_ref, *refs):
    pieces, refs = refs[:count], refs[count:]
    halves, (hidden_out, weight, low_back, low_one, work, sems) = refs[:-6], refs[-6:]
    length, width = hat_ref.shape
    copies = start_all(piece_copies(pieces, places, weight, sems))

    @functools.partial(by_rows, length)
    def _(rows):
        low_back[rows, :] = back_ref[rows, :].astype(LOW)
        low_one[:, rows] = (hat_ref[rows, :] * sums_ref[4:5, :] + sums_ref[5:6, :]).T.astype(LOW)

    if count == 1:
        wait_all(copies)

    @pl.loop(0, 4)
    def _(i):
        c = wait_chunk(count, copies, places, weight, sems, i)
        for n in range(width // TILE):
            cols = part(c * (width // TILE) + n, TILE)
            values = (dot(low_back[...], weight[cols, :], 1, 1) * slope_ref[:, cols].astype(F32)).astype(LOW)
            hidden_out[:, cols] = values
            put_blocks(halves, places, dot(low_one[...], values), slice(n * TILE, (n + 1) * TILE), work.at[n % 2], c)


def attend_back_head(head, first_head, packed_ref, mixed_back, lse_ref, same, out_ref, step, start):
    width = packed_ref.shape[0] // 3
    at = part(head + first_head, HEAD_DIM)
    queries = packed_ref[at, :] * jnp.asarray(SCORE_SCALE, LOW)
    at = part(head + first_head + width // HEAD_DIM, HEAD_DIM)
    keys = packed_ref[at, :]
    at = part(head + first_head + 2 * width // HEAD_DIM, HEAD_DIM)
    values = packed_ref[at, :]
    scores = jnp.where(same, dot(keys, queries, 0, 0), MASKED)
    probs = jnp.exp(scores - lse_ref[pl.ds(head + first_head, 1), :])
    grad_probs = dot(values, mixed_back, 0, 0)
    grad_values = dot(mixed_back, probs.astype(LOW), 1, 1)
    inner = jnp.sum(probs * grad_probs, axis=0, keepdims=True)
    grad_scores = (probs * (grad_probs - inner)).astype(LOW)
    grad_queries = dot(keys, grad_scores) * SCORE_SCALE
    grad_keys = dot(queries, grad_scores, 1, 1)
    for i, grad in enumerate((grad_queries, grad_keys, grad_values)):
        out_ref[part((i * step + start) // HEAD_DIM + head, HEAD_DIM), :] = grad.astype(LOW)


def expand_back_kernel(
    count, places, back_ref, hat_ref, inv_ref, sums_ref, hidden_ref, packed_ref, lse_ref, doc_row, doc_col, *refs
):
    ups, refs = refs[:count], refs[count:]
    (
        first_out, low_out, mixed_back_out, grads_out, grad_packed_out, weight_out, weight_up, total, sems_out, sems_up
    ) = refs
    length, width = hat_ref.shape

    def fetch(c):
        return piece_copies(ups, places, weight_up, sems_up.at[c], part(c, width), part(c, width))

    for c in range(4):
        start_all(fetch(c))
    copies_out = start_all(piece_copies(ups, places, weight_out, sems_out, pl.ds(4 * width, width)))
    total[...] = back_ref[...]

    @pl.loop(0, 4)
    def _(c):
        wait_all(fetch(c))
        total[...] += dot(hidden_ref[:, part(c, width)], weight_up[:, part(c, width)], 1, 1)

    grads_out[...] = jnp.zeros_like(grads_out)

    @functools.partial(by_rows, length)
    def _(rows):
        gradient, hat = total[rows, :], hat_ref[rows, :]
        grads_out[0:1, :] += column_sum(gradient * hat)
        grads_out[1:2, :] += column_sum(gradient)
        first = normalize_back(gradient * sums_ref[4:5, :], hat, inv_ref[rows, :])
        first_out[rows, :] = first
        low_out[rows, :] = first.astype(LOW)

    wait_all(copies_out)
    mixed_back_out[...] = dot(weight_out[...], low_out[...], 1, 1).astype(LOW)
    same = doc_col[...] == doc_row[...]
    heads = grad_packed_out.shape[0] // (3 * HEAD_DIM)

    @pl.loop(0, heads, unroll=3)
    def _(head):
        mixed_back = mixed_back_out[part(head, HEAD_DIM), :]
        attend_back_head(head, 0, packed_ref, mixed_back, lse_ref, same, grad_packed_out, heads * HEAD_DIM, 0)


def attend_back_kernel(
    count, tokens, places, packed_ref, mixed_back_ref, lse_ref, doc_row, doc_col, projected_ref, sums_ref, first_ref,
    done_ref, *refs
):
    pieces = refs[:count]
    grad_packed_out, embedded_out, grads_out, weight, sems = refs[count:]
    length, width = projected_ref.shape
    copies = start_all(piece_copies(pieces, places, weight, sems, pl.ds(0, 3 * width)))
    same = doc_col[...] == doc_row[...]
    done = done_ref.shape[0] // 3

    @pl.loop(0, (width - done) // HEAD_DIM, unroll=3)
    def _(head):
        mixed_back = mixed_back_ref[part(head + done // HEAD_DIM, HEAD_DIM), :]
        attend_back_head(head, done // HEAD_DIM, packed_ref, mixed_back, lse_ref, same, grad_packed_out, width, done)

    for i in range(3):
        grad_packed_out[i * width : i * width + done, :] = done_ref[i * done : (i + 1) * done, :]
    wait_all(copies)
    mean, _, inv = batch_scale(sums_ref, tokens)
    for n in range(width // TILE):
        cols = slice(n * TILE, (n + 1) * TILE)
        values = first_ref[:, cols] + dot(weight[cols, :], grad_packed_out[...]).T
        embedded_out[:, cols] = values
        normed = (projected_ref[:, cols] - mean[:, cols]) * inv[:, cols]
        grads_out[0:1, cols] = column_sum(values)
        grads_out[1:2, cols] = column_sum(values * normed)


def packed_gradient_kernel(tokens, places, projected_ref, sums_ref, grad_packed_ref, *refs):
    halves, (low, work, grad_packed, sems) = refs[:-4], refs[-4:]
    length, width = projected_ref.shape

    def fetch(c):
        return pltpu.make_async_copy(grad_packed_ref.at[part(c, width)], grad_packed.at[part(c, width)], sems.at[c])

    for c in range(3):
        fetch(c).start()

    @functools.partial(by_rows, length)
    def _(rows):
        low[:, rows] = embed(projected_ref, sums_ref, tokens, rows).T.astype(LOW)

    @pl.loop(0, 3)
    def _(c):
        fetch(c).wait()
        for n in range(width // TILE):
            cols = part(c * (width // TILE) + n, TILE)
            put_blocks(halves, places, dot(low[...], grad_packed[cols, :], 1, 1), cols, work.at[n % 2])


def project_back_kernel(tokens, places, embedded_ref, projected_ref, sums_ref, grads_ref, mixed_ref, low_ref, x_ref, *refs):
    halves, (low_out, work, x, sems) = refs[:-4], refs[-4:]
    copies = start_all([pltpu.make_async_copy(x_ref, x, sems.at[0])])
    mean, _, inv = batch_scale(sums_ref, tokens)
    roi_rows = x_ref.shape[1] * halves[0].shape[1] // (x_ref.shape[1] + low_ref.shape[1])

    @functools.partial(by_rows, projected_ref.shape[0])
    def _(rows):
        normed = (projected_ref[rows, :] - mean) * inv
        shift = grads_ref[0:1, :] * (1.0 / tokens) + normed * (grads_ref[1:2, :] * (1.0 / tokens))
        low_out[rows, :] = (sums_ref[2:3, :] * inv * (embedded_ref[rows, :] - shift)).astype(LOW)

    wait_all(copies)
    row_blocks(halves, places, lambda at, n: dot(x[:, lanes(at, n)], low_out[...], 0, 0), roi_rows)
    work[...] = dot(mixed_ref[...], low_ref[...]).astype(LOW)
    if len(halves) == 1:
        halves[0][0, roi_rows:, :] = work[...]
    else:
        rows = halves[0].shape[1] - roi_rows
        for rel in range(8):
            halves[rel & 1][rel >> 1, roi_rows:, :] = work[part(places[rel], rows), :]


def input_gradient_kernel(count, places, low_ref, *refs):
    pieces, (out_ref, weight, sems) = refs[:count], refs[count:]
    wait_all(start_all(piece_copies(pieces, places, weight, sems)))

    @pl.loop(0, weight.shape[0] // 512)
    def _(i):
        out_ref[:, part(i, 512)] = dot(low_ref[...], weight[part(i, 512), :], 1, 1)


def sides(own):
    return [swap(own, ACROSS), swap(own, ALONG)]


def corner_halves(across, along):
    half = across.shape[0] // 2
    return [swap(along[:half], ACROSS), swap(across[half:], ALONG)]


def with_cores(chips):
    pieces = []
    for shard in chips:
        pieces += [shard, swap(shard, CORE)]
    return pieces


def per_device(
    roi_features, doc_ids, w_roi, bn_gain, bn_beta, w_qkv, w_out, ln1_gain, ln1_beta,
    w_up, w_down, ln2_gain, ln2_beta, cotangent,
):
    _, length, roi_width = roi_features.shape
    width, hidden = w_roi.shape[1], w_up.shape[1]
    devices = lax.axis_size("dp") * lax.axis_size("shard")
    tokens = length * devices
    me = lax.axis_index("shard")
    direct = direct_mesh()
    shards, rows = 8 if direct else 1, w_up.shape[0]
    cores, chips = (2, 4) if direct else (1, 1)
    places = (me ^ jnp.arange(8)).astype(jnp.int32) if direct else jnp.zeros((8,), jnp.int32)

    x = roi_features.reshape(length, roi_width)
    doc_row, doc_col = doc_ids.reshape(1, length), doc_ids.reshape(length, 1)
    own_params = jnp.stack([bn_gain, bn_beta, ln1_gain, ln1_beta, ln2_gain, ln2_beta]).astype(F32)
    own_params = jnp.where(lax.axis_index("dp") == 0, own_params, 0.0)
    own_start = me * bn_gain.shape[0]
    params = lax.dynamic_update_slice(jnp.zeros((8, width), F32), own_params, (2, own_start))

    gather = functools.partial(lax.all_gather, axis_name="shard", axis=0, tiled=True)
    wide_up = jnp.concatenate([w_up, w_out], axis=1)
    if direct:
        roi_chips = [w_roi, *sides(w_roi), swap(w_roi, ACROSS | ALONG)]
        w_qkv = tie(w_qkv, params, wide_up)
        qkv_chips = [w_qkv, *sides(w_qkv), swap(w_qkv, ACROSS | ALONG)]
        roi_pieces = with_cores(tie(roi_chips, w_qkv))
    else:
        roi_pieces = [gather(w_roi)]
    count = len(roi_pieces)

    def blocks(r, c):
        return [shape((chips, r, c), LOW)] * cores

    def low(r, c):
        return pltpu.VMEM((r, c), LOW)

    projected, sums = call(
        functools.partial(project_kernel, count),
        [places, x, params, *roi_pieces],
        [shape((length, width)), shape((8, width))],
        [low(roi_width, width), low(length, roi_width)],
        "project",
        out_near=(0,),
        far=(1, *range(3, 100)),
        sems=((8,), (1,)),
        loose=(4, 6, 8, 10),
    )
    if direct:
        sums = sums + swap(sums, CORE)
        sums = sums + swap(sums, 1, "dp")
        sums = sums + swap(sums, 2, "dp")
        around = [swap(sums, ACROSS), swap(sums, ALONG), swap(sums, ACROSS | ALONG)]
        qkv_chips = tie(qkv_chips, sums)
        around = tie(around, qkv_chips)
        sums = (sums + around[0]) + (around[1] + around[2])
        qkv_pieces = with_cores(qkv_chips)
        up_sides = sides(tie(wide_up, sums))
    else:
        sums = lax.psum(sums, ("dp", "shard"))
        qkv_pieces = [gather(w_qkv)]

    heads = width // HEAD_DIM
    part_width = heads // 2 * HEAD_DIM
    packed_qkv, mixed, lse = call(
        functools.partial(attend_kernel, count, tokens),
        [places, projected, sums, doc_row, doc_col, *qkv_pieces],
        [shape((3 * width, length), LOW), shape((width, length), LOW), shape((heads, length))],
        [low(width, 3 * width), low(length, width)],
        "attend",
        near=(1,), out_near=(0, 1, 2),
        far=range(5, 100),
        sems=((3, 8),),
        loose=(6, 8, 10, 12),
    )
    if direct:
        up_sides = tie(up_sides, mixed)
        up_corner = jnp.concatenate(corner_halves(*up_sides))
        down_sides = sides(tie(w_down, up_sides))
        up_pieces = with_cores([wide_up, *up_sides, up_corner])
    else:
        up_pieces, down_parts = [gather(wide_up)], [gather(w_down)]
    hat, inv, active, slope = call(
        functools.partial(expand_kernel, count, tokens),
        [places, projected, sums, mixed, *up_pieces],
        [shape((length, width)), shape((length, 1)), shape((length, hidden), LOW), shape((length, hidden), LOW)],
        [low(width, width), low(width, hidden), low(length, width)],
        "expand",
        near=(1, 3), out_near=(0, 1, 2, 3),
        far=range(4, 100),
        sems=((8,), (4, 8)),
        loose=(5, 7, 9, 11),
    )
    if direct:
        down_sides = tie(down_sides, active)
        down_parts = with_cores([w_down, *down_sides, jnp.concatenate(corner_halves(*down_sides))])
    *down_halves, layer_out, back, grads_two = call(
        functools.partial(contract_kernel, count),
        [places, hat, sums, active, cotangent.reshape(length, width), *down_parts],
        blocks(hidden // shards, width) + [shape((length, width), LOW), shape((length, width)), shape((2, width))],
        [low(hidden, width), pltpu.VMEM((length, width), F32), low(length, width), low(length, width)],
        "contract",
        near=(1, 3), out_near=(cores + 1,),
        far=range(4, 100),
        sems=((8,), (1,)),
        loose=(6, 8, 10, 12),
    )
    down = OwnedSum(down_halves)
    *up_halves, grad_hidden = call(
        functools.partial(hidden_back_kernel, count),
        [places, back, hat, sums, slope, *down_parts],
        blocks(hidden // shards, width) + [shape((length, hidden), LOW)],
        [low(hidden, width), low(length, width), low(width, length), pltpu.VMEM((2, width, TILE), LOW)],
        "hidden_back",
        near=(1, 2, 4), out_near=(cores,),
        far=range(5, 100),
        sems=((8,),),
    )
    up = OwnedSum(up_halves)
    sent = down.plane_one(grad_hidden)
    first, low_first, mixed_back, grads_one, grad_part = call(
        functools.partial(expand_back_kernel, count),
        [
            tie(places, sent), back, hat, inv, sums, grad_hidden, packed_qkv, lse, doc_row, doc_col, *up_pieces,
        ],
        [
            shape((length, width)), shape((length, width), LOW), shape((width, length), LOW), shape((2, width)),
            shape((3 * part_width, length), LOW),
        ],
        [low(width, width), low(width, hidden), pltpu.VMEM((length, width), F32)],
        "expand_back",
        near=(1, 2, 3, 5, 6, 7), out_near=(0, 1, 2, 4),
        far=range(10, 100),
        sems=((8,), (4, 8)),
    )
    sent = plane_together(down, up, first) if direct else first
    grad_packed, grad_embedded, grads_bn = call(
        functools.partial(attend_back_kernel, count, tokens),
        [
            tie(places, sent), packed_qkv, mixed_back, lse, doc_row, doc_col, projected, sums, first, grad_part,
            *qkv_pieces,
        ],
        [shape((3 * width, length), LOW), shape((length, width)), shape((2, width))],
        [low(width, 3 * width)],
        "attend_back",
        near=(1, 2, 3, 6, 8, 9), out_near=(0, 1),
        far=range(10, 100),
        sems=((8,),),
    )
    second = jnp.concatenate([grads_bn, grads_one, grads_two, jnp.zeros((2, width), F32)])
    if direct:
        second = second + swap(second, CORE)
        second = second + swap(second, 1, "dp")
        second = second + swap(second, 2, "dp")
        second = tie(second, up.came)
        around = [swap(second, ACROSS), swap(second, ALONG), swap(second, ACROSS | ALONG)]
        sent = up.plane_two(second)
        down_sum = LineSum(down.plane_done(sent))
        around = tie(around, sent, down_sum.step())
        second = (second + around[0]) + (around[1] + around[2])
    else:
        second = lax.psum(second, ("dp", "shard"))
    roi_rows, out_rows = roi_width // shards, width // shards
    *roi_halves, low_projected = call(
        functools.partial(project_back_kernel, tokens),
        [places, grad_embedded, projected, sums, second, mixed, low_first, x],
        blocks(roi_rows + out_rows, width) + [shape((length, width), LOW)],
        [low(width, width), low(length, roi_width)],
        "project_back",
        near=(1, 2, 5, 6), out_near=(cores,),
        far=(8,),
        sems=((1,),),
    )
    roi = OwnedSum(roi_halves)
    start_packed = tie(places, low_projected)
    qkv_halves = call(
        functools.partial(packed_gradient_kernel, tokens),
        [start_packed, projected, sums, grad_packed],
        blocks(width // shards, 3 * width),
        [low(width, length), pltpu.VMEM((2, width, TILE), LOW), low(3 * width, length)],
        "packed_gradient",
        near=(1,),
        far=(3,),
        sems=((3,),),
    )
    qkv = OwnedSum(qkv_halves)
    sent = roi.plane_one(qkv_halves)
    if direct:
        up_sum = LineSum(up.plane_done(sent))
        sent = up_sum.step()
    def input_gradient(*sent):
        return call(
            functools.partial(input_gradient_kernel, count),
            [tie(places, *sent), low_projected, *roi_pieces],
            [shape((length, roi_width))],
            [low(roi_width, width)],
            "input_gradient",
            near=(1,),
            far=range(2, 100),
            sems=((8,),),
        )[0]

    if direct:
        sent = down_sum.step(sent)
        sent = roi.plane_two(sent)
        sent = qkv.plane_one(sent)
        sent = down_sum.step(up_sum.step(sent))
        roi_sum = LineSum(roi.plane_done(sent))
        sent = roi_sum.step()
        sent = qkv.plane_two(sent)
        sent = up_sum.step(sent)
        sent = roi_sum.step(sent)
        qkv_sum = LineSum(qkv.plane_done(sent))
        sent = qkv_sum.step()
        sent = roi_sum.step(sent)
        sent = qkv_sum.step(sent)
        sent = roi_grad = input_gradient(sent)
        sent = qkv_sum.step(sent)
        sum_roi, sum_down, sum_up, sum_qkv = [g.total() for g in (roi_sum, down_sum, up_sum, qkv_sum)]
        sum_roi, sum_out = sum_roi[:roi_rows], sum_roi[roi_rows:]
        sum_up = jnp.concatenate([sum_up[i * rows : (i + 1) * rows] for i in range(4)], axis=1)
    else:
        roi_grad = input_gradient()
        grads = [roi_halves[0][0, :roi_rows], roi_halves[0][0, roi_rows:], down_halves[0][0], qkv_halves[0][0]]
        grads.append(up_halves[0][0].reshape(4, width, width).swapaxes(0, 1).reshape(width, hidden))
        sum_roi, sum_out, sum_down, sum_qkv, sum_up = [
            lax.psum(lax.psum_scatter(grad, "shard", scatter_dimension=0, tiled=True), "dp").astype(F32) for grad in grads
        ]
    own = lax.dynamic_slice_in_dim(second, own_start, bn_gain.shape[0], 1)
    mean = sums[0] / tokens
    return (
        layer_out[None], roi_grad[None], sum_roi, own[1], own[0], sum_qkv, sum_out, own[2], own[3],
        sum_up, sum_down, own[4], own[5], mean, sums[1] / tokens - mean * mean,
    )


def solution(mesh):
    rows3, rows2, split2, split1 = P(("dp", "shard"), None, None), P(("dp", "shard"), None), P("shard", None), P("shard")
    return jax.shard_map(
        per_device,
        mesh=mesh,
        in_specs=(
            rows3, rows2, split2, split1, split1, split2, split2, split1, split1, split2, split2, split1, split1, rows3,
        ),
        out_specs=(
            rows3, rows3, split2, split1, split1, split2, split2, split1, split1, split2, split2, split1, split1, P(), P(),
        ),
        check_vma=False,
    )
```
